256 devices in a mesh: ctx: 32 (over y, x, z_lo), kv: 8 (over z_hi, core).
Axes of the slice: x: 4, y: 4, z: 8 (z_hi: 4, z_lo: 2; z = z_hi * 2 + z_lo), core: 2. Of those that a mesh axis runs over, the one named last changes fastest.
Arguments:
- hidden: bfloat16 [4096, 4096], P('ctx', 'kv'), may hold values from -18 to 18, as said below
- block_ids: int32 [4096], P('ctx'), may hold values from 0 to 255, never falling along the last dimension, each value on 1 to 32 neighbouring positions
- decode_order: int32 [4096], P('ctx'), may hold values from 0 to 31
- step_cut: int32 [256], replicated, may hold values from 0 to 32
- mask_embed: bfloat16 [4096], replicated, may hold values from -6 to 6
- q_weight: bfloat16 [4096, 4096], P(None, 'kv'), may hold values from -0.09375 to 0.09375
- k_weight: bfloat16 [4096, 1024], P(None, 'kv'), may hold values from -0.09375 to 0.09375
- v_weight: bfloat16 [4096, 1024], P(None, 'kv'), may hold values from -0.09375 to 0.09375
Outputs:
- clean_out: bfloat16 [4096, 4096], P('ctx', 'kv')
- noisy_out: bfloat16 [4096, 4096], P('ctx', 'kv')
The draws below stay inside these ranges and needn't reach their ends.
Inputs may be any that keep to these rules, and one draw needn't show every extreme that they name: `hidden`: activations; row scales differ. `block_ids`: never falling along the slab; each block has 1 to 32 tokens, one exactly 32.
All inputs are finite; a program needn't handle non-finite values.
Results may differ from the reference program's by a relative error of at most 0.013.
The reference program's roundings to bfloat16 on the way (of `noisy` and `weights`) count: a program that leaves them out, or rounds other values in their place, can miss the bound.
Values may be sent and summed in bfloat16 or wider, within the bound.
No kernel may reach another device: no remote copies, remote signals or barrier semaphores. Data moves between devices by JAX's collectives and lax.ppermute only.
A program may use at most 128 MiB of HBM per device.

```python
import math
import jax
import jax.numpy as jnp
import numpy as np
from jax import lax

D = 4096
HEADS = 32
KV_HEADS = 8
HEAD_DIM = 128
GROUP = 4
BLOCK = 32
TOKENS = 4096
BLOCKS = 256


def draw_hidden(key, part):
    key = jax.random.fold_in(key, 11)
    base_key, scale_key = jax.random.split(key)
    base = jnp.clip(jax.random.normal(base_key, (TOKENS, D), jnp.float32), -5.0, 5.0)
    scales = jnp.exp(jax.random.uniform(scale_key, (TOKENS, 1), jnp.float32, math.log(0.5), math.log(2.0)))
    return (base * scales).astype(jnp.bfloat16)


def plant(array, key, smallest, high):
    longest = array.shape.index(max(array.shape))
    spots = []
    for shift in (0, 1):
        where = [jax.random.randint(jax.random.fold_in(key, axis), (), 0, length) for axis, length in enumerate(array.shape)]
        where[longest] = (where[longest] + shift) % array.shape[longest]
        spots.append(tuple(where))
    return array.at[spots[0]].set(smallest).at[spots[1]].set(high)


def level_of(stream_key, dims, shards, low, high):
    level, own = 1.0, jax.random.fold_in(stream_key, 6)
    for position, blocks in shards:
        heights = jnp.exp(jax.random.uniform(jax.random.fold_in(own, position), (blocks,), jnp.float32, low / len(shards), high / len(shards)))
        level = level * jnp.repeat(heights, dims[position] // blocks).reshape([-1 if axis == position else 1 for axis in range(len(dims))])
    return level


def split_up(number_of, total, most, lean):
    weights = [(1 << 20) // math.isqrt(standing ** lean) + 1 for standing in range(2, number_of + 1)]
    surplus, counts = total - most - (number_of - 1), [1] * (number_of - 1)
    while surplus > 0:
        free = [i for i in range(number_of - 1) if counts[i] < most]
        mass, budget = sum([weights[i] for i in free]), surplus
        for i in free:
            extra = min(most - counts[i], max(1, budget * weights[i] // mass), surplus)
            counts[i] = counts[i] + extra
            surplus = surplus - extra
    return np.array([most] + counts)


def ragged_sizes(rng, amount, total, limit, slope):
    if amount == 2:
        one = jax.random.randint(rng, (), max(1, total - limit), min(limit, total - 1) + 1)
        return jnp.stack([one, total - one])
    lengths = jnp.asarray(split_up(amount, total, limit, slope), jnp.int32)
    couples = (amount - 1) // 2
    source_of, sink = lengths[1:1 + 2 * couples:2], lengths[2:2 + 2 * couples:2]
    room = jnp.minimum(source_of - 1, limit - sink)
    passed = jax.random.randint(jax.random.fold_in(rng, 1), (couples,), 0, 1 << 20) % (room + 1)
    lengths = lengths.at[1:1 + 2 * couples:2].set(source_of - passed).at[2:2 + 2 * couples:2].set(sink + passed)
    return lengths[jax.random.permutation(jax.random.fold_in(rng, 2), amount)]


def centred(key, dims, scale, most, shards=(), held_as=jnp.bfloat16):
    entries = jax.random.normal(key, dims, jnp.float32) * scale
    if len(shards) > 0:
        entries = level_of(key, dims, shards, -0.22, 0.18) * entries
    return jnp.clip(entries, min=-most, max=most).astype(held_as)


def setup_inputs(seed: int = 0) -> dict:
    splits = jax.random.split(jax.random.key(seed), 9)
    return {
        "hidden": draw_hidden(jax.random.fold_in(splits[8], 71), 0),
        "block_ids": jnp.searchsorted(jnp.cumsum(ragged_sizes(splits[1], BLOCKS, TOKENS, BLOCK, 0)), jnp.arange(TOKENS), side="right").astype(jnp.int32),
        "decode_order": plant(jax.random.randint(splits[2], (TOKENS,), 0, BLOCK), jax.random.fold_in(splits[2], 1), 0, BLOCK - 1).astype(jnp.int32),
        "step_cut": plant(jax.random.randint(splits[3], (BLOCKS,), 0, BLOCK + 1), jax.random.fold_in(splits[3], 1), 0, BLOCK).astype(jnp.int32),
        "mask_embed": centred(splits[4], (D,), 1.0, 6.0),
        "q_weight": centred(splits[5], (D, HEADS * HEAD_DIM), D ** -0.5, 0.09375, ((1, 8),)),
        "k_weight": centred(splits[6], (D, KV_HEADS * HEAD_DIM), D ** -0.5, 0.09375, ((1, 8),)),
        "v_weight": centred(splits[7], (D, KV_HEADS * HEAD_DIM), D ** -0.5, 0.09375, ((1, 8),)),
    }


def project(rows, weight):
    return jnp.dot(rows, weight, preferred_element_type=jnp.float32).astype(jnp.bfloat16)

def one_head(args):
    queries, keys, values, allowed = args
    scores = jnp.einsum('rqd,sd->qrs', queries, keys) / jnp.sqrt(jnp.float32(HEAD_DIM))
    scores = jnp.where(allowed[None], scores, -jnp.inf)
    top = lax.optimization_barrier(jnp.max(scores, axis=-1, keepdims=True))
    probs = jnp.exp(scores - top)
    total = lax.optimization_barrier(jnp.sum(probs, axis=-1))
    rounded = probs.astype(jnp.bfloat16).astype(jnp.float32)
    mixed = jnp.einsum('qrs,sd->qrd', rounded, values)
    return mixed / total[..., None]

def reference(hidden, block_ids, decode_order, step_cut, mask_embed, q_weight, k_weight, v_weight):
    cut = step_cut[block_ids]
    masked = decode_order >= cut
    noisy = jnp.where(masked[:, None], mask_embed[None, :], hidden)
    q_clean = project(hidden, q_weight).reshape(TOKENS, KV_HEADS, GROUP, HEAD_DIM)
    k_clean = project(hidden, k_weight).reshape(TOKENS, KV_HEADS, HEAD_DIM)
    v_clean = project(hidden, v_weight).reshape(TOKENS, KV_HEADS, HEAD_DIM)
    q_noisy = project(noisy, q_weight).reshape(TOKENS, KV_HEADS, GROUP, HEAD_DIM)
    k_noisy = project(noisy, k_weight).reshape(TOKENS, KV_HEADS, HEAD_DIM)
    v_noisy = project(noisy, v_weight).reshape(TOKENS, KV_HEADS, HEAD_DIM)
    span = min(1024, TOKENS)
    clean_parts = []
    noisy_parts = []
    for begin in range(0, TOKENS, span):
        high = min(TOKENS, begin + span + BLOCK)
        low = max(0, begin - BLOCK)
        queries = jnp.concatenate([q_clean[begin:begin + span], q_noisy[begin:begin + span]], 0).astype(jnp.float32)
        keys = jnp.concatenate([k_clean[:high], k_noisy[low:high]], 0).astype(jnp.float32)
        values = jnp.concatenate([v_clean[:high], v_noisy[low:high]], 0).astype(jnp.float32)
        key_blocks = jnp.concatenate([block_ids[:high], block_ids[low:high]], 0)
        is_noisy_key = jnp.arange(keys.shape[0]) >= high
        query_blocks = block_ids[begin:begin + span]
        clean_rows = (key_blocks[None, :] <= query_blocks[:, None]) & ~is_noisy_key[None, :]
        noisy_rows = jnp.where(is_noisy_key[None, :], key_blocks[None, :] == query_blocks[:, None], key_blocks[None, :] < query_blocks[:, None])
        allowed = jnp.concatenate([clean_rows, noisy_rows], 0)
        heads_out = lax.map(one_head, (jnp.moveaxis(queries, 1, 0), jnp.moveaxis(keys, 1, 0), jnp.moveaxis(values, 1, 0), jnp.broadcast_to(allowed, (KV_HEADS,) + allowed.shape)))
        merged = jnp.transpose(heads_out, (2, 0, 1, 3)).reshape(2 * span, HEADS * HEAD_DIM)
        clean_parts.append(merged[:span])
        noisy_parts.append(merged[span:])
    clean_out = jnp.concatenate(clean_parts, 0).astype(jnp.bfloat16)
    noisy_out = jnp.concatenate(noisy_parts, 0).astype(jnp.bfloat16)
    return (clean_out, noisy_out)
```

```python
import math

import jax
import jax.numpy as jnp
from jax import lax
from jax.sharding import PartitionSpec as P

HEAD_DIM = 128
BLOCK = 32


far_low = -1e30


def extended(block, sides, width):
    for axis, dim in sides:
        count = lax.axis_size(axis)
        forward = [(i, i + 1) for i in range(count - 1)]
        backward = [(target, source) for source, target in forward]
        low = lax.ppermute(
            lax.slice_in_dim(block, block.shape[dim] - width, None, axis=dim), axis, forward
        )
        high = lax.ppermute(lax.slice_in_dim(block, 0, width, axis=dim), axis, backward)
        block = jnp.concatenate([low, block, high], axis=dim)
    return block


def ctx_pairs(dy, dx, dz):
    pairs = []
    for i in range(32):
        y, x, z = i // 8, (i // 2) % 4, i % 2
        target = (((y + dy) % 4) * 4 + (x + dx) % 4) * 2 + (z + dz) % 2
        pairs.append((i, target))
    return pairs


def kv_pairs(dz, dc):
    pairs = []
    for i in range(8):
        z, c = i // 2, i % 2
        pairs.append((i, ((z + dz) % 4) * 2 + (c + dc) % 2))
    return pairs


def gather_ctx(block):
    block = jnp.stack([block, lax.ppermute(block, "ctx", ctx_pairs(0, 0, 1))])
    block = jnp.stack([block] + [lax.ppermute(block, "ctx", ctx_pairs(0, d, 0)) for d in (1, 2, 3)])
    block = jnp.stack([block] + [lax.ppermute(block, "ctx", ctx_pairs(d, 0, 0)) for d in (1, 2, 3)])
    return block.reshape((-1,) + block.shape[4:] if block.ndim > 4 else (-1,))


def gather_kv(block):
    parts = [block] + [lax.ppermute(block, "kv", kv_pairs(d, 0)) for d in (1, 2, 3)]
    block = jnp.stack(parts)
    block = jnp.stack([block, lax.ppermute(block, "kv", kv_pairs(0, 1))], 1)
    rows, width = block.shape[2:]
    block = block.reshape(8, rows, width)
    me = lax.axis_index("kv")
    j = jnp.arange(8)
    source = ((me // 2 - j // 2) % 4) * 2 + (me + j) % 2
    block = block[source]
    return jnp.transpose(block, (1, 0, 2)).reshape(rows, 8 * width)


def attend(state, queries, keys, values, allowed):
    top, total, accum = state
    scale = 1.0 / math.sqrt(queries.shape[-1])
    count = keys.shape[0]
    for begin in range(0, count, 1024):
        width = min(1024, count - begin)
        key_part = keys[begin : begin + width]
        value_part = values[begin : begin + width]
        permit = allowed[None, None, :, begin : begin + width]
        scores = (
            jnp.einsum("rgqd,sgd->gqrs", queries, key_part, preferred_element_type=jnp.float32)
            * scale
        )
        scores = jnp.where(permit, scores, far_low)
        new_top = jnp.maximum(top, jnp.max(scores, axis=-1))
        probs = jnp.where(permit, jnp.exp(scores - new_top[..., None]), 0.0)
        factor = jnp.exp(top - new_top)
        total = total * factor + jnp.sum(probs, axis=-1)
        accum = accum * factor[..., None] + jnp.einsum(
            "gqrs,sgd->gqrd",
            probs.astype(jnp.bfloat16),
            value_part,
            preferred_element_type=jnp.float32,
        )
        top = new_top
    return (top, total, accum)


def merge_state(first, second):
    top = jnp.maximum(first[0], second[0])
    factor_one = jnp.exp(first[0] - top)
    factor_two = jnp.exp(second[0] - top)
    total = first[1] * factor_one + second[1] * factor_two
    accum = first[2] * factor_one[..., None] + second[2] * factor_two[..., None]
    return (top, total, accum)


def empty_state(groups, group, count, head_dim):
    return (
        jnp.full((groups, group, count), far_low, jnp.float32),
        jnp.zeros((groups, group, count), jnp.float32),
        jnp.zeros((groups, group, count, head_dim), jnp.float32),
    )


def shards(hidden, block_ids, decode_order, step_cut, mask_embed, q_weight, k_weight, v_weight):
    rows = hidden.shape[0]
    half = rows // 2
    head_dim = HEAD_DIM
    groups = k_weight.shape[1] // head_dim
    match = block_ids[:, None] == jnp.arange(step_cut.shape[0], dtype=jnp.int32)[None, :]
    cut = jnp.sum(jnp.where(match, step_cut[None, :], 0), axis=1)
    masked = decode_order >= cut
    piece = gather_kv(hidden)
    noisy_piece = jnp.where(masked[:, None], mask_embed[None, :], piece)
    results = []
    for index, weight in enumerate((q_weight, k_weight, v_weight)):
        weight_rows = weight
        results.append(jnp.dot(piece, weight_rows, preferred_element_type=jnp.float32))
    for index, weight in enumerate((q_weight, k_weight, v_weight)):
        weight_rows = weight
        results.append(jnp.dot(noisy_piece, weight_rows, preferred_element_type=jnp.float32))
    projected = tuple(results)
    q_clean, k_clean, v_clean, q_noisy, k_noisy, v_noisy = [
        p.astype(jnp.bfloat16) for p in projected
    ]
    group = q_clean.shape[1] // (groups * head_dim)
    clean_queries = q_clean.reshape(rows, groups, group, head_dim)
    noisy_queries = q_noisy.reshape(rows, groups, group, head_dim)
    late_clean = clean_queries[half:]
    late_noisy = noisy_queries[half:]
    late_ids = block_ids[half:]
    halves = (
        (jnp.concatenate([clean_queries[:half], noisy_queries[:half]], 0), block_ids[:half]),
        (jnp.concatenate([late_clean, late_noisy], 0), late_ids),
    )
    noisy_row = jnp.arange(2 * half) >= half
    fresh = (
        empty_state(groups, group, 2 * half, head_dim),
        empty_state(groups, group, 2 * half, head_dim),
    )
    stacked = jnp.stack([k_noisy, v_noisy], 1)
    rim_pairs, rim_ids = (
        extended(stacked, (("ctx", 0),), BLOCK),
        extended(block_ids + 1, (("ctx", 0),), BLOCK),
    )
    count = rim_pairs.shape[0]
    near = rim_ids[None, :] == (block_ids + 1)[:, None]
    rim_state = attend(
        empty_state(groups, group, rows, head_dim),
        noisy_queries,
        rim_pairs[:, 0].reshape(count, groups, head_dim),
        rim_pairs[:, 1].reshape(count, groups, head_dim),
        near,
    )
    piece_ids = gather_ctx(block_ids)
    both = gather_ctx(jnp.concatenate([k_clean, v_clean], 1))
    keys, values = both[:, : k_clean.shape[1]], both[:, k_clean.shape[1] :]
    count_here = keys.shape[0]
    key_part = keys.reshape(count_here, groups, head_dim)
    value_part = values.reshape(count_here, groups, head_dim)
    outcome = []
    for index in range(2):
        half_queries, half_ids = halves[index]
        query_blocks = jnp.concatenate([half_ids, half_ids], 0)
        before = piece_ids[None, :] < query_blocks[:, None]
        same = piece_ids[None, :] == query_blocks[:, None]
        permit = before | same & ~noisy_row[:, None]

        def work(current, half_queries=half_queries, permit=permit):
            return attend(current, half_queries, key_part, value_part, permit)

        outcome.append(work(fresh[index]))
    states = tuple(outcome)
    early_state, late_state = states
    whole = []
    for member in range(3):
        first = early_state[member]
        second = late_state[member]
        whole.append(
            jnp.concatenate(
                [first[:, :, :half], second[:, :, :half], first[:, :, half:], second[:, :, half:]],
                2,
            )
        )
    top, total, accum = whole
    noisy_part = merge_state((top[:, :, rows:], total[:, :, rows:], accum[:, :, rows:]), rim_state)
    top = jnp.concatenate([top[:, :, :rows], noisy_part[0]], 2)
    total = jnp.concatenate([total[:, :, :rows], noisy_part[1]], 2)
    accum = jnp.concatenate([accum[:, :, :rows], noisy_part[2]], 2)
    result = accum / total[..., None]
    result = (
        jnp.transpose(result, (2, 0, 1, 3))
        .reshape(2 * rows, groups * group * head_dim)
        .astype(jnp.bfloat16)
    )
    return (result[:rows], result[rows:])


def solution(mesh):
    return jax.shard_map(
        shards,
        mesh=mesh,
        in_specs=(
            P("ctx", "kv"),
            P("ctx"),
            P("ctx"),
            P(),
            P(),
            P(None, "kv"),
            P(None, "kv"),
            P(None, "kv"),
        ),
        out_specs=(P("ctx", "kv"), P("ctx", "kv")),
        check_vma=False,
    )
```

```python
import math

import jax
import jax.numpy as jnp
from jax import lax
from jax.experimental import pallas as pl
from jax.experimental.pallas import tpu as pltpu
from jax.sharding import PartitionSpec as P

ROWS = 128
HEAD = 128
GROUP = 4
WIDTH = 512
BLOCK = 32
LAST = 31
LOW = -1e30
FAR = 1e6
POWER = math.log2(math.e) / math.sqrt(HEAD)
LIMIT = 48 * 1024 * 1024
F32 = jnp.float32
BF16 = jnp.bfloat16


def ctx_pairs(dy, dx, dz):
    pairs = []
    for i in range(32):
        y, x, z = i // 8, (i // 2) % 4, i % 2
        pairs.append((i, (((y + dy) % 4) * 4 + (x + dx) % 4) * 2 + (z + dz) % 2))
    return pairs


def kv_pairs(dz, dc):
    pairs = []
    for i in range(8):
        z, c = i // 2, i % 2
        pairs.append((i, ((z + dz) % 4) * 2 + (c + dc) % 2))
    return pairs


def dot(a, b):
    return jnp.dot(a, b, preferred_element_type=F32)


def dot_t(a, b):
    return lax.dot_general(a, b, (((1,), (1,)), ((), ())), preferred_element_type=F32)


def call(kernel, outs, args, cost, scratch=()):
    spec = pl.BlockSpec(memory_space=pltpu.VMEM)
    return pl.pallas_call(
        kernel,
        out_shape=[jax.ShapeDtypeStruct(s, t) for s, t in outs],
        in_specs=[spec] * len(args),
        out_specs=[spec] * len(outs),
        scratch_shapes=list(scratch),
        compiler_params=pltpu.CompilerParams(vmem_limit_bytes=LIMIT),
        cost_estimate=pl.CostEstimate(flops=cost[0], bytes_accessed=cost[1], transcendentals=0),
    )(*args)


def column(row):
    square = (ROWS, ROWS)
    same = lax.broadcasted_iota(jnp.int32, square, 0) == lax.broadcasted_iota(jnp.int32, square, 1)
    return jnp.sum(jnp.where(same, jnp.broadcast_to(row, square), 0.0), axis=1, keepdims=True)


def mask_kernel(ids_ref, order_ref, cut_ref, embed_ref, wq_ref, wk_ref, wv_ref, flag_ref, mq_ref, mkv_ref):
    ids = column(ids_ref[...].astype(F32))
    order = column(order_ref[...].astype(F32))
    blocks = cut_ref.shape[1]
    spots = lax.broadcasted_iota(jnp.int32, (ROWS, blocks), 1).astype(F32)
    cuts = jnp.broadcast_to(cut_ref[...].astype(F32), (ROWS, blocks))
    cut = jnp.sum(jnp.where(spots == ids, cuts, 0.0), axis=1, keepdims=True)
    flag_ref[...] = jnp.broadcast_to(jnp.where(order >= cut, 1.0, 0.0), (ROWS, HEAD))
    embed = jnp.broadcast_to(embed_ref[...], (16, embed_ref.shape[1]))
    mq_ref[...] = dot(embed, wq_ref[...]).astype(BF16)
    mkv_ref[:, :HEAD] = dot(embed, wk_ref[...]).astype(BF16)
    mkv_ref[:, HEAD:] = dot(embed, wv_ref[...]).astype(BF16)


def kv_kernel(*refs):
    pieces = refs[:8]
    wk_ref, wv_ref, flag_ref, mkv_ref, ids_ref = refs[8:13]
    x_ref, kv_ref, kvn_ref, up_ref, down_ref = refs[13:]
    me = lax.axis_index("kv")
    for dz in range(4):
        for dc in range(2):
            source = lax.rem(me // 2 + 4 - dz, 4) * 2 + lax.rem(me + dc, 2)
            x_ref[:, pl.ds(pl.multiple_of(source * WIDTH, WIDTH), WIDTH)] = pieces[2 * dz + dc][...]
    x = x_ref[...]
    masked = flag_ref[...] > 0.5
    for part, w_ref in enumerate((wk_ref, wv_ref)):
        lanes = slice(part * HEAD, (part + 1) * HEAD)
        clean = dot(x, w_ref[...])
        fixed = jnp.broadcast_to(mkv_ref[0:1, lanes].astype(F32), (ROWS, HEAD))
        noisy = jnp.where(masked, fixed, clean).astype(BF16)
        clean = clean.astype(BF16)
        kv_ref[:, lanes] = clean
        kvn_ref[:, lanes] = noisy
        up_ref[0:ROWS, lanes] = clean
        up_ref[ROWS : ROWS + BLOCK, lanes] = noisy[ROWS - BLOCK :]
        down_ref[0:BLOCK, lanes] = clean[:BLOCK]
        down_ref[BLOCK : 2 * BLOCK, lanes] = noisy[:BLOCK]
        ids = jnp.broadcast_to(ids_ref[...].astype(F32), (16, ROWS)).astype(BF16)
        up_ref[ROWS + BLOCK :, lanes] = ids
        down_ref[2 * BLOCK :, lanes] = ids


def q_kernel(x_ref, wq_ref, flag_ref, mq_ref, q_ref):
    masked = flag_ref[...] > 0.5
    x = x_ref[...]
    for h in range(GROUP):
        lanes = slice(h * HEAD, (h + 1) * HEAD)
        clean = dot(x, wq_ref[:, lanes])
        fixed = jnp.broadcast_to(mq_ref[0:1, lanes].astype(F32), (ROWS, HEAD))
        q_ref[h, :ROWS, :] = clean.astype(BF16)
        q_ref[h, ROWS:, :] = jnp.where(masked, fixed, clean).astype(BF16)


def near_kernel(q_ref, kv_ref, kvn_ref, up_ref, down_ref, ids_ref, top_ref, total_ref, accum_ref, k_ref, v_ref):
    me = lax.axis_index("ctx")
    for ref, lanes in ((k_ref, slice(0, HEAD)), (v_ref, slice(HEAD, 2 * HEAD))):
        ref[0:128, :] = up_ref[0:ROWS, lanes]
        ref[128:256, :] = kv_ref[:, lanes]
        ref[256:288, :] = down_ref[0:BLOCK, lanes]
        ref[288:320, :] = up_ref[ROWS : ROWS + BLOCK, lanes]
        ref[320:352, :] = down_ref[BLOCK : 2 * BLOCK, lanes]
        ref[352:384, :] = jnp.zeros((BLOCK, HEAD), BF16)
        ref[384:512, :] = kvn_ref[:, lanes]
    own = jnp.broadcast_to(ids_ref[...].astype(F32), (8, ROWS))
    before = up_ref[ROWS + BLOCK :, 0:ROWS].astype(F32)[:8]
    after = down_ref[2 * BLOCK :, 0:ROWS].astype(F32)[:8]
    before = jnp.where(me > 0, before, FAR)
    after = jnp.where(me < LAST, after, FAR)
    lane = lax.broadcasted_iota(jnp.int32, (8, ROWS), 1)
    mixed = jnp.where(
        lane < 32,
        after,
        jnp.where(lane < 64, pltpu.roll(before, 64, 1), jnp.where(lane < 96, pltpu.roll(after, 64, 1), -5.0)),
    )
    query = jnp.broadcast_to(column(ids_ref[...].astype(F32)), (ROWS, ROWS))
    keys = [jnp.broadcast_to(row[0:1], (ROWS, ROWS)) for row in (before, own, mixed, own)]
    early = lax.broadcasted_iota(jnp.int32, (ROWS, ROWS), 1) < 32
    zero = jnp.zeros((ROWS, ROWS), F32)
    low = jnp.full((ROWS, ROWS), LOW, F32)
    clean_bias = [
        jnp.where(keys[0] <= query, zero, low),
        jnp.where(keys[1] <= query, zero, low),
        jnp.where(early, jnp.where(keys[2] <= query, zero, low), low),
        low,
    ]
    noisy_bias = [
        jnp.where(keys[0] < query, zero, low),
        jnp.where(keys[1] < query, zero, low),
        jnp.where(early, jnp.where(keys[2] < query, zero, low), jnp.where(keys[2] == query, zero, low)),
        jnp.where(keys[3] == query, zero, low),
    ]
    bias = jnp.concatenate(
        [jnp.concatenate(clean_bias, axis=1), jnp.concatenate(noisy_bias, axis=1)], axis=0
    )
    for h in range(GROUP):
        scores = dot_t(q_ref[h], k_ref[...])
        scores = jnp.where(bias < -1.0, LOW, scores)
        top = jnp.max(scores, axis=1, keepdims=True)
        probs = jnp.exp2((scores - top) * POWER)
        top_ref[h] = jnp.broadcast_to(top, (2 * ROWS, HEAD))
        total_ref[h] = probs[:, 0:128] + probs[:, 128:256] + probs[:, 256:384] + probs[:, 384:512]
        accum_ref[h] = dot(probs.astype(BF16), v_ref[...])


def far_kernel(*refs):
    q_ref = refs[0]
    k_refs, v_refs = refs[1:5], refs[5:9]
    top_in, total_in, accum_in = refs[9:12]
    clean_ref, noisy_ref = refs[12:14]
    top_ref, total_ref, accum_ref = refs[14:]
    me = lax.axis_index("ctx")
    y, x, z = me // 8, lax.rem(me // 2, 4), lax.rem(me, 2)
    top_ref[...] = top_in[...]
    total_ref[...] = total_in[...]
    accum_ref[...] = accum_in[...]

    def chunk(h, dy, partial):
        keys = k_refs[dy][...].reshape(8 * ROWS, HEAD)
        scores = dot_t(q_ref[h], keys)
        parts = [scores[:, j * ROWS : (j + 1) * ROWS] for j in range(8)]
        if partial:
            for j in range(8):
                dx, dz = j // 2, j % 2
                index = lax.rem(y + 4 - dy, 4) * 8 + lax.rem(x + 4 - dx, 4) * 2 + lax.rem(z + dz, 2)
                parts[j] = jnp.where(index < me - 1, parts[j], LOW)
        best = parts[0]
        for part in parts[1:]:
            best = jnp.maximum(best, part)
        old = top_ref[h]
        top = jnp.maximum(old, jnp.max(best, axis=1, keepdims=True))
        factor = jnp.exp2((old - top) * POWER)
        probs = [jnp.exp2((part - top) * POWER) for part in parts]
        total = total_ref[h] * factor
        for part in probs:
            total = total + part
        accum = accum_ref[h] * factor
        probs = jnp.concatenate([part.astype(BF16) for part in probs], axis=1)
        for dx in range(4):
            values = v_refs[dx][dy].reshape(2 * ROWS, HEAD)
            accum = accum + dot(probs[:, dx * 256 : (dx + 1) * 256], values)
        top_ref[h] = top
        total_ref[h] = total
        accum_ref[h] = accum

    for dy in range(4):
        if dy == 0:
            some, whole = me - y * 8 > 1, me < 0
        else:
            whole = (y >= dy) & ((dy > 1) | (x + z > 0))
            some = (y >= dy) & jnp.logical_not(whole)
        for partial, when in ((True, some), (False, whole)):
            if dy == 0 and not partial or dy > 1 and partial:
                continue

            @pl.when(when)
            def _(dy=dy, partial=partial):
                def body(h, carry):
                    chunk(h, dy, partial)
                    return carry

                lax.fori_loop(0, GROUP, body, 0)

    for h in range(GROUP):
        lanes = slice(h * HEAD, (h + 1) * HEAD)
        total = jnp.sum(total_ref[h], axis=1, keepdims=True)
        result = (accum_ref[h] / total).astype(BF16)
        clean_ref[:, lanes] = result[:ROWS]
        noisy_ref[:, lanes] = result[ROWS:]


def shards(hidden, block_ids, decode_order, step_cut, mask_embed, q_weight, k_weight, v_weight):
    ids = block_ids.reshape(1, ROWS)
    flag, mask_q, mask_kv = call(
        mask_kernel,
        [((ROWS, HEAD), F32), ((16, GROUP * HEAD), BF16), ((16, 2 * HEAD), BF16)],
        [ids, decode_order.reshape(1, ROWS), step_cut.reshape(1, -1), mask_embed.reshape(1, -1), q_weight, k_weight, v_weight],
        (1 << 28, 6 << 20),
    )
    mine = [hidden] + [lax.ppermute(hidden, "kv", kv_pairs(d, 0)) for d in (1, 2, 3)]
    pieces = []
    for piece in mine:
        pieces += [piece, lax.ppermute(piece, "kv", kv_pairs(0, 1))]
    x, kv, kv_noisy, up, down = call(
        kv_kernel,
        [
            ((ROWS, 8 * WIDTH), BF16),
            ((ROWS, 2 * HEAD), BF16),
            ((ROWS, 2 * HEAD), BF16),
            ((ROWS + BLOCK + 16, 2 * HEAD), BF16),
            ((2 * BLOCK + 16, 2 * HEAD), BF16),
        ],
        pieces + [k_weight, v_weight, flag, mask_kv, ids],
        (1 << 29, 3 << 20),
    )
    pair = lax.ppermute(kv, "ctx", ctx_pairs(0, 0, 1))
    k = jnp.stack([kv[:, :HEAD], pair[:, :HEAD]])
    v = jnp.stack([kv[:, HEAD:], pair[:, HEAD:]])
    ks = jnp.stack([k] + [lax.ppermute(k, "ctx", ctx_pairs(0, d, 0)) for d in (1, 2, 3)])
    vs = jnp.stack([v] + [lax.ppermute(v, "ctx", ctx_pairs(d, 0, 0)) for d in (1, 2, 3)])
    count = 32
    up = lax.ppermute(up, "ctx", [(i, (i + 1) % count) for i in range(count)])
    down = lax.ppermute(down, "ctx", [(i, (i - 1) % count) for i in range(count)])
    (q,) = call(
        q_kernel,
        [((GROUP, 2 * ROWS, HEAD), BF16)],
        [x, q_weight, flag, mask_q],
        (1 << 30, 5 << 20),
    )
    state = [((GROUP, 2 * ROWS, HEAD), F32)] * 3
    near = call(
        near_kernel,
        state,
        [q, kv, kv_noisy, up, down, ids],
        (1 << 30, 2 << 20),
        [pltpu.VMEM((4 * ROWS, HEAD), BF16)] * 2,
    )
    all_k = [ks] + [lax.ppermute(ks, "ctx", ctx_pairs(d, 0, 0)) for d in (1, 2, 3)]
    all_v = [vs] + [lax.ppermute(vs, "ctx", ctx_pairs(0, d, 0)) for d in (1, 2, 3)]
    return tuple(
        call(
            far_kernel,
            [((ROWS, GROUP * HEAD), BF16)] * 2,
            [q, *all_k, *all_v, *near],
            (1 << 32, 4 << 20),
            [pltpu.VMEM((GROUP, 2 * ROWS, HEAD), F32)] * 3,
        )
    )


def solution(mesh):
    return jax.shard_map(
        shards,
        mesh=mesh,
        in_specs=(
            P("ctx", "kv"),
            P("ctx"),
            P("ctx"),
            P(),
            P(),
            P(None, "kv"),
            P(None, "kv"),
            P(None, "kv"),
        ),
        out_specs=(P("ctx", "kv"), P("ctx", "kv")),
        check_vma=False,
    )
```

```python
import math

import jax
import jax.numpy as jnp
from jax import lax
from jax.experimental import pallas as pl
from jax.experimental.pallas import tpu as pltpu
from jax.sharding import PartitionSpec as P

ROWS = 128
HEAD = 128
GROUP = 4
WIDTH = 512
BLOCK = 32
LAST = 31
LOW = -1e30
FAR = 1e6
POWER = math.log2(math.e) / math.sqrt(HEAD)
LIMIT = 48 * 1024 * 1024
F32 = jnp.float32
BF16 = jnp.bfloat16


def ctx_pairs(dy, dx, dz):
    pairs = []
    for i in range(32):
        y, x, z = i // 8, (i // 2) % 4, i % 2
        pairs.append((i, (((y + dy) % 4) * 4 + (x + dx) % 4) * 2 + (z + dz) % 2))
    return pairs


def kv_pairs(dz, dc):
    pairs = []
    for i in range(8):
        z, c = i // 2, i % 2
        pairs.append((i, ((z + dz) % 4) * 2 + (c + dc) % 2))
    return pairs


def dot(a, b):
    return jnp.dot(a, b, preferred_element_type=F32)


def dot_t(a, b):
    return lax.dot_general(a, b, (((1,), (1,)), ((), ())), preferred_element_type=F32)


def call(kernel, outs, args, cost, scratch=()):
    spec = pl.BlockSpec(memory_space=pltpu.VMEM)
    return pl.pallas_call(
        kernel,
        out_shape=[jax.ShapeDtypeStruct(s, t) for s, t in outs],
        in_specs=[spec] * len(args),
        out_specs=[spec] * len(outs),
        scratch_shapes=list(scratch),
        compiler_params=pltpu.CompilerParams(vmem_limit_bytes=LIMIT),
        cost_estimate=pl.CostEstimate(flops=cost[0], bytes_accessed=cost[1], transcendentals=0),
    )(*args)


def column(row):
    square = (ROWS, ROWS)
    same = lax.broadcasted_iota(jnp.int32, square, 0) == lax.broadcasted_iota(jnp.int32, square, 1)
    return jnp.sum(jnp.where(same, jnp.broadcast_to(row, square), 0.0), axis=1, keepdims=True)


def mask_kernel(ids_ref, order_ref, cut_ref, embed_ref, wq_ref, wk_ref, wv_ref, flag_ref, code_ref, mq_ref, mkv_ref):
    code_ref[...] = jnp.broadcast_to(ids_ref[...] * 32 + order_ref[...], (8, ROWS))
    ids = column(ids_ref[...].astype(F32))
    order = column(order_ref[...].astype(F32))
    blocks = cut_ref.shape[1]
    spots = lax.broadcasted_iota(jnp.int32, (ROWS, blocks), 1).astype(F32)
    cuts = jnp.broadcast_to(cut_ref[...].astype(F32), (ROWS, blocks))
    cut = jnp.sum(jnp.where(spots == ids, cuts, 0.0), axis=1, keepdims=True)
    flag_ref[...] = jnp.broadcast_to(jnp.where(order >= cut, 1.0, 0.0), (ROWS, HEAD))
    embed = jnp.broadcast_to(embed_ref[...], (16, embed_ref.shape[1]))
    mq_ref[...] = dot(embed, wq_ref[...]).astype(BF16)
    mkv_ref[:, :HEAD] = dot(embed, wk_ref[...]).astype(BF16)
    mkv_ref[:, HEAD:] = dot(embed, wv_ref[...]).astype(BF16)


def kv_kernel(*refs):
    pieces = refs[:8]
    wk_ref, wv_ref, flag_ref, mkv_ref = refs[8:12]
    x_ref, kv_ref, kvn_ref = refs[12:]
    me = lax.axis_index("kv")
    for dz in range(4):
        for dc in range(2):
            source = lax.rem(me // 2 + 4 - dz, 4) * 2 + lax.rem(me + dc, 2)
            x_ref[:, pl.ds(pl.multiple_of(source * WIDTH, WIDTH), WIDTH)] = pieces[2 * dz + dc][...]
    x = x_ref[...]
    masked = flag_ref[...] > 0.5
    for part, w_ref in enumerate((wk_ref, wv_ref)):
        lanes = slice(part * HEAD, (part + 1) * HEAD)
        clean = dot(x, w_ref[...])
        fixed = jnp.broadcast_to(mkv_ref[0:1, lanes].astype(F32), (ROWS, HEAD))
        kv_ref[:, lanes] = clean.astype(BF16)
        kvn_ref[:, lanes] = jnp.where(masked, fixed, clean).astype(BF16)


def q_kernel(x_ref, wq_ref, flag_ref, mq_ref, q_ref):
    masked = flag_ref[...] > 0.5
    x = x_ref[...]
    for h in range(GROUP):
        lanes = slice(h * HEAD, (h + 1) * HEAD)
        clean = dot(x, wq_ref[:, lanes])
        fixed = jnp.broadcast_to(mq_ref[0:1, lanes].astype(F32), (ROWS, HEAD))
        q_ref[h, :ROWS, :] = clean.astype(BF16)
        q_ref[h, ROWS:, :] = jnp.where(masked, fixed, clean).astype(BF16)


def near_kernel(q_ref, kv_ref, kvn_ref, ids_ref, top_ref, total_ref, accum_ref):
    row = ids_ref[...].astype(F32)
    query = jnp.broadcast_to(column(row), (ROWS, ROWS))
    key = jnp.broadcast_to(row, (ROWS, ROWS))
    zero = jnp.zeros((ROWS, ROWS), F32)
    low = jnp.full((ROWS, ROWS), LOW, F32)
    clean_bias = jnp.concatenate([jnp.where(key <= query, zero, low), low], axis=1)
    noisy_bias = jnp.concatenate([jnp.where(key < query, zero, low), jnp.where(key == query, zero, low)], axis=1)
    bias = jnp.concatenate([clean_bias, noisy_bias], axis=0)
    keys = jnp.concatenate([kv_ref[:, :HEAD], kvn_ref[:, :HEAD]], axis=0)
    values = jnp.concatenate([kv_ref[:, HEAD:], kvn_ref[:, HEAD:]], axis=0)
    for h in range(GROUP):
        scores = jnp.where(bias < -1.0, LOW, dot_t(q_ref[h], keys))
        top = jnp.max(scores, axis=1, keepdims=True)
        probs = jnp.exp2((scores - top) * POWER)
        top_ref[h] = jnp.broadcast_to(top, (2 * ROWS, HEAD))
        total_ref[h] = probs[:, :HEAD] + probs[:, HEAD:]
        accum_ref[h] = dot(probs.astype(BF16), values)


def far_kernel(*refs):
    q_ref = refs[0]
    k_refs, v_refs = refs[1:5], refs[5:9]
    top_in, total_in, accum_in = refs[9:12]
    ids_ref, code_ref, up_ref, down_ref, cut_ref, mkv_ref = refs[12:18]
    clean_ref, noisy_ref = refs[18:20]
    top_ref, total_ref, accum_ref = refs[20:]
    me = lax.axis_index("ctx")
    y, x, z = me // 8, lax.rem(me // 2, 4), lax.rem(me, 2)

    hop = jnp.where(z == 0, 1, 0)
    wrap = (z == 0) & (x == 0)
    old_y = jnp.where(wrap, 1, 0)
    step = jnp.where(z == 0, 0, 3)
    beyond = (z == 1) & (x == 3)
    new_y = jnp.where(beyond, 3, 0)
    k_old = jnp.where(wrap, k_refs[1][hop, 1], k_refs[0][hop, 1])
    v_old = jnp.where(z == 0, v_refs[1][old_y, 1], v_refs[0][old_y, 1])
    k_new = jnp.where(beyond, k_refs[3][step, 1], k_refs[0][step, 1])[:BLOCK]
    v_new = jnp.where(z == 0, v_refs[0][new_y, 1], v_refs[3][new_y, 1])[:BLOCK]

    code = code_ref[...]
    own = (code // 32).astype(F32)
    old_ids = jnp.where(me > 0, (up_ref[...] // 32).astype(F32), FAR)
    new_ids = jnp.where(me < LAST, (down_ref[...] // 32).astype(F32), FAR)
    old_order = lax.rem(up_ref[...], 32).astype(F32)
    new_order = lax.rem(down_ref[...], 32).astype(F32)
    blocks = cut_ref.shape[1]
    spots = lax.broadcasted_iota(jnp.int32, (8, blocks), 1).astype(F32)
    cuts = jnp.broadcast_to(cut_ref[...].astype(F32), (8, blocks))
    first_cut = jnp.sum(jnp.where(spots == own[:, 0:1], cuts, 0.0), axis=1, keepdims=True)
    last_cut = jnp.sum(jnp.where(spots == own[:, ROWS - 1 : ROWS], cuts, 0.0), axis=1, keepdims=True)
    old_masked = column(jnp.where(old_order >= first_cut, 1.0, 0.0)[0:1])[ROWS - BLOCK :]
    new_masked = column(jnp.where(new_order >= last_cut, 1.0, 0.0)[0:1])[:BLOCK]

    def noisy(masked, clean, lanes):
        fixed = jnp.broadcast_to(mkv_ref[0:1, lanes].astype(F32), clean.shape)
        flag = jnp.broadcast_to(masked, clean.shape) > 0.5
        return jnp.where(flag, fixed, clean.astype(F32)).astype(BF16)

    def rim(old, new, lanes):
        parts = [old, new, noisy(old_masked, old[ROWS - BLOCK :], lanes), noisy(new_masked, new, lanes)]
        return jnp.concatenate(parts + [jnp.zeros((BLOCK, HEAD), BF16)], axis=0)

    k_rim = rim(k_old, k_new, slice(0, HEAD))
    v_rim = rim(v_old, v_new, slice(HEAD, 2 * HEAD))
    lane = lax.broadcasted_iota(jnp.int32, (8, ROWS), 1)
    mixed = jnp.where(
        lane < 32,
        new_ids,
        jnp.where(lane < 64, pltpu.roll(old_ids, 64, 1), jnp.where(lane < 96, pltpu.roll(new_ids, 64, 1), -5.0)),
    )
    square = (ROWS, ROWS)
    query = jnp.broadcast_to(column(own[0:1]), square)
    old_key = jnp.broadcast_to(old_ids[0:1], square)
    mixed_key = jnp.broadcast_to(mixed[0:1], square)
    early = lax.broadcasted_iota(jnp.int32, square, 1) < 32
    zero = jnp.zeros(square, F32)
    low = jnp.full(square, LOW, F32)
    clean_bias = [
        jnp.where(old_key <= query, zero, low),
        jnp.where(early, jnp.where(mixed_key <= query, zero, low), low),
    ]
    noisy_bias = [
        jnp.where(old_key < query, zero, low),
        jnp.where(early, jnp.where(mixed_key < query, zero, low), jnp.where(mixed_key == query, zero, low)),
    ]
    bias = jnp.concatenate([jnp.concatenate(clean_bias, axis=1), jnp.concatenate(noisy_bias, axis=1)], axis=0)

    def scores_of(step):
        dy, h = step
        if dy < 0:
            return jnp.where(bias < -1.0, LOW, dot_t(q_ref[h], k_rim))
        return dot_t(q_ref[h], k_refs[dy][...].reshape(8 * ROWS, HEAD))

    def absorb(step, scores):
        dy, h = step
        parts = [scores[:, j : j + ROWS] for j in range(0, scores.shape[1], ROWS)]
        if dy in (0, 1):
            for j in range(8):
                there = lax.rem(y + 4 - dy, 4) * 8 + lax.rem(x + 4 - j // 2, 4) * 2 + lax.rem(z + j, 2)
                parts[j] = jnp.where(there < me - 1, parts[j], LOW)
        best = parts[0]
        for part in parts[1:]:
            best = jnp.maximum(best, part)
        best = jnp.max(best, axis=1, keepdims=True)
        if dy > 1:
            best = jnp.where(y >= dy, best, LOW)
        old = top_in[h] if dy < 0 else top_ref[h]
        top = jnp.maximum(old, best)
        factor = jnp.exp2((old - top) * POWER)
        level = jnp.where(y >= dy, top, -LOW) if dy > 1 else top
        probs = [jnp.exp2((part - level) * POWER) for part in parts]
        total = (total_in[h] if dy < 0 else total_ref[h]) * factor
        for part in probs:
            total = total + part
        if dy < 0:
            values = v_rim
        else:
            values = jnp.concatenate([v_refs[dx][dy].reshape(2 * ROWS, HEAD) for dx in range(4)], axis=0)
        probs = jnp.concatenate([part.astype(BF16) for part in probs], axis=1)
        accum = (accum_in[h] if dy < 0 else accum_ref[h]) * factor + dot(probs, values)
        if dy < 3:
            top_ref[h] = top
            total_ref[h] = total
            accum_ref[h] = accum
            return
        lanes = slice(h * HEAD, (h + 1) * HEAD)
        result = (accum / jnp.sum(total, axis=1, keepdims=True)).astype(BF16)
        clean_ref[:, lanes] = result[:ROWS]
        noisy_ref[:, lanes] = result[ROWS:]

    steps = [(dy, h) for dy in (-1, 0, 1, 2, 3) for h in range(GROUP)]
    scores = scores_of(steps[0])
    for now, later in zip(steps, steps[1:] + [None]):
        following = None if later is None else scores_of(later)
        absorb(now, scores)
        scores = following


def shards(hidden, block_ids, decode_order, step_cut, mask_embed, q_weight, k_weight, v_weight):
    ids = block_ids.reshape(1, ROWS)
    order = decode_order.reshape(1, ROWS)
    cuts = step_cut.reshape(1, -1)
    flag, code, mask_q, mask_kv = call(
        mask_kernel,
        [((ROWS, HEAD), F32), ((8, ROWS), jnp.int32), ((16, GROUP * HEAD), BF16), ((16, 2 * HEAD), BF16)],
        [ids, order, cuts, mask_embed.reshape(1, -1), q_weight, k_weight, v_weight],
        (1 << 28, 6 << 20),
    )
    moved = [lax.ppermute(hidden, "kv", kv_pairs(d, 0)) for d in (1, 2, 3)]
    count = 32
    up = lax.ppermute(code, "ctx", [(i, (i + 1) % count) for i in range(count)])
    down = lax.ppermute(code, "ctx", [(i, (i - 1) % count) for i in range(count)])
    flag, code, mask_q, mask_kv, up, down = lax.optimization_barrier((flag, code, mask_q, mask_kv, up, down))
    pieces = [hidden, lax.ppermute(hidden, "kv", kv_pairs(0, 1))]
    for piece in moved:
        piece, _, _ = lax.optimization_barrier((piece, up, flag))
        pieces += [piece, lax.ppermute(piece, "kv", kv_pairs(0, 1))]
    x, kv, kv_noisy = call(
        kv_kernel,
        [((ROWS, 8 * WIDTH), BF16), ((ROWS, 2 * HEAD), BF16), ((ROWS, 2 * HEAD), BF16)],
        [*pieces, k_weight, v_weight, flag, mask_kv],
        (1 << 29, 3 << 20),
    )
    pair = lax.ppermute(kv, "ctx", ctx_pairs(0, 0, 1))
    k = jnp.stack([kv[:, :HEAD], pair[:, :HEAD]])
    v = jnp.stack([kv[:, HEAD:], pair[:, HEAD:]])
    ks = jnp.stack([k] + [lax.ppermute(k, "ctx", ctx_pairs(0, d, 0)) for d in (1, 2, 3)])
    vs = jnp.stack([v] + [lax.ppermute(v, "ctx", ctx_pairs(d, 0, 0)) for d in (1, 2, 3)])
    (q,) = call(
        q_kernel,
        [((GROUP, 2 * ROWS, HEAD), BF16)],
        [x, q_weight, flag, mask_q],
        (1 << 30, 5 << 20),
    )
    near = call(
        near_kernel,
        [((GROUP, 2 * ROWS, HEAD), F32)] * 3,
        [q, kv, kv_noisy, ids],
        (1 << 30, 2 << 20),
    )
    all_k = [ks] + [lax.ppermute(ks, "ctx", ctx_pairs(d, 0, 0)) for d in (1, 2, 3)]
    all_v = [vs] + [lax.ppermute(vs, "ctx", ctx_pairs(0, d, 0)) for d in (1, 2, 3)]
    return tuple(
        call(
            far_kernel,
            [((ROWS, GROUP * HEAD), BF16)] * 2,
            [q, *all_k, *all_v, *near, ids, code, up, down, cuts, mask_kv],
            (1 << 32, 4 << 20),
            [pltpu.VMEM((GROUP, 2 * ROWS, HEAD), F32)] * 3,
        )
    )


def solution(mesh):
    return jax.shard_map(
        shards,
        mesh=mesh,
        in_specs=(
            P("ctx", "kv"),
            P("ctx"),
            P("ctx"),
            P(),
            P(),
            P(None, "kv"),
            P(None, "kv"),
            P(None, "kv"),
        ),
        out_specs=(P("ctx", "kv"), P("ctx", "kv")),
        check_vma=False,
    )
```

```python
import math

import jax
import jax.numpy as jnp
from jax import lax
from jax.experimental import pallas as pl
from jax.experimental.pallas import tpu as pltpu
from jax.sharding import PartitionSpec as P

ROWS = 128
HEAD = 128
GROUP = 4
PAD = 16
WIDTH = 512
BLOCK = 32
LAST = 31
LOW = -1e30
FAR = 1e6
POWER = math.log2(math.e) / math.sqrt(HEAD)
LIMIT = 48 * 1024 * 1024
F32 = jnp.float32
BF16 = jnp.bfloat16


def ctx_pairs(dy, dx, dz):
    pairs = []
    for i in range(32):
        y, x, z = i // 8, (i // 2) % 4, i % 2
        pairs.append((i, (((y + dy) % 4) * 4 + (x + dx) % 4) * 2 + (z + dz) % 2))
    return pairs


def kv_pairs(dz, dc):
    pairs = []
    for i in range(8):
        z, c = i // 2, i % 2
        pairs.append((i, ((z + dz) % 4) * 2 + (c + dc) % 2))
    return pairs


def dot(a, b):
    return jnp.dot(a, b, preferred_element_type=F32)


def dot_t(a, b):
    return lax.dot_general(a, b, (((1,), (1,)), ((), ())), preferred_element_type=F32)


def call(kernel, outs, args, cost, scratch=(), space=pltpu.VMEM):
    spec = pl.BlockSpec(memory_space=pltpu.VMEM)
    return pl.pallas_call(
        kernel,
        out_shape=[jax.ShapeDtypeStruct(s, t) for s, t in outs],
        in_specs=[pl.BlockSpec(memory_space=space)] * len(args),
        out_specs=[spec] * len(outs),
        scratch_shapes=list(scratch),
        compiler_params=pltpu.CompilerParams(vmem_limit_bytes=LIMIT),
        cost_estimate=pl.CostEstimate(flops=cost[0], bytes_accessed=cost[1], transcendentals=0),
    )(*args)


def column(row):
    square = (ROWS, ROWS)
    same = lax.broadcasted_iota(jnp.int32, square, 0) == lax.broadcasted_iota(jnp.int32, square, 1)
    return jnp.sum(jnp.where(same, jnp.broadcast_to(row, square), 0.0), axis=1, keepdims=True)


def prep_kernel(*refs):
    hidden_hbm, wk_hbm, wv_hbm, ids_hbm, order_hbm, embed_hbm = refs[:6]
    own_ref, wk_ref, wv_ref, code_ref, pad_ref = refs[6:11]
    ids_ref, order_ref, embed_ref, sems = refs[11:]
    pairs = (
        (ids_hbm, ids_ref),
        (order_hbm, order_ref),
        (embed_hbm, embed_ref),
        (hidden_hbm, own_ref),
        (wk_hbm, wk_ref),
        (wv_hbm, wv_ref),
    )
    copies = [pltpu.make_async_copy(a, b, sems.at[i]) for i, (a, b) in enumerate(pairs)]
    for copy in copies:
        copy.start()
    for copy in copies:
        copy.wait()
    ids = jnp.broadcast_to(ids_ref[...].astype(F32), (8, ROWS))
    order = jnp.broadcast_to(order_ref[...].astype(F32), (8, ROWS))
    code_ref[...] = jnp.concatenate([ids, order], axis=0).astype(BF16)
    pad_ref[...] = jnp.broadcast_to(embed_ref[...], pad_ref.shape)


def kv_kernel(*refs):
    pieces = refs[:8]
    pad_ref, wk_ref, wv_ref, code_ref = refs[8:12]
    x_ref, kv_ref, mkv_ref = refs[12:]
    me = lax.axis_index("kv")
    for dz in range(4):
        for dc in range(2):
            source = lax.rem(me // 2 + 4 - dz, 4) * 2 + lax.rem(me + dc, 2)
            x_ref[:ROWS, pl.ds(pl.multiple_of(source * WIDTH, WIDTH), WIDTH)] = pieces[2 * dz + dc][...]
    x_ref[ROWS:, :] = pad_ref[...]
    x = x_ref[...]
    for part, w_ref in enumerate((wk_ref, wv_ref)):
        lanes = slice(part * HEAD, (part + 1) * HEAD)
        product = dot(x, w_ref[...]).astype(BF16)
        kv_ref[:ROWS, lanes] = product[:ROWS]
        kv_ref[ROWS:, lanes] = code_ref[...]
        mkv_ref[:, lanes] = product[ROWS:]


def q_kernel(x_ref, wq_ref, code_ref, cut_ref, q_ref, flag_ref, own_cut_ref):
    code = code_ref[...].astype(F32)
    ids = column(code[0:1])
    order = column(code[8:9])
    blocks = cut_ref.shape[1]
    spots = lax.broadcasted_iota(jnp.int32, (ROWS, blocks), 1).astype(F32)
    cuts = jnp.broadcast_to(cut_ref[...].astype(F32), (ROWS, blocks))
    cut = jnp.sum(jnp.where(spots == ids, cuts, 0.0), axis=1, keepdims=True)
    flag = jnp.broadcast_to(jnp.where(order >= cut, 1.0, 0.0), (ROWS, HEAD))
    flag_ref[...] = flag
    own_cut_ref[...] = jnp.broadcast_to(cut, (ROWS, HEAD))
    x = x_ref[...]
    for h in range(GROUP):
        product = dot(x, wq_ref[:, h * HEAD : (h + 1) * HEAD])
        clean = product[:ROWS]
        fixed = jnp.broadcast_to(product[ROWS : ROWS + 1], (ROWS, HEAD))
        q_ref[h, :ROWS, :] = clean.astype(BF16)
        q_ref[h, ROWS:, :] = jnp.where(flag > 0.5, fixed, clean).astype(BF16)


def near_kernel(q_ref, kv_ref, mkv_ref, flag_ref, code_ref, top_ref, total_ref, accum_ref):
    masked = flag_ref[...] > 0.5

    def both(lanes):
        clean = kv_ref[:ROWS, lanes]
        fixed = jnp.broadcast_to(mkv_ref[0:1, lanes].astype(F32), (ROWS, HEAD))
        return jnp.concatenate([clean, jnp.where(masked, fixed, clean.astype(F32)).astype(BF16)], axis=0)

    row = code_ref[...].astype(F32)[0:1]
    query = jnp.broadcast_to(column(row), (ROWS, ROWS))
    key = jnp.broadcast_to(row, (ROWS, ROWS))
    zero = jnp.zeros((ROWS, ROWS), F32)
    low = jnp.full((ROWS, ROWS), LOW, F32)
    clean_bias = jnp.concatenate([jnp.where(key <= query, zero, low), low], axis=1)
    noisy_bias = jnp.concatenate([jnp.where(key < query, zero, low), jnp.where(key == query, zero, low)], axis=1)
    bias = jnp.concatenate([clean_bias, noisy_bias], axis=0)
    keys = both(slice(0, HEAD))
    values = both(slice(HEAD, 2 * HEAD))
    for h in range(GROUP):
        scores = jnp.where(bias < -1.0, LOW, dot_t(q_ref[h], keys))
        top = jnp.max(scores, axis=1, keepdims=True)
        probs = jnp.exp2((scores - top) * POWER)
        top_ref[h] = jnp.broadcast_to(top, (2 * ROWS, HEAD))
        total_ref[h] = probs[:, :HEAD] + probs[:, HEAD:]
        accum_ref[h] = dot(probs.astype(BF16), values)


def far_kernel(*refs):
    q_ref = refs[0]
    k_refs, v_refs = refs[1:5], refs[5:9]
    top_in, total_in, accum_in = refs[9:12]
    code_ref, pair_ref, swap_ref, own_cut_ref, mkv_ref = refs[12:17]
    clean_ref, noisy_ref = refs[17:19]
    top_ref, total_ref, accum_ref = refs[19:]
    me = lax.axis_index("ctx")
    y, x, z = me // 8, lax.rem(me // 2, 4), lax.rem(me, 2)

    hop = jnp.where(z == 0, 1, 0)
    wrap = (z == 0) & (x == 0)
    old_y = jnp.where(wrap, 1, 0)
    step = jnp.where(z == 0, 0, 3)
    beyond = (z == 1) & (x == 3)
    new_y = jnp.where(beyond, 3, 0)
    k_old = jnp.where(wrap, k_refs[1][hop, 1], k_refs[0][hop, 1])
    v_old = jnp.where(z == 0, v_refs[1][old_y, 1], v_refs[0][old_y, 1])
    k_new = jnp.where(beyond, k_refs[3][step, 1], k_refs[0][step, 1])[:BLOCK]
    v_new = jnp.where(z == 0, v_refs[0][new_y, 1], v_refs[3][new_y, 1])[:BLOCK]

    own = code_ref[...].astype(F32)[:8]
    partner = pair_ref[ROWS:, :HEAD].astype(F32)
    other = swap_ref[...].astype(F32)
    old_code = jnp.where(z == 0, other, partner)
    new_code = jnp.where(z == 0, partner, other)
    old_ids, old_order = jnp.where(me > 0, old_code[:8], FAR), old_code[8:]
    new_ids, new_order = jnp.where(me < LAST, new_code[:8], FAR), new_code[8:]
    first_cut = own_cut_ref[0:1, :]
    last_cut = own_cut_ref[ROWS - 1 : ROWS, :]
    old_masked = column(jnp.where(old_order[0:1] >= first_cut, 1.0, 0.0))[ROWS - BLOCK :]
    new_masked = column(jnp.where(new_order[0:1] >= last_cut, 1.0, 0.0))[:BLOCK]

    def noisy(masked, clean, lanes):
        fixed = jnp.broadcast_to(mkv_ref[0:1, lanes].astype(F32), clean.shape)
        flag = jnp.broadcast_to(masked, clean.shape) > 0.5
        return jnp.where(flag, fixed, clean.astype(F32)).astype(BF16)

    def rim(old, new, lanes):
        parts = [old, new, noisy(old_masked, old[ROWS - BLOCK :], lanes), noisy(new_masked, new, lanes)]
        return jnp.concatenate(parts + [jnp.zeros((BLOCK, HEAD), BF16)], axis=0)

    k_rim = rim(k_old, k_new, slice(0, HEAD))
    v_rim = rim(v_old, v_new, slice(HEAD, 2 * HEAD))
    lane = lax.broadcasted_iota(jnp.int32, (8, ROWS), 1)
    mixed = jnp.where(
        lane < 32,
        new_ids,
        jnp.where(lane < 64, pltpu.roll(old_ids, 64, 1), jnp.where(lane < 96, pltpu.roll(new_ids, 64, 1), -5.0)),
    )
    square = (ROWS, ROWS)
    query = jnp.broadcast_to(column(own[0:1]), square)
    old_key = jnp.broadcast_to(old_ids[0:1], square)
    mixed_key = jnp.broadcast_to(mixed[0:1], square)
    early = lax.broadcasted_iota(jnp.int32, square, 1) < 32
    zero = jnp.zeros(square, F32)
    low = jnp.full(square, LOW, F32)
    clean_bias = [
        jnp.where(old_key <= query, zero, low),
        jnp.where(early, jnp.where(mixed_key <= query, zero, low), low),
    ]
    noisy_bias = [
        jnp.where(old_key < query, zero, low),
        jnp.where(early, jnp.where(mixed_key < query, zero, low), jnp.where(mixed_key == query, zero, low)),
    ]
    bias = jnp.concatenate([jnp.concatenate(clean_bias, axis=1), jnp.concatenate(noisy_bias, axis=1)], axis=0)

    def scores_of(step):
        dy, h = step
        if dy < 0:
            return jnp.where(bias < -1.0, LOW, dot_t(q_ref[h], k_rim))
        return dot_t(q_ref[h], k_refs[dy][...].reshape(8 * ROWS, HEAD))

    def absorb(step, scores):
        dy, h = step
        parts = [scores[:, j : j + ROWS] for j in range(0, scores.shape[1], ROWS)]
        if dy in (0, 1):
            for j in range(8):
                there = lax.rem(y + 4 - dy, 4) * 8 + lax.rem(x + 4 - j // 2, 4) * 2 + lax.rem(z + j, 2)
                parts[j] = jnp.where(there < me - 1, parts[j], LOW)
        best = parts[0]
        for part in parts[1:]:
            best = jnp.maximum(best, part)
        best = jnp.max(best, axis=1, keepdims=True)
        if dy > 1:
            best = jnp.where(y >= dy, best, LOW)
        old = top_in[h] if dy < 0 else top_ref[h]
        top = jnp.maximum(old, best)
        factor = jnp.exp2((old - top) * POWER)
        level = jnp.where(y >= dy, top, -LOW) if dy > 1 else top
        probs = [jnp.exp2((part - level) * POWER) for part in parts]
        total = (total_in[h] if dy < 0 else total_ref[h]) * factor
        for part in probs:
            total = total + part
        if dy < 0:
            values = v_rim
        else:
            values = jnp.concatenate([v_refs[dx][dy].reshape(2 * ROWS, HEAD) for dx in range(4)], axis=0)
        probs = jnp.concatenate([part.astype(BF16) for part in probs], axis=1)
        accum = (accum_in[h] if dy < 0 else accum_ref[h]) * factor + dot(probs, values)
        if dy < 3:
            top_ref[h] = top
            total_ref[h] = total
            accum_ref[h] = accum
            return
        lanes = slice(h * HEAD, (h + 1) * HEAD)
        result = (accum / jnp.sum(total, axis=1, keepdims=True)).astype(BF16)
        clean_ref[:, lanes] = result[:ROWS]
        noisy_ref[:, lanes] = result[ROWS:]

    steps = [(dy, h) for dy in (-1, 0, 1, 2, 3) for h in range(GROUP)]
    scores = scores_of(steps[0])
    for now, later in zip(steps, steps[1:] + [None]):
        following = None if later is None else scores_of(later)
        absorb(now, scores)
        scores = following


def shards(hidden, block_ids, decode_order, step_cut, mask_embed, q_weight, k_weight, v_weight):
    ids = block_ids.reshape(1, ROWS)
    order = decode_order.reshape(1, ROWS)
    cuts = step_cut.reshape(1, -1)
    moved = [lax.ppermute(hidden, "kv", kv_pairs(d, 0)) for d in (1, 2, 3)]
    own, wk, wv, code, pad = call(
        prep_kernel,
        [
            (hidden.shape, BF16),
            (k_weight.shape, BF16),
            (v_weight.shape, BF16),
            ((PAD, ROWS), BF16),
            ((PAD, 8 * WIDTH), BF16),
        ],
        [hidden, k_weight, v_weight, ids, order, mask_embed.reshape(1, -1)],
        (1 << 20, 4 << 20),
        [
            pltpu.VMEM(ids.shape, jnp.int32),
            pltpu.VMEM(ids.shape, jnp.int32),
            pltpu.VMEM((1, 8 * WIDTH), BF16),
            pltpu.SemaphoreType.DMA((6,)),
        ],
        pltpu.HBM,
    )
    pieces = []
    for piece in (own, *moved):
        piece, _ = lax.optimization_barrier((piece, pad))
        pieces += [piece, lax.ppermute(piece, "kv", kv_pairs(0, 1))]
    x, kv, mask_kv = call(
        kv_kernel,
        [((ROWS + PAD, 8 * WIDTH), BF16), ((ROWS + PAD, 2 * HEAD), BF16), ((PAD, 2 * HEAD), BF16)],
        [*pieces, pad, wk, wv, code],
        (1 << 29, 3 << 20),
    )
    pair = lax.ppermute(kv, "ctx", ctx_pairs(0, 0, 1))
    swap = lax.ppermute(code, "ctx", [(i, (i + 2 * (i % 2) - 1) % 32) for i in range(32)])
    pair, swap = lax.optimization_barrier((pair, swap))
    k = jnp.stack([kv[:ROWS, :HEAD], pair[:ROWS, :HEAD]])
    v = jnp.stack([kv[:ROWS, HEAD:], pair[:ROWS, HEAD:]])
    k, v = lax.optimization_barrier((k, v))
    ks = jnp.stack([k] + [lax.ppermute(k, "ctx", ctx_pairs(0, d, 0)) for d in (1, 2, 3)])
    vs = jnp.stack([v] + [lax.ppermute(v, "ctx", ctx_pairs(d, 0, 0)) for d in (1, 2, 3)])
    q, flag, own_cut = call(
        q_kernel,
        [((GROUP, 2 * ROWS, HEAD), BF16), ((ROWS, HEAD), F32), ((ROWS, HEAD), F32)],
        [x, q_weight, code, cuts],
        (1 << 30, 5 << 20),
    )
    near = call(
        near_kernel,
        [((GROUP, 2 * ROWS, HEAD), F32)] * 3,
        [q, kv, mask_kv, flag, code],
        (1 << 30, 2 << 20),
    )
    all_k = [ks] + [lax.ppermute(ks, "ctx", ctx_pairs(d, 0, 0)) for d in (1, 2, 3)]
    all_v = [vs] + [lax.ppermute(vs, "ctx", ctx_pairs(0, d, 0)) for d in (1, 2, 3)]
    return tuple(
        call(
            far_kernel,
            [((ROWS, GROUP * HEAD), BF16)] * 2,
            [q, *all_k, *all_v, *near, code, pair, swap, own_cut, mask_kv],
            (1 << 32, 4 << 20),
            [pltpu.VMEM((GROUP, 2 * ROWS, HEAD), F32)] * 3,
        )
    )


def solution(mesh):
    return jax.shard_map(
        shards,
        mesh=mesh,
        in_specs=(
            P("ctx", "kv"),
            P("ctx"),
            P("ctx"),
            P(),
            P(),
            P(None, "kv"),
            P(None, "kv"),
            P(None, "kv"),
        ),
        out_specs=(P("ctx", "kv"), P("ctx", "kv")),
        check_vma=False,
    )
```

```python
import math

import jax
import jax.numpy as jnp
from jax import lax
from jax.experimental import pallas as pl
from jax.experimental.pallas import tpu as pltpu
from jax.sharding import PartitionSpec as P

ROWS = 128
HEAD = 128
GROUP = 4
PAD = 16
WIDTH = 512
BLOCK = 32
LAST = 31
LOW = -1e30
FAR = 1e6
POWER = math.log2(math.e) / math.sqrt(HEAD)
LIMIT = 48 * 1024 * 1024
F32 = jnp.float32
BF16 = jnp.bfloat16


def ctx_pairs(dy, dx, dz):
    pairs = []
    for i in range(32):
        y, x, z = i // 8, (i // 2) % 4, i % 2
        pairs.append((i, (((y + dy) % 4) * 4 + (x + dx) % 4) * 2 + (z + dz) % 2))
    return pairs


def kv_pairs(dz, dc):
    pairs = []
    for i in range(8):
        z, c = i // 2, i % 2
        pairs.append((i, ((z + dz) % 4) * 2 + (c + dc) % 2))
    return pairs


def dot(a, b):
    return jnp.dot(a, b, preferred_element_type=F32)


def dot_t(a, b):
    return lax.dot_general(a, b, (((1,), (1,)), ((), ())), preferred_element_type=F32)


def call(kernel, outs, args, cost, scratch=(), space=pltpu.VMEM):
    spec = pl.BlockSpec(memory_space=pltpu.VMEM)
    return pl.pallas_call(
        kernel,
        out_shape=[jax.ShapeDtypeStruct(s, t) for s, t in outs],
        in_specs=[pl.BlockSpec(memory_space=space)] * len(args),
        out_specs=[spec] * len(outs),
        scratch_shapes=list(scratch),
        compiler_params=pltpu.CompilerParams(vmem_limit_bytes=LIMIT),
        cost_estimate=pl.CostEstimate(flops=cost[0], bytes_accessed=cost[1], transcendentals=0),
    )(*args)


def column(row):
    square = (ROWS, ROWS)
    same = lax.broadcasted_iota(jnp.int32, square, 0) == lax.broadcasted_iota(jnp.int32, square, 1)
    return jnp.sum(jnp.where(same, jnp.broadcast_to(row, square), 0.0), axis=1, keepdims=True)


def prep_kernel(*refs):
    hidden_hbm, wk_hbm, wv_hbm, ids_hbm, order_hbm, embed_hbm = refs[:6]
    own_ref, wk_ref, wv_ref, code_ref, pad_ref = refs[6:11]
    ids_ref, order_ref, embed_ref, sems = refs[11:]
    pairs = (
        (ids_hbm, ids_ref),
        (order_hbm, order_ref),
        (embed_hbm, embed_ref),
        (hidden_hbm, own_ref),
        (wk_hbm, wk_ref),
        (wv_hbm, wv_ref),
    )
    copies = [pltpu.make_async_copy(a, b, sems.at[i]) for i, (a, b) in enumerate(pairs)]
    for copy in copies:
        copy.start()
    for copy in copies:
        copy.wait()
    ids = jnp.broadcast_to(ids_ref[...].astype(F32), (8, ROWS))
    order = jnp.broadcast_to(order_ref[...].astype(F32), (8, ROWS))
    code_ref[...] = jnp.concatenate([ids, order], axis=0).astype(BF16)
    pad_ref[...] = jnp.broadcast_to(embed_ref[...], pad_ref.shape)


def kv_kernel(*refs):
    pieces = refs[:8]
    pad_ref, wk_ref, wv_ref, code_ref = refs[8:12]
    x_ref, kv_ref, mkv_ref, send_ref = refs[12:]
    me = lax.axis_index("kv")
    for dz in range(4):
        for dc in range(2):
            source = lax.rem(me // 2 + 4 - dz, 4) * 2 + lax.rem(me + dc, 2)
            x_ref[:ROWS, pl.ds(pl.multiple_of(source * WIDTH, WIDTH), WIDTH)] = pieces[2 * dz + dc][...]
    x_ref[ROWS:, :] = pad_ref[...]
    send_ref[...] = code_ref[...]
    x = x_ref[...]
    for part, w_ref in enumerate((wk_ref, wv_ref)):
        lanes = slice(part * HEAD, (part + 1) * HEAD)
        product = dot(x, w_ref[...]).astype(BF16)
        kv_ref[:ROWS, lanes] = product[:ROWS]
        kv_ref[ROWS:, lanes] = code_ref[...]
        mkv_ref[:, lanes] = product[ROWS:]


def q_kernel(x_ref, wq_ref, code_ref, cut_ref, q_ref, flag_ref, own_cut_ref):
    code = code_ref[...].astype(F32)
    ids = column(code[0:1])
    order = column(code[8:9])
    blocks = cut_ref.shape[1]
    spots = lax.broadcasted_iota(jnp.int32, (ROWS, blocks), 1).astype(F32)
    cuts = jnp.broadcast_to(cut_ref[...].astype(F32), (ROWS, blocks))
    cut = jnp.sum(jnp.where(spots == ids, cuts, 0.0), axis=1, keepdims=True)
    flag = jnp.broadcast_to(jnp.where(order >= cut, 1.0, 0.0), (ROWS, HEAD))
    flag_ref[...] = flag
    own_cut_ref[...] = jnp.broadcast_to(cut, (ROWS, HEAD))
    x = x_ref[...]
    for h in range(GROUP):
        product = dot(x, wq_ref[:, h * HEAD : (h + 1) * HEAD])
        clean = product[:ROWS]
        fixed = jnp.broadcast_to(product[ROWS : ROWS + 1], (ROWS, HEAD))
        q_ref[h, :ROWS, :] = clean.astype(BF16)
        q_ref[h, ROWS:, :] = jnp.where(flag > 0.5, fixed, clean).astype(BF16)


def near_kernel(q_ref, kv_ref, mkv_ref, flag_ref, code_ref, top_ref, total_ref, accum_ref):
    masked = flag_ref[...] > 0.5

    def both(lanes):
        clean = kv_ref[:ROWS, lanes]
        fixed = jnp.broadcast_to(mkv_ref[0:1, lanes].astype(F32), (ROWS, HEAD))
        return jnp.concatenate([clean, jnp.where(masked, fixed, clean.astype(F32)).astype(BF16)], axis=0)

    row = code_ref[...].astype(F32)[0:1]
    query = jnp.broadcast_to(column(row), (ROWS, ROWS))
    key = jnp.broadcast_to(row, (ROWS, ROWS))
    zero = jnp.zeros((ROWS, ROWS), F32)
    low = jnp.full((ROWS, ROWS), LOW, F32)
    clean_bias = jnp.concatenate([jnp.where(key <= query, zero, low), low], axis=1)
    noisy_bias = jnp.concatenate([jnp.where(key < query, zero, low), jnp.where(key == query, zero, low)], axis=1)
    bias = jnp.concatenate([clean_bias, noisy_bias], axis=0)
    keys = both(slice(0, HEAD))
    values = both(slice(HEAD, 2 * HEAD))
    for h in range(GROUP):
        scores = jnp.where(bias < -1.0, LOW, dot_t(q_ref[h], keys))
        top = jnp.max(scores, axis=1, keepdims=True)
        probs = jnp.exp2((scores - top) * POWER)
        top_ref[h] = jnp.broadcast_to(top, (2 * ROWS, HEAD))
        total_ref[h] = probs[:, :HEAD] + probs[:, HEAD:]
        accum_ref[h] = dot(probs.astype(BF16), values)


def far_kernel(*refs):
    q_ref = refs[0]
    k_refs, v_refs = refs[1:5], refs[5:9]
    top_in, total_in, accum_in = refs[9:12]
    code_ref, pair_ref, swap_ref, own_cut_ref, mkv_ref = refs[12:17]
    clean_ref, noisy_ref = refs[17:19]
    top_ref, total_ref, accum_ref = refs[19:]
    me = lax.axis_index("ctx")
    y, x, z = me // 8, lax.rem(me // 2, 4), lax.rem(me, 2)

    hop = jnp.where(z == 0, 1, 0)
    wrap = (z == 0) & (x == 0)
    old_y = jnp.where(wrap, 1, 0)
    step = jnp.where(z == 0, 0, 3)
    beyond = (z == 1) & (x == 3)
    new_y = jnp.where(beyond, 3, 0)
    k_old = jnp.where(wrap, k_refs[1][hop, 1], k_refs[0][hop, 1])
    v_old = jnp.where(z == 0, v_refs[1][old_y, 1], v_refs[0][old_y, 1])
    k_new = jnp.where(beyond, k_refs[3][step, 1], k_refs[0][step, 1])[:BLOCK]
    v_new = jnp.where(z == 0, v_refs[0][new_y, 1], v_refs[3][new_y, 1])[:BLOCK]

    own = code_ref[...].astype(F32)[:8]
    partner = pair_ref[ROWS:, :HEAD].astype(F32)
    other = swap_ref[...].astype(F32)
    old_code = jnp.where(z == 0, other, partner)
    new_code = jnp.where(z == 0, partner, other)
    old_ids, old_order = jnp.where(me > 0, old_code[:8], FAR), old_code[8:]
    new_ids, new_order = jnp.where(me < LAST, new_code[:8], FAR), new_code[8:]
    first_cut = own_cut_ref[0:1, :]
    last_cut = own_cut_ref[ROWS - 1 : ROWS, :]
    old_masked = column(jnp.where(old_order[0:1] >= first_cut, 1.0, 0.0))[ROWS - BLOCK :]
    new_masked = column(jnp.where(new_order[0:1] >= last_cut, 1.0, 0.0))[:BLOCK]

    def noisy(masked, clean, lanes):
        fixed = jnp.broadcast_to(mkv_ref[0:1, lanes].astype(F32), clean.shape)
        flag = jnp.broadcast_to(masked, clean.shape) > 0.5
        return jnp.where(flag, fixed, clean.astype(F32)).astype(BF16)

    def rim(old, new, lanes):
        parts = [old, new, noisy(old_masked, old[ROWS - BLOCK :], lanes), noisy(new_masked, new, lanes)]
        return jnp.concatenate(parts + [jnp.zeros((BLOCK, HEAD), BF16)], axis=0)

    k_rim = rim(k_old, k_new, slice(0, HEAD))
    v_rim = rim(v_old, v_new, slice(HEAD, 2 * HEAD))
    lane = lax.broadcasted_iota(jnp.int32, (8, ROWS), 1)
    mixed = jnp.where(
        lane < 32,
        new_ids,
        jnp.where(lane < 64, pltpu.roll(old_ids, 64, 1), jnp.where(lane < 96, pltpu.roll(new_ids, 64, 1), -5.0)),
    )
    square = (ROWS, ROWS)
    query = jnp.broadcast_to(column(own[0:1]), square)
    old_key = jnp.broadcast_to(old_ids[0:1], square)
    mixed_key = jnp.broadcast_to(mixed[0:1], square)
    early = lax.broadcasted_iota(jnp.int32, square, 1) < 32
    zero = jnp.zeros(square, F32)
    low = jnp.full(square, LOW, F32)
    clean_bias = [
        jnp.where(old_key <= query, zero, low),
        jnp.where(early, jnp.where(mixed_key <= query, zero, low), low),
    ]
    noisy_bias = [
        jnp.where(old_key < query, zero, low),
        jnp.where(early, jnp.where(mixed_key < query, zero, low), jnp.where(mixed_key == query, zero, low)),
    ]
    bias = jnp.concatenate([jnp.concatenate(clean_bias, axis=1), jnp.concatenate(noisy_bias, axis=1)], axis=0)

    def scores_of(step):
        dy, h = step
        if dy < 0:
            return jnp.where(bias < -1.0, LOW, dot_t(q_ref[h], k_rim))
        return dot_t(q_ref[h], k_refs[dy][...].reshape(8 * ROWS, HEAD))

    def absorb(step, scores):
        dy, h = step
        parts = [scores[:, j : j + ROWS] for j in range(0, scores.shape[1], ROWS)]
        if dy in (0, 1):
            for j in range(8):
                there = lax.rem(y + 4 - dy, 4) * 8 + lax.rem(x + 4 - j // 2, 4) * 2 + lax.rem(z + j, 2)
                parts[j] = jnp.where(there < me - 1, parts[j], LOW)
        best = parts[0]
        for part in parts[1:]:
            best = jnp.maximum(best, part)
        best = jnp.max(best, axis=1, keepdims=True)
        if dy > 1:
            best = jnp.where(y >= dy, best, LOW)
        old = top_in[h] if dy < 0 else top_ref[h]
        top = jnp.maximum(old, best)
        factor = jnp.exp2((old - top) * POWER)
        level = jnp.where(y >= dy, top, -LOW) if dy > 1 else top
        probs = [jnp.exp2((part - level) * POWER) for part in parts]
        total = (total_in[h] if dy < 0 else total_ref[h]) * factor
        for part in probs:
            total = total + part
        if dy < 0:
            values = v_rim
        else:
            values = jnp.concatenate([v_refs[dx][dy].reshape(2 * ROWS, HEAD) for dx in range(4)], axis=0)
        probs = jnp.concatenate([part.astype(BF16) for part in probs], axis=1)
        accum = (accum_in[h] if dy < 0 else accum_ref[h]) * factor + dot(probs, values)
        if dy < 3:
            top_ref[h] = top
            total_ref[h] = total
            accum_ref[h] = accum
            return
        lanes = slice(h * HEAD, (h + 1) * HEAD)
        result = (accum / jnp.sum(total, axis=1, keepdims=True)).astype(BF16)
        clean_ref[:, lanes] = result[:ROWS]
        noisy_ref[:, lanes] = result[ROWS:]

    steps = [(dy, h) for dy in (-1, 0, 1, 2, 3) for h in range(GROUP)]
    scores = scores_of(steps[0])
    for now, later in zip(steps, steps[1:] + [None]):
        following = None if later is None else scores_of(later)
        absorb(now, scores)
        scores = following


def shards(hidden, block_ids, decode_order, step_cut, mask_embed, q_weight, k_weight, v_weight):
    ids = block_ids.reshape(1, ROWS)
    order = decode_order.reshape(1, ROWS)
    cuts = step_cut.reshape(1, -1)
    moved = [lax.ppermute(hidden, "kv", kv_pairs(d, 0)) for d in (1, 2, 3)]
    own, wk, wv, code, pad = call(
        prep_kernel,
        [
            (hidden.shape, BF16),
            (k_weight.shape, BF16),
            (v_weight.shape, BF16),
            ((PAD, ROWS), BF16),
            ((PAD, 8 * WIDTH), BF16),
        ],
        [hidden, k_weight, v_weight, ids, order, mask_embed.reshape(1, -1)],
        (1 << 20, 4 << 20),
        [
            pltpu.VMEM(ids.shape, jnp.int32),
            pltpu.VMEM(ids.shape, jnp.int32),
            pltpu.VMEM((1, 8 * WIDTH), BF16),
            pltpu.SemaphoreType.DMA((6,)),
        ],
        pltpu.HBM,
    )
    pieces = []
    for piece in (own, *moved):
        piece, _ = lax.optimization_barrier((piece, pad))
        pieces += [piece, lax.ppermute(piece, "kv", kv_pairs(0, 1))]
    x, kv, mask_kv, send = call(
        kv_kernel,
        [
            ((ROWS + PAD, 8 * WIDTH), BF16),
            ((ROWS + PAD, 2 * HEAD), BF16),
            ((PAD, 2 * HEAD), BF16),
            ((PAD, ROWS), BF16),
        ],
        [*pieces, pad, wk, wv, code],
        (1 << 29, 3 << 20),
    )
    pair = lax.ppermute(kv, "ctx", ctx_pairs(0, 0, 1))
    swap = lax.ppermute(send, "ctx", [(i, (i + 2 * (i % 2) - 1) % 32) for i in range(32)])
    pair, swap = lax.optimization_barrier((pair, swap))
    k = jnp.stack([kv[:ROWS, :HEAD], pair[:ROWS, :HEAD]])
    v = jnp.stack([kv[:ROWS, HEAD:], pair[:ROWS, HEAD:]])
    k, v = lax.optimization_barrier((k, v))
    ks = [lax.ppermute(k, "ctx", ctx_pairs(0, d, 0)) for d in (1, 2, 3)]
    vs = [lax.ppermute(v, "ctx", ctx_pairs(d, 0, 0)) for d in (1, 2, 3)]
    moved = lax.optimization_barrier((*ks, *vs))
    ks = jnp.stack([k, *moved[:3]])
    vs = jnp.stack([v, *moved[3:]])
    ks, vs = lax.optimization_barrier((ks, vs))
    q, flag, own_cut = call(
        q_kernel,
        [((GROUP, 2 * ROWS, HEAD), BF16), ((ROWS, HEAD), F32), ((ROWS, HEAD), F32)],
        [x, q_weight, code, cuts],
        (1 << 30, 5 << 20),
    )
    near = call(
        near_kernel,
        [((GROUP, 2 * ROWS, HEAD), F32)] * 3,
        [q, kv, mask_kv, flag, code],
        (1 << 30, 2 << 20),
    )
    all_k = [ks] + [lax.ppermute(ks, "ctx", ctx_pairs(d, 0, 0)) for d in (1, 2, 3)]
    all_v = [vs] + [lax.ppermute(vs, "ctx", ctx_pairs(0, d, 0)) for d in (1, 2, 3)]
    return tuple(
        call(
            far_kernel,
            [((ROWS, GROUP * HEAD), BF16)] * 2,
            [q, *all_k, *all_v, *near, code, pair, swap, own_cut, mask_kv],
            (1 << 32, 4 << 20),
            [pltpu.VMEM((GROUP, 2 * ROWS, HEAD), F32)] * 3,
        )
    )


def solution(mesh):
    return jax.shard_map(
        shards,
        mesh=mesh,
        in_specs=(
            P("ctx", "kv"),
            P("ctx"),
            P("ctx"),
            P(),
            P(),
            P(None, "kv"),
            P(None, "kv"),
            P(None, "kv"),
        ),
        out_specs=(P("ctx", "kv"), P("ctx", "kv")),
        check_vma=False,
    )
```

```python
import math

import jax
import jax.numpy as jnp
from jax import lax
from jax.experimental import pallas as pl
from jax.experimental.pallas import tpu as pltpu
from jax.sharding import PartitionSpec as P

ROWS = 128
HEAD = 128
GROUP = 4
PAD = 16
WIDTH = 512
BLOCK = 32
LAST = 31
LOW = -1e30
FAR = 1e6
POWER = math.log2(math.e) / math.sqrt(HEAD)
LIMIT = 48 * 1024 * 1024
F32 = jnp.float32
BF16 = jnp.bfloat16


def ctx_pairs(dy, dx, dz):
    pairs = []
    for i in range(32):
        y, x, z = i // 8, (i // 2) % 4, i % 2
        pairs.append((i, (((y + dy) % 4) * 4 + (x + dx) % 4) * 2 + (z + dz) % 2))
    return pairs


def kv_pairs(dz, dc):
    pairs = []
    for i in range(8):
        z, c = i // 2, i % 2
        pairs.append((i, ((z + dz) % 4) * 2 + (c + dc) % 2))
    return pairs


def dot(a, b):
    return jnp.dot(a, b, preferred_element_type=F32)


def dot_t(a, b):
    return lax.dot_general(a, b, (((1,), (1,)), ((), ())), preferred_element_type=F32)


def call(kernel, outs, args, cost, scratch=(), space=pltpu.VMEM):
    spec = pl.BlockSpec(memory_space=pltpu.VMEM)
    return pl.pallas_call(
        kernel,
        out_shape=[jax.ShapeDtypeStruct(s, t) for s, t in outs],
        in_specs=[pl.BlockSpec(memory_space=space)] * len(args),
        out_specs=[spec] * len(outs),
        scratch_shapes=list(scratch),
        compiler_params=pltpu.CompilerParams(vmem_limit_bytes=LIMIT),
        cost_estimate=pl.CostEstimate(flops=cost[0], bytes_accessed=cost[1], transcendentals=0),
    )(*args)


def column(row):
    square = (ROWS, ROWS)
    same = lax.broadcasted_iota(jnp.int32, square, 0) == lax.broadcasted_iota(jnp.int32, square, 1)
    return jnp.sum(jnp.where(same, jnp.broadcast_to(row, square), 0.0), axis=1, keepdims=True)


def prep_kernel(*refs):
    hidden_hbm, wk_hbm, wv_hbm, ids_hbm, order_hbm, embed_hbm = refs[:6]
    own_ref, wk_ref, wv_ref, code_ref, pad_ref = refs[6:11]
    ids_ref, order_ref, embed_ref, sems = refs[11:]
    pairs = (
        (ids_hbm, ids_ref),
        (order_hbm, order_ref),
        (embed_hbm, embed_ref),
        (hidden_hbm, own_ref),
        (wk_hbm, wk_ref),
        (wv_hbm, wv_ref),
    )
    copies = [pltpu.make_async_copy(a, b, sems.at[i]) for i, (a, b) in enumerate(pairs)]
    for copy in copies:
        copy.start()
    for copy in copies:
        copy.wait()
    ids = jnp.broadcast_to(ids_ref[...].astype(F32), (PAD, ROWS))
    order = jnp.broadcast_to(order_ref[...].astype(F32), (PAD, ROWS))
    row = lax.broadcasted_iota(jnp.int32, (PAD, ROWS), 0)
    code_ref[...] = jnp.where(lax.rem(row, 2) == 0, ids, order).astype(BF16)
    pad_ref[...] = jnp.broadcast_to(embed_ref[...], pad_ref.shape)


def kv_kernel(*refs):
    pieces = refs[:8]
    pad_ref, wk_ref, wv_ref, code_ref = refs[8:12]
    x_ref, kv_ref, mkv_ref = refs[12:]
    me = lax.axis_index("kv")
    for dz in range(4):
        for dc in range(2):
            source = lax.rem(me // 2 + 4 - dz, 4) * 2 + lax.rem(me + dc, 2)
            x_ref[:ROWS, pl.ds(pl.multiple_of(source * WIDTH, WIDTH), WIDTH)] = pieces[2 * dz + dc][...]
    x_ref[ROWS:, :] = pad_ref[...]
    x = x_ref[...]
    for part, w_ref in enumerate((wk_ref, wv_ref)):
        lanes = slice(part * HEAD, (part + 1) * HEAD)
        product = dot(x, w_ref[...]).astype(BF16)
        kv_ref[:ROWS, lanes] = product[:ROWS]
        kv_ref[ROWS:, lanes] = code_ref[...]
        mkv_ref[:, lanes] = product[ROWS:]


def pair_kernel(own_ref, other_ref, k_ref, v_ref):
    for i, ref in enumerate((own_ref, other_ref)):
        rows = slice(i * ROWS, (i + 1) * ROWS)
        k_ref[rows, :] = ref[:ROWS, :HEAD]
        v_ref[rows, :] = ref[:ROWS, HEAD:]
    row = lax.broadcasted_iota(jnp.int32, (PAD, HEAD), 0)
    first = ref_tail(own_ref, ROWS)
    code = jnp.where(lax.rem(row, 4) < 2, first, ref_tail(other_ref, ROWS))
    k_ref[2 * ROWS :, :] = code.astype(BF16)


def ref_tail(ref, start):
    return ref[start:, :HEAD].astype(F32)


def stack_kernel(*refs):
    ks, vs = refs[:4], refs[4:8]
    k_ref, v_ref = refs[8:]
    row = lax.broadcasted_iota(jnp.int32, (PAD, HEAD), 0)
    code = jnp.zeros((PAD, HEAD), F32)
    for i in range(4):
        rows = slice(i * 2 * ROWS, (i + 1) * 2 * ROWS)
        k_ref[rows, :] = ks[i][: 2 * ROWS, :]
        v_ref[rows, :] = vs[i][...]
        code = jnp.where(row // 4 == i, ref_tail(ks[i], 2 * ROWS), code)
    k_ref[8 * ROWS :, :] = code.astype(BF16)


def q_kernel(x_ref, wq_ref, code_ref, cut_ref, q_ref, flag_ref, own_cut_ref):
    code = code_ref[...].astype(F32)
    ids = column(code[0:1])
    order = column(code[1:2])
    blocks = cut_ref.shape[1]
    spots = lax.broadcasted_iota(jnp.int32, (ROWS, blocks), 1).astype(F32)
    cuts = jnp.broadcast_to(cut_ref[...].astype(F32), (ROWS, blocks))
    cut = jnp.sum(jnp.where(spots == ids, cuts, 0.0), axis=1, keepdims=True)
    flag = jnp.broadcast_to(jnp.where(order >= cut, 1.0, 0.0), (ROWS, HEAD))
    flag_ref[...] = flag
    own_cut_ref[...] = jnp.broadcast_to(cut, (ROWS, HEAD))
    x = x_ref[...]
    for h in range(GROUP):
        product = dot(x, wq_ref[:, h * HEAD : (h + 1) * HEAD])
        clean = product[:ROWS]
        fixed = jnp.broadcast_to(product[ROWS : ROWS + 1], (ROWS, HEAD))
        q_ref[h, :ROWS, :] = clean.astype(BF16)
        q_ref[h, ROWS:, :] = jnp.where(flag > 0.5, fixed, clean).astype(BF16)


def near_kernel(q_ref, kv_ref, mkv_ref, flag_ref, code_ref, top_ref, total_ref, accum_ref):
    masked = flag_ref[...] > 0.5

    def both(lanes):
        clean = kv_ref[:ROWS, lanes]
        fixed = jnp.broadcast_to(mkv_ref[0:1, lanes].astype(F32), (ROWS, HEAD))
        return jnp.concatenate([clean, jnp.where(masked, fixed, clean.astype(F32)).astype(BF16)], axis=0)

    row = code_ref[...].astype(F32)[0:1]
    query = jnp.broadcast_to(column(row), (ROWS, ROWS))
    key = jnp.broadcast_to(row, (ROWS, ROWS))
    zero = jnp.zeros((ROWS, ROWS), F32)
    low = jnp.full((ROWS, ROWS), LOW, F32)
    clean_bias = jnp.concatenate([jnp.where(key <= query, zero, low), low], axis=1)
    noisy_bias = jnp.concatenate([jnp.where(key < query, zero, low), jnp.where(key == query, zero, low)], axis=1)
    bias = jnp.concatenate([clean_bias, noisy_bias], axis=0)
    keys = both(slice(0, HEAD))
    values = both(slice(HEAD, 2 * HEAD))
    for h in range(GROUP):
        scores = jnp.where(bias < -1.0, LOW, dot_t(q_ref[h], keys))
        top = jnp.max(scores, axis=1, keepdims=True)
        probs = jnp.exp2((scores - top) * POWER)
        top_ref[h] = jnp.broadcast_to(top, (2 * ROWS, HEAD))
        total_ref[h] = probs[:, :HEAD] + probs[:, HEAD:]
        accum_ref[h] = dot(probs.astype(BF16), values)


def place():
    me = lax.axis_index("ctx")
    return me, me // 8, lax.rem(me // 2, 4), lax.rem(me, 2)


def pipeline(q_ref, pieces, state_in, state, finish):
    top_ref, total_ref, accum_ref = state

    def scores_of(step):
        h, chunk, _, _ = step
        keys, _, mask, _ = pieces[chunk]
        scores = dot_t(q_ref[h], keys())
        parts = [scores[:, j : j + ROWS] for j in range(0, scores.shape[1], ROWS)]
        return mask(parts) if mask is not None else parts

    def absorb(step, parts):
        h, chunk, first, last = step
        _, values, _, seen = pieces[chunk]
        best = parts[0]
        for part in parts[1:]:
            best = jnp.maximum(best, part)
        best = jnp.max(best, axis=1, keepdims=True)
        if seen is not None:
            best = jnp.where(seen, best, LOW)
        source = state_in if first else state
        old = source[0][h]
        top = jnp.maximum(old, best)
        factor = jnp.exp2((old - top) * POWER)
        level = top if seen is None else jnp.where(seen, top, -LOW)
        probs = [jnp.exp2((part - level) * POWER) for part in parts]
        total = source[1][h] * factor
        for part in probs:
            total = total + part
        probs = jnp.concatenate([part.astype(BF16) for part in probs], axis=1)
        accum = source[2][h] * factor + dot(probs, values())
        if last and finish is not None:
            finish(h, accum, total)
        else:
            top_ref[h] = top
            total_ref[h] = total
            accum_ref[h] = accum

    order = [(h, i, i == 0, i == len(pieces) - 1) for i in range(len(pieces)) for h in range(GROUP)]
    parts = scores_of(order[0])
    for now, later in zip(order, order[1:] + [None]):
        following = None if later is None else scores_of(later)
        absorb(now, parts)
        parts = following


def blocks_of(ref, which):
    return jnp.concatenate([ref[i * 2 * ROWS : (i + 1) * 2 * ROWS, :] for i in which], axis=0)


def shard_mask(where, spots):
    me, y, x, z = where

    def mask(parts):
        kept = []
        for j, part in enumerate(parts):
            dy, dx = spots[j // 2]
            there = lax.rem(y + 4 - dy, 4) * 8 + lax.rem(x + 4 - dx, 4) * 2 + lax.rem(z + j, 2)
            kept.append(jnp.where(there < me - 1, part, LOW))
        return kept

    return mask


def far_kernel(*refs):
    q_ref = refs[0]
    k_refs = dict(zip((0, 1, 3), refs[1:4]))
    v_refs = dict(zip((0, 1, 3), refs[4:7]))
    state_in = refs[7:10]
    code_ref, own_cut_ref, mkv_ref = refs[10:13]
    state = refs[13:16]
    me, y, x, z = place()

    wrap = (z == 0) & (x == 0)
    beyond = (z == 1) & (x == 3)

    def block(ref, index):
        return ref[index * ROWS : (index + 1) * ROWS, :]

    k_old = jnp.where(wrap, block(k_refs[1], 3), jnp.where(z == 0, block(k_refs[0], 3), block(k_refs[0], 1)))
    v_old = jnp.where(wrap, block(v_refs[1], 3), jnp.where(z == 0, block(v_refs[1], 1), block(v_refs[0], 1)))
    k_new = jnp.where(beyond, block(k_refs[3], 7), jnp.where(z == 1, block(k_refs[0], 7), block(k_refs[0], 1)))
    v_new = jnp.where(beyond, block(v_refs[3], 7), jnp.where(z == 1, block(v_refs[3], 1), block(v_refs[0], 1)))
    k_new, v_new = k_new[:BLOCK], v_new[:BLOCK]

    own = code_ref[...].astype(F32)[0:1]
    tails = {dy: ref_tail(k_refs[dy], 8 * ROWS) for dy in (0, 1, 3)}

    def line(i):
        old = jnp.where(wrap, tails[1][6 + i : 7 + i], jnp.where(z == 0, tails[0][6 + i : 7 + i], tails[0][2 + i : 3 + i]))
        new = jnp.where(beyond, tails[3][14 + i : 15 + i], jnp.where(z == 1, tails[0][14 + i : 15 + i], tails[0][2 + i : 3 + i]))
        return old, new

    old_ids, new_ids = line(0)
    old_order, new_order = line(1)
    old_ids = jnp.broadcast_to(jnp.where(me > 0, old_ids, FAR), (8, ROWS))
    new_ids = jnp.broadcast_to(jnp.where(me < LAST, new_ids, FAR), (8, ROWS))
    first_cut = own_cut_ref[0:1, :]
    last_cut = own_cut_ref[ROWS - 1 : ROWS, :]
    old_masked = column(jnp.where(old_order >= first_cut, 1.0, 0.0))[ROWS - BLOCK :]
    new_masked = column(jnp.where(new_order >= last_cut, 1.0, 0.0))[:BLOCK]

    def noisy(masked, clean, lanes):
        fixed = jnp.broadcast_to(mkv_ref[0:1, lanes].astype(F32), clean.shape)
        flag = jnp.broadcast_to(masked, clean.shape) > 0.5
        return jnp.where(flag, fixed, clean.astype(F32)).astype(BF16)

    def rim(old, new, lanes):
        parts = [old, new, noisy(old_masked, old[ROWS - BLOCK :], lanes), noisy(new_masked, new, lanes)]
        return jnp.concatenate(parts + [jnp.zeros((BLOCK, HEAD), BF16)], axis=0)

    k_rim = rim(k_old, k_new, slice(0, HEAD))
    v_rim = rim(v_old, v_new, slice(HEAD, 2 * HEAD))
    lane = lax.broadcasted_iota(jnp.int32, (8, ROWS), 1)
    mixed = jnp.where(
        lane < 32,
        new_ids,
        jnp.where(lane < 64, pltpu.roll(old_ids, 64, 1), jnp.where(lane < 96, pltpu.roll(new_ids, 64, 1), -5.0)),
    )
    square = (ROWS, ROWS)
    query = jnp.broadcast_to(column(own), square)
    old_key = jnp.broadcast_to(old_ids[0:1], square)
    mixed_key = jnp.broadcast_to(mixed[0:1], square)
    early = lax.broadcasted_iota(jnp.int32, square, 1) < 32
    zero = jnp.zeros(square, F32)
    low = jnp.full(square, LOW, F32)
    clean_bias = [
        jnp.where(old_key <= query, zero, low),
        jnp.where(early, jnp.where(mixed_key <= query, zero, low), low),
    ]
    noisy_bias = [
        jnp.where(old_key < query, zero, low),
        jnp.where(early, jnp.where(mixed_key < query, zero, low), jnp.where(mixed_key == query, zero, low)),
    ]
    bias = jnp.concatenate([jnp.concatenate(clean_bias, axis=1), jnp.concatenate(noisy_bias, axis=1)], axis=0)

    def rim_mask(parts):
        return [jnp.where(bias[:, j * ROWS : (j + 1) * ROWS] < -1.0, LOW, part) for j, part in enumerate(parts)]

    near = (0, 1, 3)
    pieces = [(lambda: k_rim, lambda: v_rim, rim_mask, None)]
    for dy in near:
        pieces.append(
            (
                lambda dy=dy: blocks_of(k_refs[dy], near),
                lambda dy=dy: jnp.concatenate([blocks_of(v_refs[dx], (dy,)) for dx in near], axis=0),
                shard_mask((me, y, x, z), [(dy, dx) for dx in near]) if dy < 3 else None,
                y >= dy if dy == 3 else None,
            )
        )
    pipeline(q_ref, pieces, state_in, state, None)


def last_kernel(*refs):
    q_ref, k_refs, v_refs = refs[0], refs[1:5], refs[5:9]
    state_in = refs[9:12]
    clean_ref, noisy_ref = refs[12:14]
    state = refs[14:]
    where = place()
    near = (0, 1, 3)
    pieces = [
        (
            lambda: blocks_of(k_refs[2], range(4)),
            lambda: jnp.concatenate([blocks_of(v_refs[dx], (2,)) for dx in range(4)], axis=0),
            None,
            where[1] >= 2,
        ),
        (
            lambda: jnp.concatenate([blocks_of(k_refs[dy], (2,)) for dy in near], axis=0),
            lambda: blocks_of(v_refs[2], near),
            shard_mask(where, [(dy, 2) for dy in near]),
            None,
        ),
    ]

    def finish(h, accum, total):
        lanes = slice(h * HEAD, (h + 1) * HEAD)
        result = (accum / jnp.sum(total, axis=1, keepdims=True)).astype(BF16)
        clean_ref[:, lanes] = result[:ROWS]
        noisy_ref[:, lanes] = result[ROWS:]

    pipeline(q_ref, pieces, state_in, state, finish)


def shards(hidden, block_ids, decode_order, step_cut, mask_embed, q_weight, k_weight, v_weight):
    ids = block_ids.reshape(1, ROWS)
    order = decode_order.reshape(1, ROWS)
    cuts = step_cut.reshape(1, -1)
    moved = [lax.ppermute(hidden, "kv", kv_pairs(d, 0)) for d in (1, 2, 3)]
    own, wk, wv, code, pad = call(
        prep_kernel,
        [
            (hidden.shape, BF16),
            (k_weight.shape, BF16),
            (v_weight.shape, BF16),
            ((PAD, ROWS), BF16),
            ((PAD, 8 * WIDTH), BF16),
        ],
        [hidden, k_weight, v_weight, ids, order, mask_embed.reshape(1, -1)],
        (1 << 20, 4 << 20),
        [
            pltpu.VMEM(ids.shape, jnp.int32),
            pltpu.VMEM(ids.shape, jnp.int32),
            pltpu.VMEM((1, 8 * WIDTH), BF16),
            pltpu.SemaphoreType.DMA((6,)),
        ],
        pltpu.HBM,
    )
    pieces = []
    for piece in (own, *moved):
        piece, _ = lax.optimization_barrier((piece, pad))
        pieces += [piece, lax.ppermute(piece, "kv", kv_pairs(0, 1))]
    x, kv, mask_kv = call(
        kv_kernel,
        [
            ((ROWS + PAD, 8 * WIDTH), BF16),
            ((ROWS + PAD, 2 * HEAD), BF16),
            ((PAD, 2 * HEAD), BF16),
        ],
        [*pieces, pad, wk, wv, code],
        (1 << 29, 3 << 20),
    )
    pair = lax.ppermute(kv, "ctx", ctx_pairs(0, 0, 1))
    k, v = call(
        pair_kernel,
        [((2 * ROWS + PAD, HEAD), BF16), ((2 * ROWS, HEAD), BF16)],
        [kv, pair],
        (1 << 10, 1 << 18),
    )
    ks = [lax.ppermute(k, "ctx", ctx_pairs(0, d, 0)) for d in (1, 2, 3)]
    vs = [lax.ppermute(v, "ctx", ctx_pairs(d, 0, 0)) for d in (1, 2, 3)]
    ks, vs = call(
        stack_kernel,
        [((8 * ROWS + PAD, HEAD), BF16), ((8 * ROWS, HEAD), BF16)],
        [k, *ks, v, *vs],
        (1 << 10, 1 << 20),
    )
    q, flag, own_cut = call(
        q_kernel,
        [((GROUP, 2 * ROWS, HEAD), BF16), ((ROWS, HEAD), F32), ((ROWS, HEAD), F32)],
        [x, q_weight, code, cuts],
        (1 << 30, 5 << 20),
    )
    near = call(
        near_kernel,
        [((GROUP, 2 * ROWS, HEAD), F32)] * 3,
        [q, kv, mask_kv, flag, code],
        (1 << 30, 2 << 20),
    )
    all_k = [ks] + [lax.ppermute(ks, "ctx", ctx_pairs(d, 0, 0)) for d in (1, 2, 3)]
    all_v = [vs] + [lax.ppermute(vs, "ctx", ctx_pairs(0, d, 0)) for d in (1, 2, 3)]
    state = [((GROUP, 2 * ROWS, HEAD), F32)] * 3
    far = call(
        far_kernel,
        state,
        [q, *[all_k[d] for d in (0, 1, 3)], *[all_v[d] for d in (0, 1, 3)], *near, code, own_cut, mask_kv],
        (1 << 31, 4 << 20),
    )
    return tuple(
        call(
            last_kernel,
            [((ROWS, GROUP * HEAD), BF16)] * 2,
            [q, *all_k, *all_v, *far],
            (1 << 31, 4 << 20),
            [pltpu.VMEM((GROUP, 2 * ROWS, HEAD), F32)] * 3,
        )
    )


def solution(mesh):
    return jax.shard_map(
        shards,
        mesh=mesh,
        in_specs=(
            P("ctx", "kv"),
            P("ctx"),
            P("ctx"),
            P(),
            P(),
            P(None, "kv"),
            P(None, "kv"),
            P(None, "kv"),
        ),
        out_specs=(P("ctx", "kv"), P("ctx", "kv")),
        check_vma=False,
    )
```

```python
import math

import jax
import jax.numpy as jnp
from jax import lax
from jax.experimental import pallas as pl
from jax.experimental.pallas import tpu as pltpu
from jax.sharding import PartitionSpec as P

ROWS = 128
HEAD = 128
GROUP = 4
PAD = 16
WIDTH = 512
BLOCK = 32
LAST = 31
LOW = -1e30
FAR = 1e6
POWER = math.log2(math.e) / math.sqrt(HEAD)
LIMIT = 48 * 1024 * 1024
F32 = jnp.float32
BF16 = jnp.bfloat16


def ctx_pairs(dy, dx, dz):
    pairs = []
    for i in range(32):
        y, x, z = i // 8, (i // 2) % 4, i % 2
        pairs.append((i, (((y + dy) % 4) * 4 + (x + dx) % 4) * 2 + (z + dz) % 2))
    return pairs


def kv_pairs(dz, dc):
    pairs = []
    for i in range(8):
        z, c = i // 2, i % 2
        pairs.append((i, ((z + dz) % 4) * 2 + (c + dc) % 2))
    return pairs


def dot(a, b):
    return jnp.dot(a, b, preferred_element_type=F32)


def dot_t(a, b):
    return lax.dot_general(a, b, (((1,), (1,)), ((), ())), preferred_element_type=F32)


def call(kernel, outs, args, cost, scratch=(), space=pltpu.VMEM):
    spec = pl.BlockSpec(memory_space=pltpu.VMEM)
    return pl.pallas_call(
        kernel,
        out_shape=[jax.ShapeDtypeStruct(s, t) for s, t in outs],
        in_specs=[pl.BlockSpec(memory_space=space)] * len(args),
        out_specs=[spec] * len(outs),
        scratch_shapes=list(scratch),
        compiler_params=pltpu.CompilerParams(vmem_limit_bytes=LIMIT),
        cost_estimate=pl.CostEstimate(flops=cost[0], bytes_accessed=cost[1], transcendentals=0),
    )(*args)


def held(array):
    return pltpu.with_memory_space_constraint(array, pltpu.HBM)


def column(row):
    square = (ROWS, ROWS)
    same = lax.broadcasted_iota(jnp.int32, square, 0) == lax.broadcasted_iota(jnp.int32, square, 1)
    return jnp.sum(jnp.where(same, jnp.broadcast_to(row, square), 0.0), axis=1, keepdims=True)


def prep_kernel(*refs):
    hidden_hbm, wk_hbm, wv_hbm, ids_hbm, order_hbm, embed_hbm = refs[:6]
    own_ref, wk_ref, wv_ref, code_ref, pad_ref = refs[6:11]
    ids_ref, order_ref, embed_ref, sems = refs[11:]
    pairs = (
        (ids_hbm, ids_ref),
        (order_hbm, order_ref),
        (embed_hbm, embed_ref),
        (hidden_hbm, own_ref),
        (wk_hbm, wk_ref),
        (wv_hbm, wv_ref),
    )
    copies = [pltpu.make_async_copy(a, b, sems.at[i]) for i, (a, b) in enumerate(pairs)]
    for copy in copies:
        copy.start()
    for copy in copies:
        copy.wait()
    ids = jnp.broadcast_to(ids_ref[...].astype(F32), (PAD, ROWS))
    order = jnp.broadcast_to(order_ref[...].astype(F32), (PAD, ROWS))
    row = lax.broadcasted_iota(jnp.int32, (PAD, ROWS), 0)
    code_ref[...] = jnp.where(lax.rem(row, 2) == 0, ids, order).astype(BF16)
    pad_ref[...] = jnp.broadcast_to(embed_ref[...], pad_ref.shape)


def low_kernel(source_ref, out_ref):
    out_ref[...] = source_ref[: out_ref.shape[0], :]


def high_kernel(source_ref, out_ref):
    rows = out_ref.shape[0]
    out_ref[...] = source_ref[rows : 2 * rows, :]


def half(kernel, array, rows):
    (out,) = call(kernel, [((rows, array.shape[1]), BF16)], [array], (1 << 10, 1 << 16))
    return out


def kv_kernel(*refs):
    pieces = refs[:10]
    pad_ref, wk_ref, wv_ref, code_ref = refs[10:14]
    x_ref, kv_ref, mkv_ref = refs[14:]
    me = lax.axis_index("kv")
    spots = ((0, 0, ROWS), (1, 0, ROWS), (3, 0, ROWS), (2, 0, ROWS // 2), (2, ROWS // 2, ROWS // 2))
    for i, (dz, start, count) in enumerate(spots):
        for dc in range(2):
            source = lax.rem(me // 2 + 4 - dz, 4) * 2 + lax.rem(me + dc, 2)
            lanes = pl.ds(pl.multiple_of(source * WIDTH, WIDTH), WIDTH)
            x_ref[start : start + count, lanes] = pieces[2 * i + dc][...]
    x_ref[ROWS:, :] = pad_ref[...]
    x = x_ref[...]
    for part, w_ref in enumerate((wk_ref, wv_ref)):
        lanes = slice(part * HEAD, (part + 1) * HEAD)
        product = dot(x, w_ref[...]).astype(BF16)
        kv_ref[:ROWS, lanes] = product[:ROWS]
        kv_ref[ROWS:, lanes] = code_ref[...]
        mkv_ref[:, lanes] = product[ROWS:]


def pair_kernel(own_ref, other_ref, k_ref, v_ref):
    for i, ref in enumerate((own_ref, other_ref)):
        rows = slice(i * ROWS, (i + 1) * ROWS)
        k_ref[rows, :] = ref[:ROWS, :HEAD]
        v_ref[rows, :] = ref[:ROWS, HEAD:]
    row = lax.broadcasted_iota(jnp.int32, (PAD, HEAD), 0)
    first = ref_tail(own_ref, ROWS)
    code = jnp.where(lax.rem(row, 4) < 2, first, ref_tail(other_ref, ROWS))
    k_ref[2 * ROWS :, :] = code.astype(BF16)


def ref_tail(ref, start):
    return ref[start:, :HEAD].astype(F32)


def stack_kernel(*refs):
    ks, vs = refs[:4], refs[4:8]
    k_ref, v_ref = refs[8:]
    row = lax.broadcasted_iota(jnp.int32, (PAD, HEAD), 0)
    code = jnp.zeros((PAD, HEAD), F32)
    for i in range(4):
        rows = slice(i * 2 * ROWS, (i + 1) * 2 * ROWS)
        k_ref[rows, :] = ks[i][: 2 * ROWS, :]
        v_ref[rows, :] = vs[i][...]
        code = jnp.where(row // 4 == i, ref_tail(ks[i], 2 * ROWS), code)
    k_ref[8 * ROWS :, :] = code.astype(BF16)


def q_kernel(x_ref, wq_ref, code_ref, cut_ref, q_ref, flag_ref, own_cut_ref):
    code = code_ref[...].astype(F32)
    ids = column(code[0:1])
    order = column(code[1:2])
    blocks = cut_ref.shape[1]
    spots = lax.broadcasted_iota(jnp.int32, (ROWS, blocks), 1).astype(F32)
    cuts = jnp.broadcast_to(cut_ref[...].astype(F32), (ROWS, blocks))
    cut = jnp.sum(jnp.where(spots == ids, cuts, 0.0), axis=1, keepdims=True)
    flag = jnp.broadcast_to(jnp.where(order >= cut, 1.0, 0.0), (ROWS, HEAD))
    flag_ref[...] = flag
    own_cut_ref[...] = jnp.broadcast_to(cut, (ROWS, HEAD))
    x = x_ref[...]
    for h in range(GROUP):
        product = dot(x, wq_ref[:, h * HEAD : (h + 1) * HEAD])
        clean = product[:ROWS]
        fixed = jnp.broadcast_to(product[ROWS : ROWS + 1], (ROWS, HEAD))
        q_ref[h, :ROWS, :] = clean.astype(BF16)
        q_ref[h, ROWS:, :] = jnp.where(flag > 0.5, fixed, clean).astype(BF16)


def near_kernel(q_ref, kv_ref, mkv_ref, flag_ref, code_ref, top_ref, total_ref, accum_ref):
    masked = flag_ref[...] > 0.5

    def both(lanes):
        clean = kv_ref[:ROWS, lanes]
        fixed = jnp.broadcast_to(mkv_ref[0:1, lanes].astype(F32), (ROWS, HEAD))
        return jnp.concatenate([clean, jnp.where(masked, fixed, clean.astype(F32)).astype(BF16)], axis=0)

    row = code_ref[...].astype(F32)[0:1]
    query = jnp.broadcast_to(column(row), (ROWS, ROWS))
    key = jnp.broadcast_to(row, (ROWS, ROWS))
    zero = jnp.zeros((ROWS, ROWS), F32)
    low = jnp.full((ROWS, ROWS), LOW, F32)
    clean_bias = jnp.concatenate([jnp.where(key <= query, zero, low), low], axis=1)
    noisy_bias = jnp.concatenate([jnp.where(key < query, zero, low), jnp.where(key == query, zero, low)], axis=1)
    bias = jnp.concatenate([clean_bias, noisy_bias], axis=0)
    keys = both(slice(0, HEAD))
    values = both(slice(HEAD, 2 * HEAD))
    for h in range(GROUP):
        scores = jnp.where(bias < -1.0, LOW, dot_t(q_ref[h], keys))
        top = jnp.max(scores, axis=1, keepdims=True)
        probs = jnp.exp2((scores - top) * POWER)
        top_ref[h] = jnp.broadcast_to(top, (2 * ROWS, HEAD))
        total_ref[h] = probs[:, :HEAD] + probs[:, HEAD:]
        accum_ref[h] = dot(probs.astype(BF16), values)


def place():
    me = lax.axis_index("ctx")
    return me, me // 8, lax.rem(me // 2, 4), lax.rem(me, 2)


def pipeline(q_ref, pieces, state_in, state, finish):
    top_ref, total_ref, accum_ref = state

    def scores_of(step):
        h, chunk, _, _ = step
        keys, _, mask, _ = pieces[chunk]
        scores = dot_t(q_ref[h], keys())
        parts = [scores[:, j : j + ROWS] for j in range(0, scores.shape[1], ROWS)]
        return mask(parts) if mask is not None else parts

    def absorb(step, parts):
        h, chunk, first, last = step
        _, values, _, seen = pieces[chunk]
        best = parts[0]
        for part in parts[1:]:
            best = jnp.maximum(best, part)
        best = jnp.max(best, axis=1, keepdims=True)
        if seen is not None:
            best = jnp.where(seen, best, LOW)
        source = state_in if first else state
        old = source[0][h]
        top = jnp.maximum(old, best)
        factor = jnp.exp2((old - top) * POWER)
        level = top if seen is None else jnp.where(seen, top, -LOW)
        probs = [jnp.exp2((part - level) * POWER) for part in parts]
        total = source[1][h] * factor
        for part in probs:
            total = total + part
        probs = jnp.concatenate([part.astype(BF16) for part in probs], axis=1)
        accum = source[2][h] * factor + dot(probs, values())
        if last and finish is not None:
            finish(h, accum, total)
        else:
            top_ref[h] = top
            total_ref[h] = total
            accum_ref[h] = accum

    order = [(h, i, i == 0, i == len(pieces) - 1) for i in range(len(pieces)) for h in range(GROUP)]
    parts = scores_of(order[0])
    for now, later in zip(order, order[1:] + [None]):
        following = None if later is None else scores_of(later)
        absorb(now, parts)
        parts = following


def blocks_of(ref, which):
    return jnp.concatenate([ref[i * 2 * ROWS : (i + 1) * 2 * ROWS, :] for i in which], axis=0)


def shard_mask(where, spots):
    me, y, x, z = where

    def mask(parts):
        kept = []
        for j, part in enumerate(parts):
            dy, dx = spots[j // 2]
            there = lax.rem(y + 4 - dy, 4) * 8 + lax.rem(x + 4 - dx, 4) * 2 + lax.rem(z + j, 2)
            kept.append(jnp.where(there < me - 1, part, LOW))
        return kept

    return mask


def far_kernel(*refs):
    q_ref = refs[0]
    k_refs = dict(zip((0, 1, 3), refs[1:4]))
    v_refs = dict(zip((0, 1, 3), refs[4:7]))
    state_in = refs[7:10]
    code_ref, own_cut_ref, mkv_ref = refs[10:13]
    state = refs[13:16]
    me, y, x, z = place()

    wrap = (z == 0) & (x == 0)
    beyond = (z == 1) & (x == 3)

    def block(ref, index):
        return ref[index * ROWS : (index + 1) * ROWS, :]

    k_old = jnp.where(wrap, block(k_refs[1], 3), jnp.where(z == 0, block(k_refs[0], 3), block(k_refs[0], 1)))
    v_old = jnp.where(wrap, block(v_refs[1], 3), jnp.where(z == 0, block(v_refs[1], 1), block(v_refs[0], 1)))
    k_new = jnp.where(beyond, block(k_refs[3], 7), jnp.where(z == 1, block(k_refs[0], 7), block(k_refs[0], 1)))
    v_new = jnp.where(beyond, block(v_refs[3], 7), jnp.where(z == 1, block(v_refs[3], 1), block(v_refs[0], 1)))
    k_new, v_new = k_new[:BLOCK], v_new[:BLOCK]

    own = code_ref[...].astype(F32)[0:1]
    tails = {dy: ref_tail(k_refs[dy], 8 * ROWS) for dy in (0, 1, 3)}

    def line(i):
        old = jnp.where(wrap, tails[1][6 + i : 7 + i], jnp.where(z == 0, tails[0][6 + i : 7 + i], tails[0][2 + i : 3 + i]))
        new = jnp.where(beyond, tails[3][14 + i : 15 + i], jnp.where(z == 1, tails[0][14 + i : 15 + i], tails[0][2 + i : 3 + i]))
        return old, new

    old_ids, new_ids = line(0)
    old_order, new_order = line(1)
    old_ids = jnp.broadcast_to(jnp.where(me > 0, old_ids, FAR), (8, ROWS))
    new_ids = jnp.broadcast_to(jnp.where(me < LAST, new_ids, FAR), (8, ROWS))
    first_cut = own_cut_ref[0:1, :]
    last_cut = own_cut_ref[ROWS - 1 : ROWS, :]
    old_masked = column(jnp.where(old_order >= first_cut, 1.0, 0.0))[ROWS - BLOCK :]
    new_masked = column(jnp.where(new_order >= last_cut, 1.0, 0.0))[:BLOCK]

    def noisy(masked, clean, lanes):
        fixed = jnp.broadcast_to(mkv_ref[0:1, lanes].astype(F32), clean.shape)
        flag = jnp.broadcast_to(masked, clean.shape) > 0.5
        return jnp.where(flag, fixed, clean.astype(F32)).astype(BF16)

    def rim(old, new, lanes):
        parts = [old, new, noisy(old_masked, old[ROWS - BLOCK :], lanes), noisy(new_masked, new, lanes)]
        return jnp.concatenate(parts + [jnp.zeros((BLOCK, HEAD), BF16)], axis=0)

    k_rim = rim(k_old, k_new, slice(0, HEAD))
    v_rim = rim(v_old, v_new, slice(HEAD, 2 * HEAD))
    lane = lax.broadcasted_iota(jnp.int32, (8, ROWS), 1)
    mixed = jnp.where(
        lane < 32,
        new_ids,
        jnp.where(lane < 64, pltpu.roll(old_ids, 64, 1), jnp.where(lane < 96, pltpu.roll(new_ids, 64, 1), -5.0)),
    )
    square = (ROWS, ROWS)
    query = jnp.broadcast_to(column(own), square)
    old_key = jnp.broadcast_to(old_ids[0:1], square)
    mixed_key = jnp.broadcast_to(mixed[0:1], square)
    early = lax.broadcasted_iota(jnp.int32, square, 1) < 32
    zero = jnp.zeros(square, F32)
    low = jnp.full(square, LOW, F32)
    clean_bias = [
        jnp.where(old_key <= query, zero, low),
        jnp.where(early, jnp.where(mixed_key <= query, zero, low), low),
    ]
    noisy_bias = [
        jnp.where(old_key < query, zero, low),
        jnp.where(early, jnp.where(mixed_key < query, zero, low), jnp.where(mixed_key == query, zero, low)),
    ]
    bias = jnp.concatenate([jnp.concatenate(clean_bias, axis=1), jnp.concatenate(noisy_bias, axis=1)], axis=0)

    def rim_mask(parts):
        return [jnp.where(bias[:, j * ROWS : (j + 1) * ROWS] < -1.0, LOW, part) for j, part in enumerate(parts)]

    near = (0, 1, 3)
    pieces = [(lambda: k_rim, lambda: v_rim, rim_mask, None)]
    for dy in near:
        pieces.append(
            (
                lambda dy=dy: blocks_of(k_refs[dy], near),
                lambda dy=dy: jnp.concatenate([blocks_of(v_refs[dx], (dy,)) for dx in near], axis=0),
                shard_mask((me, y, x, z), [(dy, dx) for dx in near]) if dy < 3 else None,
                y >= dy if dy == 3 else None,
            )
        )
    pipeline(q_ref, pieces, state_in, state, None)


def last_kernel(*refs):
    q_ref, k_refs, v_refs = refs[0], refs[1:5], refs[5:9]
    state_in = refs[9:12]
    clean_ref, noisy_ref = refs[12:14]
    state = refs[14:]
    where = place()
    near = (0, 1, 3)
    pieces = [
        (
            lambda: blocks_of(k_refs[2], range(4)),
            lambda: jnp.concatenate([blocks_of(v_refs[dx], (2,)) for dx in range(4)], axis=0),
            None,
            where[1] >= 2,
        ),
        (
            lambda: jnp.concatenate([blocks_of(k_refs[dy], (2,)) for dy in near], axis=0),
            lambda: blocks_of(v_refs[2], near),
            shard_mask(where, [(dy, 2) for dy in near]),
            None,
        ),
    ]

    def finish(h, accum, total):
        lanes = slice(h * HEAD, (h + 1) * HEAD)
        result = (accum / jnp.sum(total, axis=1, keepdims=True)).astype(BF16)
        clean_ref[:, lanes] = result[:ROWS]
        noisy_ref[:, lanes] = result[ROWS:]

    pipeline(q_ref, pieces, state_in, state, finish)


def shards(hidden, block_ids, decode_order, step_cut, mask_embed, q_weight, k_weight, v_weight):
    ids = block_ids.reshape(1, ROWS)
    order = decode_order.reshape(1, ROWS)
    cuts = step_cut.reshape(1, -1)
    moved = [lax.ppermute(hidden, "kv", kv_pairs(d, 0)) for d in (1, 3)]
    moved.append(lax.ppermute(half(low_kernel, moved[0], ROWS // 2), "kv", kv_pairs(1, 0)))
    moved.append(lax.ppermute(half(high_kernel, moved[1], ROWS // 2), "kv", kv_pairs(3, 0)))
    own, wk, wv, code, pad = call(
        prep_kernel,
        [
            (hidden.shape, BF16),
            (k_weight.shape, BF16),
            (v_weight.shape, BF16),
            ((PAD, ROWS), BF16),
            ((PAD, 8 * WIDTH), BF16),
        ],
        [held(a) for a in (hidden, k_weight, v_weight, ids, order, mask_embed.reshape(1, -1))],
        (1 << 20, 4 << 20),
        [
            pltpu.VMEM(ids.shape, jnp.int32),
            pltpu.VMEM(ids.shape, jnp.int32),
            pltpu.VMEM((1, 8 * WIDTH), BF16),
            pltpu.SemaphoreType.DMA((6,)),
        ],
        pl.ANY,
    )
    pieces = []
    for piece in (own, *moved):
        piece, _ = lax.optimization_barrier((piece, pad))
        pieces += [piece, lax.ppermute(piece, "kv", kv_pairs(0, 1))]
    x, kv, mask_kv = call(
        kv_kernel,
        [
            ((ROWS + PAD, 8 * WIDTH), BF16),
            ((ROWS + PAD, 2 * HEAD), BF16),
            ((PAD, 2 * HEAD), BF16),
        ],
        [*pieces, pad, wk, wv, code],
        (1 << 29, 3 << 20),
    )
    pair = lax.ppermute(kv, "ctx", ctx_pairs(0, 0, 1))
    k, v = call(
        pair_kernel,
        [((2 * ROWS + PAD, HEAD), BF16), ((2 * ROWS, HEAD), BF16)],
        [kv, pair],
        (1 << 10, 1 << 18),
    )
    ks = [lax.ppermute(k, "ctx", ctx_pairs(0, d, 0)) for d in (1, 2, 3)]
    vs = [lax.ppermute(v, "ctx", ctx_pairs(d, 0, 0)) for d in (1, 2, 3)]
    ks, vs = call(
        stack_kernel,
        [((8 * ROWS + PAD, HEAD), BF16), ((8 * ROWS, HEAD), BF16)],
        [k, *ks, v, *vs],
        (1 << 10, 1 << 20),
    )
    q, flag, own_cut = call(
        q_kernel,
        [((GROUP, 2 * ROWS, HEAD), BF16), ((ROWS, HEAD), F32), ((ROWS, HEAD), F32)],
        [x, q_weight, code, cuts],
        (1 << 30, 5 << 20),
    )
    near = call(
        near_kernel,
        [((GROUP, 2 * ROWS, HEAD), F32)] * 3,
        [q, kv, mask_kv, flag, code],
        (1 << 30, 2 << 20),
    )
    all_k = [ks] + [lax.ppermute(ks, "ctx", ctx_pairs(d, 0, 0)) for d in (1, 2, 3)]
    all_v = [vs] + [lax.ppermute(vs, "ctx", ctx_pairs(0, d, 0)) for d in (1, 2, 3)]
    state = [((GROUP, 2 * ROWS, HEAD), F32)] * 3
    far = call(
        far_kernel,
        state,
        [q, *[all_k[d] for d in (0, 1, 3)], *[all_v[d] for d in (0, 1, 3)], *near, code, own_cut, mask_kv],
        (1 << 31, 4 << 20),
    )
    return tuple(
        call(
            last_kernel,
            [((ROWS, GROUP * HEAD), BF16)] * 2,
            [q, *all_k, *all_v, *far],
            (1 << 31, 4 << 20),
            [pltpu.VMEM((GROUP, 2 * ROWS, HEAD), F32)] * 3,
        )
    )


def solution(mesh):
    return jax.shard_map(
        shards,
        mesh=mesh,
        in_specs=(
            P("ctx", "kv"),
            P("ctx"),
            P("ctx"),
            P(),
            P(),
            P(None, "kv"),
            P(None, "kv"),
            P(None, "kv"),
        ),
        out_specs=(P("ctx", "kv"), P("ctx", "kv")),
        check_vma=False,
    )
```

```python
import math

import jax
import jax.numpy as jnp
from jax import lax
from jax.experimental import pallas as pl
from jax.experimental.pallas import tpu as pltpu
from jax.sharding import PartitionSpec as P

ROWS = 128
HEAD = 128
GROUP = 4
PAD = 16
WIDTH = 512
BLOCK = 32
LAST = 31
LOW = -1e30
FAR = 1e6
POWER = math.log2(math.e) / math.sqrt(HEAD)
LIMIT = 48 * 1024 * 1024
F32 = jnp.float32
BF16 = jnp.bfloat16


def ctx_pairs(dy, dx, dz):
    pairs = []
    for i in range(32):
        y, x, z = i // 8, (i // 2) % 4, i % 2
        pairs.append((i, (((y + dy) % 4) * 4 + (x + dx) % 4) * 2 + (z + dz) % 2))
    return pairs


def kv_pairs(dz, dc):
    pairs = []
    for i in range(8):
        z, c = i // 2, i % 2
        pairs.append((i, ((z + dz) % 4) * 2 + (c + dc) % 2))
    return pairs


def dot(a, b):
    return jnp.dot(a, b, preferred_element_type=F32)


def dot_t(a, b):
    return lax.dot_general(a, b, (((1,), (1,)), ((), ())), preferred_element_type=F32)


def call(kernel, outs, args, cost, scratch=(), space=pltpu.VMEM):
    spec = pl.BlockSpec(memory_space=pltpu.VMEM)
    return pl.pallas_call(
        kernel,
        out_shape=[jax.ShapeDtypeStruct(s, t) for s, t in outs],
        in_specs=[pl.BlockSpec(memory_space=space)] * len(args),
        out_specs=[spec] * len(outs),
        scratch_shapes=list(scratch),
        compiler_params=pltpu.CompilerParams(vmem_limit_bytes=LIMIT),
        cost_estimate=pl.CostEstimate(flops=cost[0], bytes_accessed=cost[1], transcendentals=0),
    )(*args)


def held(array):
    return pltpu.with_memory_space_constraint(array, pltpu.HBM)


def column(row):
    square = (ROWS, ROWS)
    same = lax.broadcasted_iota(jnp.int32, square, 0) == lax.broadcasted_iota(jnp.int32, square, 1)
    return jnp.sum(jnp.where(same, jnp.broadcast_to(row, square), 0.0), axis=1, keepdims=True)


def prep_kernel(*refs):
    hidden_hbm, wk_hbm, wv_hbm, ids_hbm, order_hbm, embed_hbm = refs[:6]
    own_ref, wk_ref, wv_ref, code_ref, pad_ref = refs[6:11]
    ids_ref, order_ref, embed_ref, sems = refs[11:]
    pairs = (
        (ids_hbm, ids_ref),
        (order_hbm, order_ref),
        (embed_hbm, embed_ref),
        (hidden_hbm, own_ref),
        (wk_hbm, wk_ref),
        (wv_hbm, wv_ref),
    )
    copies = [pltpu.make_async_copy(a, b, sems.at[i]) for i, (a, b) in enumerate(pairs)]
    for copy in copies:
        copy.start()
    for copy in copies:
        copy.wait()
    ids = jnp.broadcast_to(ids_ref[...].astype(F32), (PAD, ROWS))
    order = jnp.broadcast_to(order_ref[...].astype(F32), (PAD, ROWS))
    row = lax.broadcasted_iota(jnp.int32, (PAD, ROWS), 0)
    code_ref[...] = jnp.where(lax.rem(row, 2) == 0, ids, order).astype(BF16)
    pad_ref[...] = jnp.broadcast_to(embed_ref[...], pad_ref.shape)


def low_kernel(source_ref, out_ref):
    out_ref[...] = source_ref[: out_ref.shape[0], :]


def high_kernel(source_ref, out_ref):
    rows = out_ref.shape[0]
    out_ref[...] = source_ref[rows : 2 * rows, :]


def half(kernel, array):
    (out,) = call(kernel, [((ROWS // 2, WIDTH), BF16)], [array], (1 << 10, 1 << 16))
    return out


def join_kernel(*refs):
    out_ref = refs[-1]
    rows = refs[0].shape[0]
    for i, ref in enumerate(refs[:-1]):
        out_ref[i * rows : (i + 1) * rows, :] = ref[...]


def join(*arrays):
    rows = sum(a.shape[0] for a in arrays)
    (out,) = call(join_kernel, [((rows, WIDTH), BF16)], arrays, (1 << 10, 1 << 19))
    return out


def kv_kernel(*refs):
    early, early_other, late, late_other, pad_ref, wk_ref, wv_ref, code_ref = refs[:8]
    x_ref, kv_ref, mkv_ref = refs[8:]
    me = lax.axis_index("kv")
    for dc, (first, second) in enumerate(((early, late), (early_other, late_other))):
        for dz in range(4):
            source = lax.rem(me // 2 + 4 - dz, 4) * 2 + lax.rem(me + dc, 2)
            lanes = pl.ds(pl.multiple_of(source * WIDTH, WIDTH), WIDTH)
            i = (0, 1, None, 2)[dz]
            x_ref[:ROWS, lanes] = second[...] if i is None else first[i * ROWS : (i + 1) * ROWS, :]
    x_ref[ROWS:, :] = pad_ref[...]
    x = x_ref[...]
    for part, w_ref in enumerate((wk_ref, wv_ref)):
        lanes = slice(part * HEAD, (part + 1) * HEAD)
        product = dot(x, w_ref[...]).astype(BF16)
        kv_ref[:ROWS, lanes] = product[:ROWS]
        kv_ref[ROWS:, lanes] = code_ref[...]
        mkv_ref[:, lanes] = product[ROWS:]


def pair_kernel(own_ref, other_ref, k_ref, v_ref):
    for i, ref in enumerate((own_ref, other_ref)):
        rows = slice(i * ROWS, (i + 1) * ROWS)
        k_ref[rows, :] = ref[:ROWS, :HEAD]
        v_ref[rows, :] = ref[:ROWS, HEAD:]
    row = lax.broadcasted_iota(jnp.int32, (PAD, HEAD), 0)
    first = ref_tail(own_ref, ROWS)
    code = jnp.where(lax.rem(row, 4) < 2, first, ref_tail(other_ref, ROWS))
    k_ref[2 * ROWS :, :] = code.astype(BF16)


def ref_tail(ref, start):
    return ref[start:, :HEAD].astype(F32)


def stack_kernel(*refs):
    ks, vs = refs[:4], refs[4:8]
    k_ref, v_ref = refs[8:]
    row = lax.broadcasted_iota(jnp.int32, (PAD, HEAD), 0)
    code = jnp.zeros((PAD, HEAD), F32)
    for i in range(4):
        rows = slice(i * 2 * ROWS, (i + 1) * 2 * ROWS)
        k_ref[rows, :] = ks[i][: 2 * ROWS, :]
        v_ref[rows, :] = vs[i][...]
        code = jnp.where(row // 4 == i, ref_tail(ks[i], 2 * ROWS), code)
    k_ref[8 * ROWS :, :] = code.astype(BF16)


def q_kernel(x_ref, wq_ref, code_ref, cut_ref, q_ref, flag_ref, own_cut_ref):
    code = code_ref[...].astype(F32)
    ids = column(code[0:1])
    order = column(code[1:2])
    blocks = cut_ref.shape[1]
    spots = lax.broadcasted_iota(jnp.int32, (ROWS, blocks), 1).astype(F32)
    cuts = jnp.broadcast_to(cut_ref[...].astype(F32), (ROWS, blocks))
    cut = jnp.sum(jnp.where(spots == ids, cuts, 0.0), axis=1, keepdims=True)
    flag = jnp.broadcast_to(jnp.where(order >= cut, 1.0, 0.0), (ROWS, HEAD))
    flag_ref[...] = flag
    own_cut_ref[...] = jnp.broadcast_to(cut, (ROWS, HEAD))
    x = x_ref[...]
    for h in range(GROUP):
        product = dot(x, wq_ref[:, h * HEAD : (h + 1) * HEAD])
        clean = product[:ROWS]
        fixed = jnp.broadcast_to(product[ROWS : ROWS + 1], (ROWS, HEAD))
        q_ref[h, :ROWS, :] = clean.astype(BF16)
        q_ref[h, ROWS:, :] = jnp.where(flag > 0.5, fixed, clean).astype(BF16)


def near_kernel(q_ref, kv_ref, mkv_ref, flag_ref, code_ref, top_ref, total_ref, accum_ref):
    masked = flag_ref[...] > 0.5

    def both(lanes):
        clean = kv_ref[:ROWS, lanes]
        fixed = jnp.broadcast_to(mkv_ref[0:1, lanes].astype(F32), (ROWS, HEAD))
        return jnp.concatenate([clean, jnp.where(masked, fixed, clean.astype(F32)).astype(BF16)], axis=0)

    row = code_ref[...].astype(F32)[0:1]
    query = jnp.broadcast_to(column(row), (ROWS, ROWS))
    key = jnp.broadcast_to(row, (ROWS, ROWS))
    zero = jnp.zeros((ROWS, ROWS), F32)
    low = jnp.full((ROWS, ROWS), LOW, F32)
    clean_bias = jnp.concatenate([jnp.where(key <= query, zero, low), low], axis=1)
    noisy_bias = jnp.concatenate([jnp.where(key < query, zero, low), jnp.where(key == query, zero, low)], axis=1)
    bias = jnp.concatenate([clean_bias, noisy_bias], axis=0)
    keys = both(slice(0, HEAD))
    values = both(slice(HEAD, 2 * HEAD))
    for h in range(GROUP):
        scores = jnp.where(bias < -1.0, LOW, dot_t(q_ref[h], keys))
        top = jnp.max(scores, axis=1, keepdims=True)
        probs = jnp.exp2((scores - top) * POWER)
        top_ref[h] = jnp.broadcast_to(top, (2 * ROWS, HEAD))
        total_ref[h] = probs[:, :HEAD] + probs[:, HEAD:]
        accum_ref[h] = dot(probs.astype(BF16), values)


def place():
    me = lax.axis_index("ctx")
    return me, me // 8, lax.rem(me // 2, 4), lax.rem(me, 2)


def pipeline(q_ref, pieces, state_in, state, finish):
    top_ref, total_ref, accum_ref = state

    def scores_of(step):
        h, chunk, _, _ = step
        keys, _, mask, _ = pieces[chunk]
        scores = dot_t(q_ref[h], keys())
        parts = [scores[:, j : j + ROWS] for j in range(0, scores.shape[1], ROWS)]
        return mask(parts) if mask is not None else parts

    def absorb(step, parts):
        h, chunk, first, last = step
        _, values, _, seen = pieces[chunk]
        best = parts[0]
        for part in parts[1:]:
            best = jnp.maximum(best, part)
        best = jnp.max(best, axis=1, keepdims=True)
        if seen is not None:
            best = jnp.where(seen, best, LOW)
        source = state_in if first else state
        old = source[0][h]
        top = jnp.maximum(old, best)
        factor = jnp.exp2((old - top) * POWER)
        level = top if seen is None else jnp.where(seen, top, -LOW)
        probs = [jnp.exp2((part - level) * POWER) for part in parts]
        total = source[1][h] * factor
        for part in probs:
            total = total + part
        probs = jnp.concatenate([part.astype(BF16) for part in probs], axis=1)
        accum = source[2][h] * factor + dot(probs, values())
        if last and finish is not None:
            finish(h, accum, total)
        else:
            top_ref[h] = top
            total_ref[h] = total
            accum_ref[h] = accum

    order = [(h, i, i == 0, i == len(pieces) - 1) for i in range(len(pieces)) for h in range(GROUP)]
    parts = scores_of(order[0])
    for now, later in zip(order, order[1:] + [None]):
        following = None if later is None else scores_of(later)
        absorb(now, parts)
        parts = following


def blocks_of(ref, which):
    return jnp.concatenate([ref[i * 2 * ROWS : (i + 1) * 2 * ROWS, :] for i in which], axis=0)


def shard_mask(where, spots):
    me, y, x, z = where

    def mask(parts):
        kept = []
        for j, part in enumerate(parts):
            dy, dx = spots[j // 2]
            there = lax.rem(y + 4 - dy, 4) * 8 + lax.rem(x + 4 - dx, 4) * 2 + lax.rem(z + j, 2)
            kept.append(jnp.where(there < me - 1, part, LOW))
        return kept

    return mask


def far_kernel(*refs):
    q_ref = refs[0]
    k_refs = dict(zip((0, 1, 3), refs[1:4]))
    v_refs = dict(zip((0, 1, 3), refs[4:7]))
    state_in = refs[7:10]
    code_ref, own_cut_ref, mkv_ref = refs[10:13]
    state = refs[13:16]
    me, y, x, z = place()

    wrap = (z == 0) & (x == 0)
    beyond = (z == 1) & (x == 3)

    def block(ref, index):
        return ref[index * ROWS : (index + 1) * ROWS, :]

    k_old = jnp.where(wrap, block(k_refs[1], 3), jnp.where(z == 0, block(k_refs[0], 3), block(k_refs[0], 1)))
    v_old = jnp.where(wrap, block(v_refs[1], 3), jnp.where(z == 0, block(v_refs[1], 1), block(v_refs[0], 1)))
    k_new = jnp.where(beyond, block(k_refs[3], 7), jnp.where(z == 1, block(k_refs[0], 7), block(k_refs[0], 1)))
    v_new = jnp.where(beyond, block(v_refs[3], 7), jnp.where(z == 1, block(v_refs[3], 1), block(v_refs[0], 1)))
    k_new, v_new = k_new[:BLOCK], v_new[:BLOCK]

    own = code_ref[...].astype(F32)[0:1]
    tails = {dy: ref_tail(k_refs[dy], 8 * ROWS) for dy in (0, 1, 3)}

    def line(i):
        old = jnp.where(wrap, tails[1][6 + i : 7 + i], jnp.where(z == 0, tails[0][6 + i : 7 + i], tails[0][2 + i : 3 + i]))
        new = jnp.where(beyond, tails[3][14 + i : 15 + i], jnp.where(z == 1, tails[0][14 + i : 15 + i], tails[0][2 + i : 3 + i]))
        return old, new

    old_ids, new_ids = line(0)
    old_order, new_order = line(1)
    old_ids = jnp.broadcast_to(jnp.where(me > 0, old_ids, FAR), (8, ROWS))
    new_ids = jnp.broadcast_to(jnp.where(me < LAST, new_ids, FAR), (8, ROWS))
    first_cut = own_cut_ref[0:1, :]
    last_cut = own_cut_ref[ROWS - 1 : ROWS, :]
    old_masked = column(jnp.where(old_order >= first_cut, 1.0, 0.0))[ROWS - BLOCK :]
    new_masked = column(jnp.where(new_order >= last_cut, 1.0, 0.0))[:BLOCK]

    def noisy(masked, clean, lanes):
        fixed = jnp.broadcast_to(mkv_ref[0:1, lanes].astype(F32), clean.shape)
        flag = jnp.broadcast_to(masked, clean.shape) > 0.5
        return jnp.where(flag, fixed, clean.astype(F32)).astype(BF16)

    def rim(old, new, lanes):
        parts = [old, new, noisy(old_masked, old[ROWS - BLOCK :], lanes), noisy(new_masked, new, lanes)]
        return jnp.concatenate(parts + [jnp.zeros((BLOCK, HEAD), BF16)], axis=0)

    k_rim = rim(k_old, k_new, slice(0, HEAD))
    v_rim = rim(v_old, v_new, slice(HEAD, 2 * HEAD))
    lane = lax.broadcasted_iota(jnp.int32, (8, ROWS), 1)
    mixed = jnp.where(
        lane < 32,
        new_ids,
        jnp.where(lane < 64, pltpu.roll(old_ids, 64, 1), jnp.where(lane < 96, pltpu.roll(new_ids, 64, 1), -5.0)),
    )
    square = (ROWS, ROWS)
    query = jnp.broadcast_to(column(own), square)
    old_key = jnp.broadcast_to(old_ids[0:1], square)
    mixed_key = jnp.broadcast_to(mixed[0:1], square)
    early = lax.broadcasted_iota(jnp.int32, square, 1) < 32
    zero = jnp.zeros(square, F32)
    low = jnp.full(square, LOW, F32)
    clean_bias = [
        jnp.where(old_key <= query, zero, low),
        jnp.where(early, jnp.where(mixed_key <= query, zero, low), low),
    ]
    noisy_bias = [
        jnp.where(old_key < query, zero, low),
        jnp.where(early, jnp.where(mixed_key < query, zero, low), jnp.where(mixed_key == query, zero, low)),
    ]
    bias = jnp.concatenate([jnp.concatenate(clean_bias, axis=1), jnp.concatenate(noisy_bias, axis=1)], axis=0)

    def rim_mask(parts):
        return [jnp.where(bias[:, j * ROWS : (j + 1) * ROWS] < -1.0, LOW, part) for j, part in enumerate(parts)]

    near = (0, 1, 3)
    pieces = [(lambda: k_rim, lambda: v_rim, rim_mask, None)]
    for dy in near:
        pieces.append(
            (
                lambda dy=dy: blocks_of(k_refs[dy], near),
                lambda dy=dy: jnp.concatenate([blocks_of(v_refs[dx], (dy,)) for dx in near], axis=0),
                shard_mask((me, y, x, z), [(dy, dx) for dx in near]) if dy < 3 else None,
                y >= dy if dy == 3 else None,
            )
        )
    pipeline(q_ref, pieces, state_in, state, None)


def last_kernel(*refs):
    q_ref, k_refs, v_refs = refs[0], refs[1:5], refs[5:9]
    state_in = refs[9:12]
    clean_ref, noisy_ref = refs[12:14]
    state = refs[14:]
    where = place()
    near = (0, 1, 3)
    pieces = [
        (
            lambda: blocks_of(k_refs[2], range(4)),
            lambda: jnp.concatenate([blocks_of(v_refs[dx], (2,)) for dx in range(4)], axis=0),
            None,
            where[1] >= 2,
        ),
        (
            lambda: jnp.concatenate([blocks_of(k_refs[dy], (2,)) for dy in near], axis=0),
            lambda: blocks_of(v_refs[2], near),
            shard_mask(where, [(dy, 2) for dy in near]),
            None,
        ),
    ]

    def finish(h, accum, total):
        lanes = slice(h * HEAD, (h + 1) * HEAD)
        result = (accum / jnp.sum(total, axis=1, keepdims=True)).astype(BF16)
        clean_ref[:, lanes] = result[:ROWS]
        noisy_ref[:, lanes] = result[ROWS:]

    pipeline(q_ref, pieces, state_in, state, finish)


def shards(hidden, block_ids, decode_order, step_cut, mask_embed, q_weight, k_weight, v_weight):
    ids = block_ids.reshape(1, ROWS)
    order = decode_order.reshape(1, ROWS)
    cuts = step_cut.reshape(1, -1)
    one, three = [lax.ppermute(hidden, "kv", kv_pairs(d, 0)) for d in (1, 3)]
    low = lax.ppermute(half(low_kernel, one), "kv", kv_pairs(1, 0))
    high = lax.ppermute(half(high_kernel, three), "kv", kv_pairs(3, 0))
    own, wk, wv, code, pad = call(
        prep_kernel,
        [
            (hidden.shape, BF16),
            (k_weight.shape, BF16),
            (v_weight.shape, BF16),
            ((PAD, ROWS), BF16),
            ((PAD, 8 * WIDTH), BF16),
        ],
        [held(a) for a in (hidden, k_weight, v_weight, ids, order, mask_embed.reshape(1, -1))],
        (1 << 20, 4 << 20),
        [
            pltpu.VMEM(ids.shape, jnp.int32),
            pltpu.VMEM(ids.shape, jnp.int32),
            pltpu.VMEM((1, 8 * WIDTH), BF16),
            pltpu.SemaphoreType.DMA((6,)),
        ],
        pl.ANY,
    )
    early = join(own, one, three)
    early_other = lax.ppermute(early, "kv", kv_pairs(0, 1))
    late = join(low, high)
    late_other = lax.ppermute(late, "kv", kv_pairs(0, 1))
    x, kv, mask_kv = call(
        kv_kernel,
        [
            ((ROWS + PAD, 8 * WIDTH), BF16),
            ((ROWS + PAD, 2 * HEAD), BF16),
            ((PAD, 2 * HEAD), BF16),
        ],
        [early, early_other, late, late_other, pad, wk, wv, code],
        (1 << 29, 3 << 20),
    )
    pair = lax.ppermute(kv, "ctx", ctx_pairs(0, 0, 1))
    k, v = call(
        pair_kernel,
        [((2 * ROWS + PAD, HEAD), BF16), ((2 * ROWS, HEAD), BF16)],
        [kv, pair],
        (1 << 10, 1 << 18),
    )
    ks = [lax.ppermute(k, "ctx", ctx_pairs(0, d, 0)) for d in (1, 2, 3)]
    vs = [lax.ppermute(v, "ctx", ctx_pairs(d, 0, 0)) for d in (1, 2, 3)]
    ks, vs = call(
        stack_kernel,
        [((8 * ROWS + PAD, HEAD), BF16), ((8 * ROWS, HEAD), BF16)],
        [k, *ks, v, *vs],
        (1 << 10, 1 << 20),
    )
    q, flag, own_cut = call(
        q_kernel,
        [((GROUP, 2 * ROWS, HEAD), BF16), ((ROWS, HEAD), F32), ((ROWS, HEAD), F32)],
        [x, q_weight, code, cuts],
        (1 << 30, 5 << 20),
    )
    near = call(
        near_kernel,
        [((GROUP, 2 * ROWS, HEAD), F32)] * 3,
        [q, kv, mask_kv, flag, code],
        (1 << 30, 2 << 20),
    )
    all_k = [ks] + [lax.ppermute(ks, "ctx", ctx_pairs(d, 0, 0)) for d in (1, 2, 3)]
    all_v = [vs] + [lax.ppermute(vs, "ctx", ctx_pairs(0, d, 0)) for d in (1, 2, 3)]
    state = [((GROUP, 2 * ROWS, HEAD), F32)] * 3
    far = call(
        far_kernel,
        state,
        [q, *[all_k[d] for d in (0, 1, 3)], *[all_v[d] for d in (0, 1, 3)], *near, code, own_cut, mask_kv],
        (1 << 31, 4 << 20),
    )
    return tuple(
        call(
            last_kernel,
            [((ROWS, GROUP * HEAD), BF16)] * 2,
            [q, *all_k, *all_v, *far],
            (1 << 31, 4 << 20),
            [pltpu.VMEM((GROUP, 2 * ROWS, HEAD), F32)] * 3,
        )
    )


def solution(mesh):
    return jax.shard_map(
        shards,
        mesh=mesh,
        in_specs=(
            P("ctx", "kv"),
            P("ctx"),
            P("ctx"),
            P(),
            P(),
            P(None, "kv"),
            P(None, "kv"),
            P(None, "kv"),
        ),
        out_specs=(P("ctx", "kv"), P("ctx", "kv")),
        check_vma=False,
    )
```

```python
import math

import jax
import jax.numpy as jnp
from jax import lax
from jax.experimental import pallas as pl
from jax.experimental.pallas import tpu as pltpu
from jax.sharding import PartitionSpec as P

ROWS = 128
HEAD = 128
GROUP = 4
PAD = 16
WIDTH = 512
BLOCK = 32
LAST = 31
LOW = -1e30
FAR = 1e6
POWER = math.log2(math.e) / math.sqrt(HEAD)
LIMIT = 48 * 1024 * 1024
F32 = jnp.float32
BF16 = jnp.bfloat16


def ctx_pairs(dy, dx, dz):
    pairs = []
    for i in range(32):
        y, x, z = i // 8, (i // 2) % 4, i % 2
        pairs.append((i, (((y + dy) % 4) * 4 + (x + dx) % 4) * 2 + (z + dz) % 2))
    return pairs


def kv_pairs(dz, dc):
    pairs = []
    for i in range(8):
        z, c = i // 2, i % 2
        pairs.append((i, ((z + dz) % 4) * 2 + (c + dc) % 2))
    return pairs


def dot(a, b):
    return jnp.dot(a, b, preferred_element_type=F32)


def dot_t(a, b):
    return lax.dot_general(a, b, (((1,), (1,)), ((), ())), preferred_element_type=F32)


def call(kernel, outs, args, cost, scratch=(), space=pltpu.VMEM):
    spec = pl.BlockSpec(memory_space=pltpu.VMEM)
    return pl.pallas_call(
        kernel,
        out_shape=[jax.ShapeDtypeStruct(s, t) for s, t in outs],
        in_specs=[pl.BlockSpec(memory_space=space)] * len(args),
        out_specs=[spec] * len(outs),
        scratch_shapes=list(scratch),
        compiler_params=pltpu.CompilerParams(vmem_limit_bytes=LIMIT),
        cost_estimate=pl.CostEstimate(flops=cost[0], bytes_accessed=cost[1], transcendentals=0),
    )(*args)


def held(array):
    return pltpu.with_memory_space_constraint(array, pltpu.HBM)


def column(row):
    square = (ROWS, ROWS)
    same = lax.broadcasted_iota(jnp.int32, square, 0) == lax.broadcasted_iota(jnp.int32, square, 1)
    return jnp.sum(jnp.where(same, jnp.broadcast_to(row, square), 0.0), axis=1, keepdims=True)


def prep_kernel(*refs):
    hidden_hbm, wk_hbm, wv_hbm, ids_hbm, order_hbm, embed_hbm = refs[:6]
    own_ref, wk_ref, wv_ref, code_ref, pad_ref = refs[6:11]
    ids_ref, order_ref, embed_ref, sems = refs[11:]
    pairs = (
        (ids_hbm, ids_ref),
        (order_hbm, order_ref),
        (embed_hbm, embed_ref),
        (hidden_hbm, own_ref),
        (wk_hbm, wk_ref),
        (wv_hbm, wv_ref),
    )
    copies = [pltpu.make_async_copy(a, b, sems.at[i]) for i, (a, b) in enumerate(pairs)]
    for copy in copies:
        copy.start()
    for copy in copies:
        copy.wait()
    ids = jnp.broadcast_to(ids_ref[...].astype(F32), (PAD, ROWS))
    order = jnp.broadcast_to(order_ref[...].astype(F32), (PAD, ROWS))
    row = lax.broadcasted_iota(jnp.int32, (PAD, ROWS), 0)
    code_ref[...] = jnp.where(lax.rem(row, 2) == 0, ids, order).astype(BF16)
    pad_ref[...] = jnp.broadcast_to(embed_ref[...], pad_ref.shape)


def join_kernel(*refs):
    out_ref = refs[-1]
    rows = refs[0].shape[0]
    for i, ref in enumerate(refs[:-1]):
        out_ref[i * rows : (i + 1) * rows, :] = ref[...]


def join(*arrays):
    rows = sum(a.shape[0] for a in arrays)
    (out,) = call(join_kernel, [((rows, WIDTH), BF16)], arrays, (1 << 10, 1 << 19))
    return out


def kv_kernel(*refs):
    mine, other, pad_ref, wk_ref, wv_ref, code_ref = refs[:6]
    x_ref, kv_ref, mkv_ref = refs[6:]
    me = lax.axis_index("kv")
    for dc, ref in enumerate((mine, other)):
        for dz in range(4):
            source = lax.rem(me // 2 + 4 - dz, 4) * 2 + lax.rem(me + dc, 2)
            lanes = pl.ds(pl.multiple_of(source * WIDTH, WIDTH), WIDTH)
            x_ref[:ROWS, lanes] = ref[dz * ROWS : (dz + 1) * ROWS, :]
    x_ref[ROWS:, :] = pad_ref[...]
    x = x_ref[...]
    for part, w_ref in enumerate((wk_ref, wv_ref)):
        lanes = slice(part * HEAD, (part + 1) * HEAD)
        product = dot(x, w_ref[...]).astype(BF16)
        kv_ref[:ROWS, lanes] = product[:ROWS]
        kv_ref[ROWS:, lanes] = code_ref[...]
        mkv_ref[:, lanes] = product[ROWS:]


def pair_kernel(own_ref, other_ref, k_ref, v_ref):
    for i, ref in enumerate((own_ref, other_ref)):
        rows = slice(i * ROWS, (i + 1) * ROWS)
        k_ref[rows, :] = ref[:ROWS, :HEAD]
        v_ref[rows, :] = ref[:ROWS, HEAD:]
    row = lax.broadcasted_iota(jnp.int32, (PAD, HEAD), 0)
    first = ref_tail(own_ref, ROWS)
    code = jnp.where(lax.rem(row, 4) < 2, first, ref_tail(other_ref, ROWS))
    k_ref[2 * ROWS :, :] = code.astype(BF16)


def ref_tail(ref, start):
    return ref[start:, :HEAD].astype(F32)


def stack_kernel(*refs):
    ks, vs = refs[:4], refs[4:8]
    k_ref, v_ref = refs[8:]
    row = lax.broadcasted_iota(jnp.int32, (PAD, HEAD), 0)
    code = jnp.zeros((PAD, HEAD), F32)
    for i in range(4):
        rows = slice(i * 2 * ROWS, (i + 1) * 2 * ROWS)
        k_ref[rows, :] = ks[i][: 2 * ROWS, :]
        v_ref[rows, :] = vs[i][...]
        code = jnp.where(row // 4 == i, ref_tail(ks[i], 2 * ROWS), code)
    k_ref[8 * ROWS :, :] = code.astype(BF16)


def q_kernel(x_ref, wq_ref, code_ref, cut_ref, q_ref, flag_ref, own_cut_ref):
    code = code_ref[...].astype(F32)
    ids = column(code[0:1])
    order = column(code[1:2])
    blocks = cut_ref.shape[1]
    spots = lax.broadcasted_iota(jnp.int32, (ROWS, blocks), 1).astype(F32)
    cuts = jnp.broadcast_to(cut_ref[...].astype(F32), (ROWS, blocks))
    cut = jnp.sum(jnp.where(spots == ids, cuts, 0.0), axis=1, keepdims=True)
    flag = jnp.broadcast_to(jnp.where(order >= cut, 1.0, 0.0), (ROWS, HEAD))
    flag_ref[...] = flag
    own_cut_ref[...] = jnp.broadcast_to(cut, (ROWS, HEAD))
    x = x_ref[...]
    for h in range(GROUP):
        product = dot(x, wq_ref[:, h * HEAD : (h + 1) * HEAD])
        clean = product[:ROWS]
        fixed = jnp.broadcast_to(product[ROWS : ROWS + 1], (ROWS, HEAD))
        q_ref[h, :ROWS, :] = clean.astype(BF16)
        q_ref[h, ROWS:, :] = jnp.where(flag > 0.5, fixed, clean).astype(BF16)


def near_kernel(q_ref, kv_ref, mkv_ref, flag_ref, code_ref, top_ref, total_ref, accum_ref):
    masked = flag_ref[...] > 0.5

    def both(lanes):
        clean = kv_ref[:ROWS, lanes]
        fixed = jnp.broadcast_to(mkv_ref[0:1, lanes].astype(F32), (ROWS, HEAD))
        return jnp.concatenate([clean, jnp.where(masked, fixed, clean.astype(F32)).astype(BF16)], axis=0)

    row = code_ref[...].astype(F32)[0:1]
    query = jnp.broadcast_to(column(row), (ROWS, ROWS))
    key = jnp.broadcast_to(row, (ROWS, ROWS))
    zero = jnp.zeros((ROWS, ROWS), F32)
    low = jnp.full((ROWS, ROWS), LOW, F32)
    clean_bias = jnp.concatenate([jnp.where(key <= query, zero, low), low], axis=1)
    noisy_bias = jnp.concatenate([jnp.where(key < query, zero, low), jnp.where(key == query, zero, low)], axis=1)
    bias = jnp.concatenate([clean_bias, noisy_bias], axis=0)
    keys = both(slice(0, HEAD))
    values = both(slice(HEAD, 2 * HEAD))
    for h in range(GROUP):
        scores = jnp.where(bias < -1.0, LOW, dot_t(q_ref[h], keys))
        top = jnp.max(scores, axis=1, keepdims=True)
        probs = jnp.exp2((scores - top) * POWER)
        top_ref[h] = jnp.broadcast_to(top, (2 * ROWS, HEAD))
        total_ref[h] = probs[:, :HEAD] + probs[:, HEAD:]
        accum_ref[h] = dot(probs.astype(BF16), values)


def place():
    me = lax.axis_index("ctx")
    return me, me // 8, lax.rem(me // 2, 4), lax.rem(me, 2)


def pipeline(q_ref, pieces, state_in, state, finish):
    top_ref, total_ref, accum_ref = state

    def scores_of(step):
        h, chunk, _, _ = step
        keys, _, mask, _ = pieces[chunk]
        scores = dot_t(q_ref[h], keys())
        parts = [scores[:, j : j + ROWS] for j in range(0, scores.shape[1], ROWS)]
        return mask(parts) if mask is not None else parts

    def absorb(step, parts):
        h, chunk, first, last = step
        _, values, _, seen = pieces[chunk]
        best = parts[0]
        for part in parts[1:]:
            best = jnp.maximum(best, part)
        best = jnp.max(best, axis=1, keepdims=True)
        if seen is not None:
            best = jnp.where(seen, best, LOW)
        source = state_in if first else state
        old = source[0][h]
        top = jnp.maximum(old, best)
        factor = jnp.exp2((old - top) * POWER)
        level = top if seen is None else jnp.where(seen, top, -LOW)
        probs = [jnp.exp2((part - level) * POWER) for part in parts]
        total = source[1][h] * factor
        for part in probs:
            total = total + part
        probs = jnp.concatenate([part.astype(BF16) for part in probs], axis=1)
        accum = source[2][h] * factor + dot(probs, values())
        if last and finish is not None:
            finish(h, accum, total)
        else:
            top_ref[h] = top
            total_ref[h] = total
            accum_ref[h] = accum

    order = [(h, i, i == 0, i == len(pieces) - 1) for i in range(len(pieces)) for h in range(GROUP)]
    parts = scores_of(order[0])
    for now, later in zip(order, order[1:] + [None]):
        following = None if later is None else scores_of(later)
        absorb(now, parts)
        parts = following


def blocks_of(ref, which):
    return jnp.concatenate([ref[i * 2 * ROWS : (i + 1) * 2 * ROWS, :] for i in which], axis=0)


def shard_mask(where, spots):
    me, y, x, z = where

    def mask(parts):
        kept = []
        for j, part in enumerate(parts):
            dy, dx = spots[j // 2]
            there = lax.rem(y + 4 - dy, 4) * 8 + lax.rem(x + 4 - dx, 4) * 2 + lax.rem(z + j, 2)
            kept.append(jnp.where(there < me - 1, part, LOW))
        return kept

    return mask


def spots_piece(where, k_of, v_of, spots):
    def keys():
        return jnp.concatenate([k_of[dy][dx * 2 * ROWS : (dx + 1) * 2 * ROWS, :] for dy, dx in spots], axis=0)

    def values():
        return jnp.concatenate([v_of[dx][dy * 2 * ROWS : (dy + 1) * 2 * ROWS, :] for dy, dx in spots], axis=0)

    return keys, values, shard_mask(where, spots), None


def first_kernel(*refs):
    q_ref = refs[0]
    k_of, v_of = dict(zip((0, 1), refs[1:3])), dict(zip((0, 1), refs[3:5]))
    piece = spots_piece(place(), k_of, v_of, ((0, 0), (0, 1), (1, 0), (1, 1)))
    pipeline(q_ref, [piece], refs[5:8], refs[8:11], None)


def far_kernel(*refs):
    q_ref = refs[0]
    k_refs = dict(zip((0, 1, 3), refs[1:4]))
    v_refs = dict(zip((0, 1, 3), refs[4:7]))
    state_in = refs[7:10]
    code_ref, own_cut_ref, mkv_ref = refs[10:13]
    state = refs[13:16]
    me, y, x, z = place()

    wrap = (z == 0) & (x == 0)
    beyond = (z == 1) & (x == 3)

    def block(ref, index):
        return ref[index * ROWS : (index + 1) * ROWS, :]

    k_old = jnp.where(wrap, block(k_refs[1], 3), jnp.where(z == 0, block(k_refs[0], 3), block(k_refs[0], 1)))
    v_old = jnp.where(wrap, block(v_refs[1], 3), jnp.where(z == 0, block(v_refs[1], 1), block(v_refs[0], 1)))
    k_new = jnp.where(beyond, block(k_refs[3], 7), jnp.where(z == 1, block(k_refs[0], 7), block(k_refs[0], 1)))
    v_new = jnp.where(beyond, block(v_refs[3], 7), jnp.where(z == 1, block(v_refs[3], 1), block(v_refs[0], 1)))
    k_new, v_new = k_new[:BLOCK], v_new[:BLOCK]

    own = code_ref[...].astype(F32)[0:1]
    tails = {dy: ref_tail(k_refs[dy], 8 * ROWS) for dy in (0, 1, 3)}

    def line(i):
        old = jnp.where(wrap, tails[1][6 + i : 7 + i], jnp.where(z == 0, tails[0][6 + i : 7 + i], tails[0][2 + i : 3 + i]))
        new = jnp.where(beyond, tails[3][14 + i : 15 + i], jnp.where(z == 1, tails[0][14 + i : 15 + i], tails[0][2 + i : 3 + i]))
        return old, new

    old_ids, new_ids = line(0)
    old_order, new_order = line(1)
    old_ids = jnp.broadcast_to(jnp.where(me > 0, old_ids, FAR), (8, ROWS))
    new_ids = jnp.broadcast_to(jnp.where(me < LAST, new_ids, FAR), (8, ROWS))
    first_cut = own_cut_ref[0:1, :]
    last_cut = own_cut_ref[ROWS - 1 : ROWS, :]
    old_masked = column(jnp.where(old_order >= first_cut, 1.0, 0.0))[ROWS - BLOCK :]
    new_masked = column(jnp.where(new_order >= last_cut, 1.0, 0.0))[:BLOCK]

    def noisy(masked, clean, lanes):
        fixed = jnp.broadcast_to(mkv_ref[0:1, lanes].astype(F32), clean.shape)
        flag = jnp.broadcast_to(masked, clean.shape) > 0.5
        return jnp.where(flag, fixed, clean.astype(F32)).astype(BF16)

    def rim(old, new, lanes):
        parts = [old, new, noisy(old_masked, old[ROWS - BLOCK :], lanes), noisy(new_masked, new, lanes)]
        return jnp.concatenate(parts + [jnp.zeros((BLOCK, HEAD), BF16)], axis=0)

    k_rim = rim(k_old, k_new, slice(0, HEAD))
    v_rim = rim(v_old, v_new, slice(HEAD, 2 * HEAD))
    lane = lax.broadcasted_iota(jnp.int32, (8, ROWS), 1)
    mixed = jnp.where(
        lane < 32,
        new_ids,
        jnp.where(lane < 64, pltpu.roll(old_ids, 64, 1), jnp.where(lane < 96, pltpu.roll(new_ids, 64, 1), -5.0)),
    )
    square = (ROWS, ROWS)
    query = jnp.broadcast_to(column(own), square)
    old_key = jnp.broadcast_to(old_ids[0:1], square)
    mixed_key = jnp.broadcast_to(mixed[0:1], square)
    early = lax.broadcasted_iota(jnp.int32, square, 1) < 32
    zero = jnp.zeros(square, F32)
    low = jnp.full(square, LOW, F32)
    clean_bias = [
        jnp.where(old_key <= query, zero, low),
        jnp.where(early, jnp.where(mixed_key <= query, zero, low), low),
    ]
    noisy_bias = [
        jnp.where(old_key < query, zero, low),
        jnp.where(early, jnp.where(mixed_key < query, zero, low), jnp.where(mixed_key == query, zero, low)),
    ]
    bias = jnp.concatenate([jnp.concatenate(clean_bias, axis=1), jnp.concatenate(noisy_bias, axis=1)], axis=0)

    def rim_mask(parts):
        return [jnp.where(bias[:, j * ROWS : (j + 1) * ROWS] < -1.0, LOW, part) for j, part in enumerate(parts)]

    spots = ((0, 3), (1, 3), (3, 0), (3, 1), (3, 3))
    pieces = [
        (lambda: k_rim, lambda: v_rim, rim_mask, None),
        spots_piece((me, y, x, z), k_refs, v_refs, spots),
    ]
    pipeline(q_ref, pieces, state_in, state, None)


def last_kernel(*refs):
    q_ref, k_refs, v_refs = refs[0], refs[1:5], refs[5:9]
    state_in = refs[9:12]
    clean_ref, noisy_ref = refs[12:14]
    state = refs[14:]
    where = place()
    near = (0, 1, 3)
    pieces = [
        (
            lambda: blocks_of(k_refs[2], range(4)),
            lambda: jnp.concatenate([blocks_of(v_refs[dx], (2,)) for dx in range(4)], axis=0),
            None,
            where[1] >= 2,
        ),
        (
            lambda: jnp.concatenate([blocks_of(k_refs[dy], (2,)) for dy in near], axis=0),
            lambda: blocks_of(v_refs[2], near),
            shard_mask(where, [(dy, 2) for dy in near]),
            None,
        ),
    ]

    def finish(h, accum, total):
        lanes = slice(h * HEAD, (h + 1) * HEAD)
        result = (accum / jnp.sum(total, axis=1, keepdims=True)).astype(BF16)
        clean_ref[:, lanes] = result[:ROWS]
        noisy_ref[:, lanes] = result[ROWS:]

    pipeline(q_ref, pieces, state_in, state, finish)


def shards(hidden, block_ids, decode_order, step_cut, mask_embed, q_weight, k_weight, v_weight):
    ids = block_ids.reshape(1, ROWS)
    order = decode_order.reshape(1, ROWS)
    cuts = step_cut.reshape(1, -1)
    moved = [lax.ppermute(hidden, "kv", kv_pairs(d, 0)) for d in (1, 2, 3)]
    own, wk, wv, code, pad = call(
        prep_kernel,
        [
            (hidden.shape, BF16),
            (k_weight.shape, BF16),
            (v_weight.shape, BF16),
            ((PAD, ROWS), BF16),
            ((PAD, 8 * WIDTH), BF16),
        ],
        [held(a) for a in (hidden, k_weight, v_weight, ids, order, mask_embed.reshape(1, -1))],
        (1 << 20, 4 << 20),
        [
            pltpu.VMEM(ids.shape, jnp.int32),
            pltpu.VMEM(ids.shape, jnp.int32),
            pltpu.VMEM((1, 8 * WIDTH), BF16),
            pltpu.SemaphoreType.DMA((6,)),
        ],
        pl.ANY,
    )
    mine = join(own, *moved)
    other = lax.ppermute(mine, "kv", kv_pairs(0, 1))
    x, kv, mask_kv = call(
        kv_kernel,
        [
            ((ROWS + PAD, 8 * WIDTH), BF16),
            ((ROWS + PAD, 2 * HEAD), BF16),
            ((PAD, 2 * HEAD), BF16),
        ],
        [mine, other, pad, wk, wv, code],
        (1 << 29, 3 << 20),
    )
    pair = lax.ppermute(kv, "ctx", ctx_pairs(0, 0, 1))
    k, v = call(
        pair_kernel,
        [((2 * ROWS + PAD, HEAD), BF16), ((2 * ROWS, HEAD), BF16)],
        [kv, pair],
        (1 << 10, 1 << 18),
    )
    ks = [lax.ppermute(k, "ctx", ctx_pairs(0, d, 0)) for d in (1, 2, 3)]
    vs = [lax.ppermute(v, "ctx", ctx_pairs(d, 0, 0)) for d in (1, 2, 3)]
    ks, vs = call(
        stack_kernel,
        [((8 * ROWS + PAD, HEAD), BF16), ((8 * ROWS, HEAD), BF16)],
        [k, *ks, v, *vs],
        (1 << 10, 1 << 20),
    )
    q, flag, own_cut = call(
        q_kernel,
        [((GROUP, 2 * ROWS, HEAD), BF16), ((ROWS, HEAD), F32), ((ROWS, HEAD), F32)],
        [x, q_weight, code, cuts],
        (1 << 30, 5 << 20),
    )
    near = call(
        near_kernel,
        [((GROUP, 2 * ROWS, HEAD), F32)] * 3,
        [q, kv, mask_kv, flag, code],
        (1 << 30, 2 << 20),
    )
    all_k = [ks] + [lax.ppermute(ks, "ctx", ctx_pairs(d, 0, 0)) for d in (1, 2, 3)]
    all_v = [vs] + [lax.ppermute(vs, "ctx", ctx_pairs(0, d, 0)) for d in (1, 2, 3)]
    state = [((GROUP, 2 * ROWS, HEAD), F32)] * 3
    first = call(
        first_kernel,
        state,
        [q, *all_k[:2], *all_v[:2], *near],
        (1 << 30, 2 << 20),
    )
    far = call(
        far_kernel,
        state,
        [q, *[all_k[d] for d in (0, 1, 3)], *[all_v[d] for d in (0, 1, 3)], *first, code, own_cut, mask_kv],
        (1 << 31, 4 << 20),
    )
    return tuple(
        call(
            last_kernel,
            [((ROWS, GROUP * HEAD), BF16)] * 2,
            [q, *all_k, *all_v, *far],
            (1 << 31, 4 << 20),
            [pltpu.VMEM((GROUP, 2 * ROWS, HEAD), F32)] * 3,
        )
    )


def solution(mesh):
    return jax.shard_map(
        shards,
        mesh=mesh,
        in_specs=(
            P("ctx", "kv"),
            P("ctx"),
            P("ctx"),
            P(),
            P(),
            P(None, "kv"),
            P(None, "kv"),
            P(None, "kv"),
        ),
        out_specs=(P("ctx", "kv"), P("ctx", "kv")),
        check_vma=False,
    )
```

```python
import math

import jax
import jax.numpy as jnp
from jax import lax
from jax.experimental import pallas as pl
from jax.experimental.pallas import tpu as pltpu
from jax.sharding import PartitionSpec as P

ROWS = 128
HEAD = 128
GROUP = 4
PAD = 16
WIDTH = 512
BLOCK = 32
LAST = 31
LOW = -1e30
FAR = 1e6
POWER = math.log2(math.e) / math.sqrt(HEAD)
LIMIT = 48 * 1024 * 1024
F32 = jnp.float32
BF16 = jnp.bfloat16


def ctx_pairs(dy, dx, dz):
    pairs = []
    for i in range(32):
        y, x, z = i // 8, (i // 2) % 4, i % 2
        pairs.append((i, (((y + dy) % 4) * 4 + (x + dx) % 4) * 2 + (z + dz) % 2))
    return pairs


def kv_pairs(dz, dc):
    pairs = []
    for i in range(8):
        z, c = i // 2, i % 2
        pairs.append((i, ((z + dz) % 4) * 2 + (c + dc) % 2))
    return pairs


def cross_pairs(first, d):
    pairs = []
    for i in range(256):
        c, g = i // 8, i % 8
        y, x, z = c // 8, (c // 2) % 4, c % 2
        if (g % 2 == 0) == first:
            x = (x + d) % 4
        else:
            y = (y + d) % 4
        pairs.append((i, ((y * 4 + x) * 2 + z) * 8 + g))
    return pairs


def dot(a, b):
    return jnp.dot(a, b, preferred_element_type=F32)


def dot_t(a, b):
    return lax.dot_general(a, b, (((1,), (1,)), ((), ())), preferred_element_type=F32)


def call(kernel, outs, args, cost, scratch=(), space=pltpu.VMEM):
    spec = pl.BlockSpec(memory_space=pltpu.VMEM)
    return pl.pallas_call(
        kernel,
        out_shape=[jax.ShapeDtypeStruct(s, t) for s, t in outs],
        in_specs=[pl.BlockSpec(memory_space=space)] * len(args),
        out_specs=[spec] * len(outs),
        scratch_shapes=list(scratch),
        compiler_params=pltpu.CompilerParams(vmem_limit_bytes=LIMIT),
        cost_estimate=pl.CostEstimate(flops=cost[0], bytes_accessed=cost[1], transcendentals=0),
    )(*args)


def held(array):
    return pltpu.with_memory_space_constraint(array, pltpu.HBM)


def column(row):
    square = (ROWS, ROWS)
    same = lax.broadcasted_iota(jnp.int32, square, 0) == lax.broadcasted_iota(jnp.int32, square, 1)
    return jnp.sum(jnp.where(same, jnp.broadcast_to(row, square), 0.0), axis=1, keepdims=True)


def prep_kernel(*refs):
    hidden_hbm, wk_hbm, wv_hbm, ids_hbm, order_hbm, embed_hbm = refs[:6]
    own_ref, wk_ref, wv_ref, code_ref, pad_ref = refs[6:11]
    ids_ref, order_ref, embed_ref, sems = refs[11:]
    pairs = (
        (ids_hbm, ids_ref),
        (order_hbm, order_ref),
        (embed_hbm, embed_ref),
        (hidden_hbm, own_ref),
        (wk_hbm, wk_ref),
        (wv_hbm, wv_ref),
    )
    copies = [pltpu.make_async_copy(a, b, sems.at[i]) for i, (a, b) in enumerate(pairs)]
    for copy in copies:
        copy.start()
    for copy in copies:
        copy.wait()
    ids = jnp.broadcast_to(ids_ref[...].astype(F32), (PAD, ROWS))
    order = jnp.broadcast_to(order_ref[...].astype(F32), (PAD, ROWS))
    row = lax.broadcasted_iota(jnp.int32, (PAD, ROWS), 0)
    code_ref[...] = jnp.where(lax.rem(row, 2) == 0, ids, order).astype(BF16)
    pad_ref[...] = jnp.broadcast_to(embed_ref[...], pad_ref.shape)


def join_kernel(*refs):
    out_ref = refs[-1]
    rows = refs[0].shape[0]
    for i, ref in enumerate(refs[:-1]):
        out_ref[i * rows : (i + 1) * rows, :] = ref[...]


def join(*arrays):
    rows = sum(a.shape[0] for a in arrays)
    (out,) = call(join_kernel, [((rows, WIDTH), BF16)], arrays, (1 << 10, 1 << 19))
    return out


def kv_kernel(*refs):
    mine, other, pad_ref, wk_ref, wv_ref = refs[:5]
    x_ref, kv_ref, mkv_ref, keep_ref, give_ref = refs[5:]
    me = lax.axis_index("kv")
    for dc, ref in enumerate((mine, other)):
        for dz in range(4):
            source = lax.rem(me // 2 + 4 - dz, 4) * 2 + lax.rem(me + dc, 2)
            lanes = pl.ds(pl.multiple_of(source * WIDTH, WIDTH), WIDTH)
            x_ref[:ROWS, lanes] = ref[dz * ROWS : (dz + 1) * ROWS, :]
    x_ref[ROWS:, :] = pad_ref[...]
    x = x_ref[...]
    products = [dot(x, w_ref[...]).astype(BF16) for w_ref in (wk_ref, wv_ref)]
    for part, product in enumerate(products):
        lanes = slice(part * HEAD, (part + 1) * HEAD)
        kv_ref[:, lanes] = product[:ROWS]
        mkv_ref[:, lanes] = product[ROWS:]
    even = lax.rem(me, 2) == 0

    @pl.when(even)
    def _():
        keep_ref[...] = products[0][:ROWS]
        give_ref[...] = products[1][:ROWS]

    @pl.when(jnp.logical_not(even))
    def _():
        keep_ref[...] = products[1][:ROWS]
        give_ref[...] = products[0][:ROWS]


def merge_kernel(keep_ref, got_ref, code_ref, out_ref):
    for ref, lanes in ((keep_ref, slice(0, HEAD)), (got_ref, slice(HEAD, 2 * HEAD))):
        out_ref[:ROWS, lanes] = ref[...]
        out_ref[ROWS:, lanes] = code_ref[...]


def pair_kernel(own_ref, other_ref, out_ref):
    out_ref[:ROWS, :] = own_ref[:ROWS, :]
    out_ref[ROWS : 2 * ROWS, :] = other_ref[:ROWS, :]
    row = lax.broadcasted_iota(jnp.int32, (PAD, 2 * HEAD), 0)
    code = jnp.where(lax.rem(row, 4) < 2, own_ref[ROWS:, :].astype(F32), other_ref[ROWS:, :].astype(F32))
    out_ref[2 * ROWS :, :] = code.astype(BF16)


def stack_kernel(a_ref, b_ref, c_ref, d_ref, out_ref, over_ref):
    row = lax.broadcasted_iota(jnp.int32, (PAD, 2 * HEAD), 0)
    code = jnp.zeros((PAD, 2 * HEAD), F32)
    for i, ref in enumerate((a_ref, b_ref, c_ref, d_ref)):
        rows = slice(i * 2 * ROWS, (i + 1) * 2 * ROWS)
        out_ref[rows, :] = ref[: 2 * ROWS, :]
        over_ref[rows, :] = ref[: 2 * ROWS, HEAD:]
        code = jnp.where(row // 4 == i, ref[2 * ROWS :, :].astype(F32), code)
    out_ref[8 * ROWS :, :] = code.astype(BF16)
    over_ref[8 * ROWS :, :] = code[:, :HEAD].astype(BF16)


def ref_tail(ref, start):
    return ref[start:, :HEAD].astype(F32)


def over_kernel(source_ref, out_ref):
    out_ref[...] = source_ref[:, HEAD:]


def sort_out(direct, swapped, keys, values):
    even = lax.rem(lax.axis_index("kv"), 2) == 0

    @pl.when(even)
    def _():
        for a, b, k, v in zip(direct, swapped, keys, values):
            k[...] = a[:, :HEAD]
            v[...] = b[: v.shape[0], :]

    @pl.when(jnp.logical_not(even))
    def _():
        for a, b, k, v in zip(direct, swapped, keys, values):
            v[...] = a[:, :HEAD]
            k[...] = b[: k.shape[0], :]


def mask_rows(mkv_ref):
    rows = mkv_ref[0:1, :].astype(F32)
    return rows[:, :HEAD], rows[:, HEAD:]


def q_kernel(x_ref, wq_ref, code_ref, cut_ref, q_ref, flag_ref, own_cut_ref):
    code = code_ref[...].astype(F32)
    ids = column(code[0:1])
    order = column(code[1:2])
    blocks = cut_ref.shape[1]
    spots = lax.broadcasted_iota(jnp.int32, (ROWS, blocks), 1).astype(F32)
    cuts = jnp.broadcast_to(cut_ref[...].astype(F32), (ROWS, blocks))
    cut = jnp.sum(jnp.where(spots == ids, cuts, 0.0), axis=1, keepdims=True)
    flag = jnp.broadcast_to(jnp.where(order >= cut, 1.0, 0.0), (ROWS, HEAD))
    flag_ref[...] = flag
    own_cut_ref[...] = jnp.broadcast_to(cut, (ROWS, HEAD))
    x = x_ref[...]
    for h in range(GROUP):
        product = dot(x, wq_ref[:, h * HEAD : (h + 1) * HEAD])
        clean = product[:ROWS]
        fixed = jnp.broadcast_to(product[ROWS : ROWS + 1], (ROWS, HEAD))
        q_ref[h, :ROWS, :] = clean.astype(BF16)
        q_ref[h, ROWS:, :] = jnp.where(flag > 0.5, fixed, clean).astype(BF16)


def near_kernel(q_ref, kv_ref, mkv_ref, flag_ref, code_ref, top_ref, total_ref, accum_ref):
    masked = flag_ref[...] > 0.5

    def both(clean, fixed):
        fixed = jnp.broadcast_to(fixed, (ROWS, HEAD))
        return jnp.concatenate([clean, jnp.where(masked, fixed, clean.astype(F32)).astype(BF16)], axis=0)

    row = code_ref[...].astype(F32)[0:1]
    query = jnp.broadcast_to(column(row), (ROWS, ROWS))
    key = jnp.broadcast_to(row, (ROWS, ROWS))
    zero = jnp.zeros((ROWS, ROWS), F32)
    low = jnp.full((ROWS, ROWS), LOW, F32)
    clean_bias = jnp.concatenate([jnp.where(key <= query, zero, low), low], axis=1)
    noisy_bias = jnp.concatenate([jnp.where(key < query, zero, low), jnp.where(key == query, zero, low)], axis=1)
    bias = jnp.concatenate([clean_bias, noisy_bias], axis=0)
    k_fixed, v_fixed = mask_rows(mkv_ref)
    keys = both(kv_ref[:, :HEAD], k_fixed)
    values = both(kv_ref[:, HEAD:], v_fixed)
    for h in range(GROUP):
        scores = jnp.where(bias < -1.0, LOW, dot_t(q_ref[h], keys))
        top = jnp.max(scores, axis=1, keepdims=True)
        probs = jnp.exp2((scores - top) * POWER)
        top_ref[h] = jnp.broadcast_to(top, (2 * ROWS, HEAD))
        total_ref[h] = probs[:, :HEAD] + probs[:, HEAD:]
        accum_ref[h] = dot(probs.astype(BF16), values)


def place():
    me = lax.axis_index("ctx")
    return me, me // 8, lax.rem(me // 2, 4), lax.rem(me, 2)


def pipeline(q_ref, pieces, state_in, state, finish):
    top_ref, total_ref, accum_ref = state

    def scores_of(step):
        h, chunk, _, _ = step
        keys, _, mask, _ = pieces[chunk]
        scores = dot_t(q_ref[h], keys())
        parts = [scores[:, j : j + ROWS] for j in range(0, scores.shape[1], ROWS)]
        return mask(parts) if mask is not None else parts

    def absorb(step, parts):
        h, chunk, first, last = step
        _, values, _, seen = pieces[chunk]
        best = parts[0]
        for part in parts[1:]:
            best = jnp.maximum(best, part)
        best = jnp.max(best, axis=1, keepdims=True)
        if seen is not None:
            best = jnp.where(seen, best, LOW)
        source = state_in if first else state
        old = source[0][h]
        top = jnp.maximum(old, best)
        factor = jnp.exp2((old - top) * POWER)
        level = top if seen is None else jnp.where(seen, top, -LOW)
        probs = [jnp.exp2((part - level) * POWER) for part in parts]
        total = source[1][h] * factor
        for part in probs:
            total = total + part
        probs = jnp.concatenate([part.astype(BF16) for part in probs], axis=1)
        accum = source[2][h] * factor + dot(probs, values())
        if last and finish is not None:
            finish(h, accum, total)
        else:
            top_ref[h] = top
            total_ref[h] = total
            accum_ref[h] = accum

    order = [(h, i, i == 0, i == len(pieces) - 1) for i in range(len(pieces)) for h in range(GROUP)]
    parts = scores_of(order[0])
    for now, later in zip(order, order[1:] + [None]):
        following = None if later is None else scores_of(later)
        absorb(now, parts)
        parts = following


def blocks_of(ref, which):
    return jnp.concatenate([ref[i * 2 * ROWS : (i + 1) * 2 * ROWS, :] for i in which], axis=0)


def shard_mask(where, spots):
    me, y, x, z = where

    def mask(parts):
        kept = []
        for j, part in enumerate(parts):
            dy, dx = spots[j // 2]
            there = lax.rem(y + 4 - dy, 4) * 8 + lax.rem(x + 4 - dx, 4) * 2 + lax.rem(z + j, 2)
            kept.append(jnp.where(there < me - 1, part, LOW))
        return kept

    return mask


def spots_piece(where, k_of, v_of, spots):
    def keys():
        return jnp.concatenate([k_of[dy][dx * 2 * ROWS : (dx + 1) * 2 * ROWS, :] for dy, dx in spots], axis=0)

    def values():
        return jnp.concatenate([v_of[dx][dy * 2 * ROWS : (dy + 1) * 2 * ROWS, :] for dy, dx in spots], axis=0)

    return keys, values, shard_mask(where, spots), None


def first_kernel(*refs):
    q_ref, direct, swapped = refs[0], refs[1:3], refs[3:5]
    keys, values = refs[11:13], refs[13:15]
    sort_out(direct, swapped, keys, values)
    k_of, v_of = dict(zip((0, 1), keys)), dict(zip((0, 1), values))
    piece = spots_piece(place(), k_of, v_of, ((0, 0), (0, 1), (1, 0), (1, 1)))
    pipeline(q_ref, [piece], refs[5:8], refs[8:11], None)


def far_kernel(*refs):
    q_ref, direct, swapped = refs[0], refs[1:4], refs[4:7]
    state_in = refs[7:10]
    code_ref, own_cut_ref, mkv_ref = refs[10:13]
    state = refs[13:16]
    keys, values = refs[16:19], refs[19:22]
    sort_out(direct, swapped, keys, values)
    k_refs = dict(zip((0, 1, 3), keys))
    v_refs = dict(zip((0, 1, 3), values))
    k_fixed, v_fixed = mask_rows(mkv_ref)
    me, y, x, z = place()

    wrap = (z == 0) & (x == 0)
    beyond = (z == 1) & (x == 3)

    def block(ref, index):
        return ref[index * ROWS : (index + 1) * ROWS, :]

    k_old = jnp.where(wrap, block(k_refs[1], 3), jnp.where(z == 0, block(k_refs[0], 3), block(k_refs[0], 1)))
    v_old = jnp.where(wrap, block(v_refs[1], 3), jnp.where(z == 0, block(v_refs[1], 1), block(v_refs[0], 1)))
    k_new = jnp.where(beyond, block(k_refs[3], 7), jnp.where(z == 1, block(k_refs[0], 7), block(k_refs[0], 1)))
    v_new = jnp.where(beyond, block(v_refs[3], 7), jnp.where(z == 1, block(v_refs[3], 1), block(v_refs[0], 1)))
    k_new, v_new = k_new[:BLOCK], v_new[:BLOCK]

    own = code_ref[...].astype(F32)[0:1]
    tails = {dy: ref_tail(k_refs[dy], 8 * ROWS) for dy in (0, 1, 3)}

    def line(i):
        old = jnp.where(wrap, tails[1][6 + i : 7 + i], jnp.where(z == 0, tails[0][6 + i : 7 + i], tails[0][2 + i : 3 + i]))
        new = jnp.where(beyond, tails[3][14 + i : 15 + i], jnp.where(z == 1, tails[0][14 + i : 15 + i], tails[0][2 + i : 3 + i]))
        return old, new

    old_ids, new_ids = line(0)
    old_order, new_order = line(1)
    old_ids = jnp.broadcast_to(jnp.where(me > 0, old_ids, FAR), (8, ROWS))
    new_ids = jnp.broadcast_to(jnp.where(me < LAST, new_ids, FAR), (8, ROWS))
    first_cut = own_cut_ref[0:1, :]
    last_cut = own_cut_ref[ROWS - 1 : ROWS, :]
    old_masked = column(jnp.where(old_order >= first_cut, 1.0, 0.0))[ROWS - BLOCK :]
    new_masked = column(jnp.where(new_order >= last_cut, 1.0, 0.0))[:BLOCK]

    def noisy(masked, clean, fixed):
        fixed = jnp.broadcast_to(fixed, clean.shape)
        flag = jnp.broadcast_to(masked, clean.shape) > 0.5
        return jnp.where(flag, fixed, clean.astype(F32)).astype(BF16)

    def rim(old, new, fixed):
        parts = [old, new, noisy(old_masked, old[ROWS - BLOCK :], fixed), noisy(new_masked, new, fixed)]
        return jnp.concatenate(parts + [jnp.zeros((BLOCK, HEAD), BF16)], axis=0)

    k_rim = rim(k_old, k_new, k_fixed)
    v_rim = rim(v_old, v_new, v_fixed)
    lane = lax.broadcasted_iota(jnp.int32, (8, ROWS), 1)
    mixed = jnp.where(
        lane < 32,
        new_ids,
        jnp.where(lane < 64, pltpu.roll(old_ids, 64, 1), jnp.where(lane < 96, pltpu.roll(new_ids, 64, 1), -5.0)),
    )
    square = (ROWS, ROWS)
    query = jnp.broadcast_to(column(own), square)
    old_key = jnp.broadcast_to(old_ids[0:1], square)
    mixed_key = jnp.broadcast_to(mixed[0:1], square)
    early = lax.broadcasted_iota(jnp.int32, square, 1) < 32
    zero = jnp.zeros(square, F32)
    low = jnp.full(square, LOW, F32)
    clean_bias = [
        jnp.where(old_key <= query, zero, low),
        jnp.where(early, jnp.where(mixed_key <= query, zero, low), low),
    ]
    noisy_bias = [
        jnp.where(old_key < query, zero, low),
        jnp.where(early, jnp.where(mixed_key < query, zero, low), jnp.where(mixed_key == query, zero, low)),
    ]
    bias = jnp.concatenate([jnp.concatenate(clean_bias, axis=1), jnp.concatenate(noisy_bias, axis=1)], axis=0)

    def rim_mask(parts):
        return [jnp.where(bias[:, j * ROWS : (j + 1) * ROWS] < -1.0, LOW, part) for j, part in enumerate(parts)]

    spots = ((0, 3), (1, 3), (3, 0), (3, 1), (3, 3))
    pieces = [
        (lambda: k_rim, lambda: v_rim, rim_mask, None),
        spots_piece((me, y, x, z), k_refs, v_refs, spots),
    ]
    pipeline(q_ref, pieces, state_in, state, None)


def last_kernel(*refs):
    q_ref, direct, swapped = refs[0], refs[1:5], refs[5:9]
    state_in = refs[9:12]
    clean_ref, noisy_ref = refs[12:14]
    state = refs[14:17]
    k_refs, v_refs = refs[17:21], refs[21:25]
    sort_out(direct, swapped, k_refs, v_refs)
    where = place()
    near = (0, 1, 3)
    pieces = [
        (
            lambda: blocks_of(k_refs[2], range(4)),
            lambda: jnp.concatenate([blocks_of(v_refs[dx], (2,)) for dx in range(4)], axis=0),
            None,
            where[1] >= 2,
        ),
        (
            lambda: jnp.concatenate([blocks_of(k_refs[dy], (2,)) for dy in near], axis=0),
            lambda: blocks_of(v_refs[2], near),
            shard_mask(where, [(dy, 2) for dy in near]),
            None,
        ),
    ]

    def finish(h, accum, total):
        lanes = slice(h * HEAD, (h + 1) * HEAD)
        result = (accum / jnp.sum(total, axis=1, keepdims=True)).astype(BF16)
        clean_ref[:, lanes] = result[:ROWS]
        noisy_ref[:, lanes] = result[ROWS:]

    pipeline(q_ref, pieces, state_in, state, finish)


def shards(hidden, block_ids, decode_order, step_cut, mask_embed, q_weight, k_weight, v_weight):
    ids = block_ids.reshape(1, ROWS)
    order = decode_order.reshape(1, ROWS)
    cuts = step_cut.reshape(1, -1)
    moved = [lax.ppermute(hidden, "kv", kv_pairs(d, 0)) for d in (1, 2, 3)]
    own, wk, wv, code, pad = call(
        prep_kernel,
        [
            (hidden.shape, BF16),
            (k_weight.shape, BF16),
            (v_weight.shape, BF16),
            ((PAD, ROWS), BF16),
            ((PAD, 8 * WIDTH), BF16),
        ],
        [held(a) for a in (hidden, k_weight, v_weight, ids, order, mask_embed.reshape(1, -1))],
        (1 << 20, 4 << 20),
        [
            pltpu.VMEM(ids.shape, jnp.int32),
            pltpu.VMEM(ids.shape, jnp.int32),
            pltpu.VMEM((1, 8 * WIDTH), BF16),
            pltpu.SemaphoreType.DMA((6,)),
        ],
        pl.ANY,
    )
    mine = join(own, *moved)
    other = lax.ppermute(mine, "kv", kv_pairs(0, 1))
    x, kv, mask_kv, keep, give = call(
        kv_kernel,
        [
            ((ROWS + PAD, 8 * WIDTH), BF16),
            ((ROWS, 2 * HEAD), BF16),
            ((PAD, 2 * HEAD), BF16),
            ((ROWS, HEAD), BF16),
            ((ROWS, HEAD), BF16),
        ],
        [mine, other, pad, wk, wv],
        (1 << 29, 3 << 20),
    )
    got = lax.ppermute(give, "kv", kv_pairs(0, 1))
    (lot,) = call(merge_kernel, [((ROWS + PAD, 2 * HEAD), BF16)], [keep, got, code], (1 << 10, 1 << 18))
    pair = lax.ppermute(lot, "ctx", ctx_pairs(0, 0, 1))
    (both,) = call(pair_kernel, [((2 * ROWS + PAD, 2 * HEAD), BF16)], [lot, pair], (1 << 10, 1 << 18))
    axes = ("ctx", "kv")
    parts = [both] + [lax.ppermute(both, axes, cross_pairs(True, d)) for d in (1, 2, 3)]
    tall = 8 * ROWS + PAD
    held_here, over = call(
        stack_kernel,
        [((tall, 2 * HEAD), BF16), ((tall, HEAD), BF16)],
        parts,
        (1 << 10, 1 << 20),
    )
    direct = [held_here] + [lax.ppermute(held_here, axes, cross_pairs(False, d)) for d in (1, 2, 3)]
    swapped = [lax.ppermute(over, "kv", kv_pairs(0, 1)), None, None, None]
    q, flag, own_cut = call(
        q_kernel,
        [((GROUP, 2 * ROWS, HEAD), BF16), ((ROWS, HEAD), F32), ((ROWS, HEAD), F32)],
        [x, q_weight, code, cuts],
        (1 << 30, 5 << 20),
    )
    state = [((GROUP, 2 * ROWS, HEAD), F32)] * 3

    def room(count):
        return [pltpu.VMEM((tall, HEAD), BF16)] * (2 * count)

    near = call(
        near_kernel,
        state,
        [q, kv, mask_kv, flag, code],
        (1 << 30, 2 << 20),
    )
    def cross(i, before):
        direct[i], _ = lax.optimization_barrier((direct[i], before[0]))
        (over,) = call(over_kernel, [((tall, HEAD), BF16)], [direct[i]], (1 << 10, 1 << 19))
        swapped[i] = lax.ppermute(over, "kv", kv_pairs(0, 1))

    cross(1, near)
    cross(3, near)
    first = call(first_kernel, state, [q, *direct[:2], *swapped[:2], *near], (1 << 30, 2 << 20), room(2))
    cross(2, first)
    some = (0, 1, 3)
    far = call(
        far_kernel,
        state,
        [q, *[direct[d] for d in some], *[swapped[d] for d in some], *first, code, own_cut, mask_kv],
        (1 << 31, 4 << 20),
        room(3),
    )
    return tuple(
        call(
            last_kernel,
            [((ROWS, GROUP * HEAD), BF16)] * 2,
            [q, *direct, *swapped, *far],
            (1 << 31, 4 << 20),
            [pltpu.VMEM((GROUP, 2 * ROWS, HEAD), F32)] * 3 + room(4),
        )
    )


def solution(mesh):
    return jax.shard_map(
        shards,
        mesh=mesh,
        in_specs=(
            P("ctx", "kv"),
            P("ctx"),
            P("ctx"),
            P(),
            P(),
            P(None, "kv"),
            P(None, "kv"),
            P(None, "kv"),
        ),
        out_specs=(P("ctx", "kv"), P("ctx", "kv")),
        check_vma=False,
    )
```

```python
import math

import jax
import jax.numpy as jnp
from jax import lax
from jax.experimental import pallas as pl
from jax.experimental.pallas import tpu as pltpu
from jax.sharding import PartitionSpec as P

ROWS = 128
HEAD = 128
GROUP = 4
PAD = 16
WIDTH = 512
BLOCK = 32
LAST = 31
LOW = -1e30
FAR = 1e6
POWER = math.log2(math.e) / math.sqrt(HEAD)
LIMIT = 48 * 1024 * 1024
F32 = jnp.float32
BF16 = jnp.bfloat16


def ctx_pairs(dy, dx, dz):
    pairs = []
    for i in range(32):
        y, x, z = i // 8, (i // 2) % 4, i % 2
        pairs.append((i, (((y + dy) % 4) * 4 + (x + dx) % 4) * 2 + (z + dz) % 2))
    return pairs


def kv_pairs(dz, dc):
    pairs = []
    for i in range(8):
        z, c = i // 2, i % 2
        pairs.append((i, ((z + dz) % 4) * 2 + (c + dc) % 2))
    return pairs


def dot(a, b):
    return jnp.dot(a, b, preferred_element_type=F32)


def dot_t(a, b):
    return lax.dot_general(a, b, (((1,), (1,)), ((), ())), preferred_element_type=F32)


def call(kernel, outs, args, cost, scratch=(), space=pltpu.VMEM):
    spec = pl.BlockSpec(memory_space=pltpu.VMEM)
    return pl.pallas_call(
        kernel,
        out_shape=[jax.ShapeDtypeStruct(s, t) for s, t in outs],
        in_specs=[pl.BlockSpec(memory_space=space)] * len(args),
        out_specs=[spec] * len(outs),
        scratch_shapes=list(scratch),
        compiler_params=pltpu.CompilerParams(vmem_limit_bytes=LIMIT),
        cost_estimate=pl.CostEstimate(flops=cost[0], bytes_accessed=cost[1], transcendentals=0),
    )(*args)


def held(array):
    return pltpu.with_memory_space_constraint(array, pltpu.HBM)


def column(row):
    square = (ROWS, ROWS)
    same = lax.broadcasted_iota(jnp.int32, square, 0) == lax.broadcasted_iota(jnp.int32, square, 1)
    return jnp.sum(jnp.where(same, jnp.broadcast_to(row, square), 0.0), axis=1, keepdims=True)


def prep_kernel(*refs):
    hidden_hbm, wk_hbm, wv_hbm, ids_hbm, order_hbm, embed_hbm = refs[:6]
    own_ref, wk_ref, wv_ref, code_ref, pad_ref = refs[6:11]
    ids_ref, order_ref, embed_ref, sems = refs[11:]
    pairs = (
        (ids_hbm, ids_ref),
        (order_hbm, order_ref),
        (embed_hbm, embed_ref),
        (hidden_hbm, own_ref),
        (wk_hbm, wk_ref),
        (wv_hbm, wv_ref),
    )
    copies = [pltpu.make_async_copy(a, b, sems.at[i]) for i, (a, b) in enumerate(pairs)]
    for copy in copies:
        copy.start()
    for copy in copies:
        copy.wait()
    ids = jnp.broadcast_to(ids_ref[...].astype(F32), (PAD, ROWS))
    order = jnp.broadcast_to(order_ref[...].astype(F32), (PAD, ROWS))
    row = lax.broadcasted_iota(jnp.int32, (PAD, ROWS), 0)
    code_ref[...] = jnp.where(lax.rem(row, 2) == 0, ids, order).astype(BF16)
    pad_ref[...] = jnp.broadcast_to(embed_ref[...], pad_ref.shape)


def kv_kernel(*refs):
    pieces = refs[:8]
    pad_ref, wk_ref, wv_ref, code_ref = refs[8:12]
    x_ref, kv_ref, mkv_ref = refs[12:]
    me = lax.axis_index("kv")
    for dz in range(4):
        for dc in range(2):
            source = lax.rem(me // 2 + 4 - dz, 4) * 2 + lax.rem(me + dc, 2)
            lanes = pl.ds(pl.multiple_of(source * WIDTH, WIDTH), WIDTH)
            x_ref[:ROWS, lanes] = pieces[2 * dz + dc][...]
    x_ref[ROWS:, :] = pad_ref[...]
    x = x_ref[...]
    for part, w_ref in enumerate((wk_ref, wv_ref)):
        lanes = slice(part * HEAD, (part + 1) * HEAD)
        product = dot(x, w_ref[...]).astype(BF16)
        kv_ref[:ROWS, lanes] = product[:ROWS]
        kv_ref[ROWS:, lanes] = code_ref[...]
        mkv_ref[:, lanes] = product[ROWS:]


def pair_kernel(own_ref, other_ref, k_ref, v_ref):
    for i, ref in enumerate((own_ref, other_ref)):
        rows = slice(i * ROWS, (i + 1) * ROWS)
        k_ref[rows, :] = ref[:ROWS, :HEAD]
        v_ref[rows, :] = ref[:ROWS, HEAD:]
    row = lax.broadcasted_iota(jnp.int32, (PAD, HEAD), 0)
    first = ref_tail(own_ref, ROWS)
    code = jnp.where(lax.rem(row, 4) < 2, first, ref_tail(other_ref, ROWS))
    k_ref[2 * ROWS :, :] = code.astype(BF16)


def ref_tail(ref, start):
    return ref[start:, :HEAD].astype(F32)


def stack_kernel(*refs):
    ks, vs = refs[:4], refs[4:8]
    k_ref, v_ref = refs[8:]
    row = lax.broadcasted_iota(jnp.int32, (PAD, HEAD), 0)
    code = jnp.zeros((PAD, HEAD), F32)
    for i in range(4):
        rows = slice(i * 2 * ROWS, (i + 1) * 2 * ROWS)
        k_ref[rows, :] = ks[i][: 2 * ROWS, :]
        v_ref[rows, :] = vs[i][...]
        code = jnp.where(row // 4 == i, ref_tail(ks[i], 2 * ROWS), code)
    k_ref[8 * ROWS :, :] = code.astype(BF16)


def q_kernel(x_ref, wq_ref, code_ref, cut_ref, q_ref, flag_ref, own_cut_ref):
    code = code_ref[...].astype(F32)
    ids = column(code[0:1])
    order = column(code[1:2])
    blocks = cut_ref.shape[1]
    spots = lax.broadcasted_iota(jnp.int32, (ROWS, blocks), 1).astype(F32)
    cuts = jnp.broadcast_to(cut_ref[...].astype(F32), (ROWS, blocks))
    cut = jnp.sum(jnp.where(spots == ids, cuts, 0.0), axis=1, keepdims=True)
    flag = jnp.broadcast_to(jnp.where(order >= cut, 1.0, 0.0), (ROWS, HEAD))
    flag_ref[...] = flag
    own_cut_ref[...] = jnp.broadcast_to(cut, (ROWS, HEAD))
    x = x_ref[...]
    for h in range(GROUP):
        product = dot(x, wq_ref[:, h * HEAD : (h + 1) * HEAD])
        clean = product[:ROWS]
        fixed = jnp.broadcast_to(product[ROWS : ROWS + 1], (ROWS, HEAD))
        q_ref[h, :ROWS, :] = clean.astype(BF16)
        q_ref[h, ROWS:, :] = jnp.where(flag > 0.5, fixed, clean).astype(BF16)


def near_kernel(q_ref, kv_ref, mkv_ref, flag_ref, code_ref, top_ref, total_ref, accum_ref):
    masked = flag_ref[...] > 0.5

    def both(lanes):
        clean = kv_ref[:ROWS, lanes]
        fixed = jnp.broadcast_to(mkv_ref[0:1, lanes].astype(F32), (ROWS, HEAD))
        return jnp.concatenate([clean, jnp.where(masked, fixed, clean.astype(F32)).astype(BF16)], axis=0)

    row = code_ref[...].astype(F32)[0:1]
    query = jnp.broadcast_to(column(row), (ROWS, ROWS))
    key = jnp.broadcast_to(row, (ROWS, ROWS))
    zero = jnp.zeros((ROWS, ROWS), F32)
    low = jnp.full((ROWS, ROWS), LOW, F32)
    clean_bias = jnp.concatenate([jnp.where(key <= query, zero, low), low], axis=1)
    noisy_bias = jnp.concatenate([jnp.where(key < query, zero, low), jnp.where(key == query, zero, low)], axis=1)
    bias = jnp.concatenate([clean_bias, noisy_bias], axis=0)
    keys = both(slice(0, HEAD))
    values = both(slice(HEAD, 2 * HEAD))
    for h in range(GROUP):
        scores = jnp.where(bias < -1.0, LOW, dot_t(q_ref[h], keys))
        top = jnp.max(scores, axis=1, keepdims=True)
        probs = jnp.exp2((scores - top) * POWER)
        top_ref[h] = jnp.broadcast_to(top, (2 * ROWS, HEAD))
        total_ref[h] = probs[:, :HEAD] + probs[:, HEAD:]
        accum_ref[h] = dot(probs.astype(BF16), values)


def place():
    me = lax.axis_index("ctx")
    return me, me // 8, lax.rem(me // 2, 4), lax.rem(me, 2)


def pipeline(q_ref, pieces, state_in, state, finish):
    top_ref, total_ref, accum_ref = state

    def scores_of(step):
        h, chunk, _, _ = step
        keys, _, mask, _ = pieces[chunk]
        scores = dot_t(q_ref[h], keys())
        parts = [scores[:, j : j + ROWS] for j in range(0, scores.shape[1], ROWS)]
        return mask(parts) if mask is not None else parts

    def absorb(step, parts):
        h, chunk, first, last = step
        _, values, _, seen = pieces[chunk]
        best = parts[0]
        for part in parts[1:]:
            best = jnp.maximum(best, part)
        best = jnp.max(best, axis=1, keepdims=True)
        if seen is not None:
            best = jnp.where(seen, best, LOW)
        source = state_in if first else state
        old = source[0][h]
        top = jnp.maximum(old, best)
        factor = jnp.exp2((old - top) * POWER)
        level = top if seen is None else jnp.where(seen, top, -LOW)
        probs = [jnp.exp2((part - level) * POWER) for part in parts]
        total = source[1][h] * factor
        for part in probs:
            total = total + part
        probs = jnp.concatenate([part.astype(BF16) for part in probs], axis=1)
        accum = source[2][h] * factor + dot(probs, values())
        if last and finish is not None:
            finish(h, accum, total)
        else:
            top_ref[h] = top
            total_ref[h] = total
            accum_ref[h] = accum

    order = [(h, i, i == 0, i == len(pieces) - 1) for i in range(len(pieces)) for h in range(GROUP)]
    parts = scores_of(order[0])
    for now, later in zip(order, order[1:] + [None]):
        following = None if later is None else scores_of(later)
        absorb(now, parts)
        parts = following


def blocks_of(ref, which):
    return jnp.concatenate([ref[i * 2 * ROWS : (i + 1) * 2 * ROWS, :] for i in which], axis=0)


def shard_mask(where, spots):
    me, y, x, z = where

    def mask(parts):
        kept = []
        for j, part in enumerate(parts):
            dy, dx = spots[j // 2]
            there = lax.rem(y + 4 - dy, 4) * 8 + lax.rem(x + 4 - dx, 4) * 2 + lax.rem(z + j, 2)
            kept.append(jnp.where(there < me - 1, part, LOW))
        return kept

    return mask


def spots_piece(where, k_of, v_of, spots):
    def keys():
        return jnp.concatenate([k_of[dy][dx * 2 * ROWS : (dx + 1) * 2 * ROWS, :] for dy, dx in spots], axis=0)

    def values():
        return jnp.concatenate([v_of[dx][dy * 2 * ROWS : (dy + 1) * 2 * ROWS, :] for dy, dx in spots], axis=0)

    return keys, values, shard_mask(where, spots), None


def first_kernel(*refs):
    q_ref = refs[0]
    k_of, v_of = dict(zip((0, 1), refs[1:3])), dict(zip((0, 1), refs[3:5]))
    piece = spots_piece(place(), k_of, v_of, ((0, 0), (0, 1), (1, 0), (1, 1)))
    pipeline(q_ref, [piece], refs[5:8], refs[8:11], None)


def far_kernel(*refs):
    q_ref = refs[0]
    k_refs = dict(zip((0, 1, 3), refs[1:4]))
    v_refs = dict(zip((0, 1, 3), refs[4:7]))
    state_in = refs[7:10]
    code_ref, own_cut_ref, mkv_ref = refs[10:13]
    state = refs[13:16]
    me, y, x, z = place()

    wrap = (z == 0) & (x == 0)
    beyond = (z == 1) & (x == 3)

    def block(ref, index):
        return ref[index * ROWS : (index + 1) * ROWS, :]

    k_old = jnp.where(wrap, block(k_refs[1], 3), jnp.where(z == 0, block(k_refs[0], 3), block(k_refs[0], 1)))
    v_old = jnp.where(wrap, block(v_refs[1], 3), jnp.where(z == 0, block(v_refs[1], 1), block(v_refs[0], 1)))
    k_new = jnp.where(beyond, block(k_refs[3], 7), jnp.where(z == 1, block(k_refs[0], 7), block(k_refs[0], 1)))
    v_new = jnp.where(beyond, block(v_refs[3], 7), jnp.where(z == 1, block(v_refs[3], 1), block(v_refs[0], 1)))
    k_new, v_new = k_new[:BLOCK], v_new[:BLOCK]

    own = code_ref[...].astype(F32)[0:1]
    tails = {dy: ref_tail(k_refs[dy], 8 * ROWS) for dy in (0, 1, 3)}

    def line(i):
        old = jnp.where(wrap, tails[1][6 + i : 7 + i], jnp.where(z == 0, tails[0][6 + i : 7 + i], tails[0][2 + i : 3 + i]))
        new = jnp.where(beyond, tails[3][14 + i : 15 + i], jnp.where(z == 1, tails[0][14 + i : 15 + i], tails[0][2 + i : 3 + i]))
        return old, new

    old_ids, new_ids = line(0)
    old_order, new_order = line(1)
    old_ids = jnp.broadcast_to(jnp.where(me > 0, old_ids, FAR), (8, ROWS))
    new_ids = jnp.broadcast_to(jnp.where(me < LAST, new_ids, FAR), (8, ROWS))
    first_cut = own_cut_ref[0:1, :]
    last_cut = own_cut_ref[ROWS - 1 : ROWS, :]
    old_masked = column(jnp.where(old_order >= first_cut, 1.0, 0.0))[ROWS - BLOCK :]
    new_masked = column(jnp.where(new_order >= last_cut, 1.0, 0.0))[:BLOCK]

    def noisy(masked, clean, lanes):
        fixed = jnp.broadcast_to(mkv_ref[0:1, lanes].astype(F32), clean.shape)
        flag = jnp.broadcast_to(masked, clean.shape) > 0.5
        return jnp.where(flag, fixed, clean.astype(F32)).astype(BF16)

    def rim(old, new, lanes):
        parts = [old, new, noisy(old_masked, old[ROWS - BLOCK :], lanes), noisy(new_masked, new, lanes)]
        return jnp.concatenate(parts + [jnp.zeros((BLOCK, HEAD), BF16)], axis=0)

    k_rim = rim(k_old, k_new, slice(0, HEAD))
    v_rim = rim(v_old, v_new, slice(HEAD, 2 * HEAD))
    lane = lax.broadcasted_iota(jnp.int32, (8, ROWS), 1)
    mixed = jnp.where(
        lane < 32,
        new_ids,
        jnp.where(lane < 64, pltpu.roll(old_ids, 64, 1), jnp.where(lane < 96, pltpu.roll(new_ids, 64, 1), -5.0)),
    )
    square = (ROWS, ROWS)
    query = jnp.broadcast_to(column(own), square)
    old_key = jnp.broadcast_to(old_ids[0:1], square)
    mixed_key = jnp.broadcast_to(mixed[0:1], square)
    early = lax.broadcasted_iota(jnp.int32, square, 1) < 32
    zero = jnp.zeros(square, F32)
    low = jnp.full(square, LOW, F32)
    clean_bias = [
        jnp.where(old_key <= query, zero, low),
        jnp.where(early, jnp.where(mixed_key <= query, zero, low), low),
    ]
    noisy_bias = [
        jnp.where(old_key < query, zero, low),
        jnp.where(early, jnp.where(mixed_key < query, zero, low), jnp.where(mixed_key == query, zero, low)),
    ]
    bias = jnp.concatenate([jnp.concatenate(clean_bias, axis=1), jnp.concatenate(noisy_bias, axis=1)], axis=0)

    def rim_mask(parts):
        return [jnp.where(bias[:, j * ROWS : (j + 1) * ROWS] < -1.0, LOW, part) for j, part in enumerate(parts)]

    spots = ((0, 3), (1, 3), (3, 0), (3, 1), (3, 3))
    pieces = [
        (lambda: k_rim, lambda: v_rim, rim_mask, None),
        spots_piece((me, y, x, z), k_refs, v_refs, spots),
    ]
    pipeline(q_ref, pieces, state_in, state, None)


def third_kernel(*refs):
    q_ref, k_ref, v_refs = refs[0], refs[1], refs[2:5]
    where = place()
    near = (0, 1, 3)
    piece = spots_piece(where, {2: k_ref}, dict(zip(near, v_refs)), [(2, dx) for dx in near])
    pipeline(q_ref, [piece], refs[5:8], refs[8:11], None)


def last_kernel(*refs):
    q_ref, k_refs, v_ref = refs[0], refs[1:5], refs[5]
    state_in = refs[6:9]
    clean_ref, noisy_ref = refs[9:11]
    state = refs[11:]
    piece = spots_piece(place(), dict(enumerate(k_refs)), {2: v_ref}, [(dy, 2) for dy in range(4)])

    def finish(h, accum, total):
        lanes = slice(h * HEAD, (h + 1) * HEAD)
        result = (accum / jnp.sum(total, axis=1, keepdims=True)).astype(BF16)
        clean_ref[:, lanes] = result[:ROWS]
        noisy_ref[:, lanes] = result[ROWS:]

    pipeline(q_ref, [piece], state_in, state, finish)


def shards(hidden, block_ids, decode_order, step_cut, mask_embed, q_weight, k_weight, v_weight):
    ids = block_ids.reshape(1, ROWS)
    order = decode_order.reshape(1, ROWS)
    cuts = step_cut.reshape(1, -1)
    moved = [lax.ppermute(hidden, "kv", kv_pairs(d, 0)) for d in (1, 2, 3)]
    own, wk, wv, code, pad = call(
        prep_kernel,
        [
            (hidden.shape, BF16),
            (k_weight.shape, BF16),
            (v_weight.shape, BF16),
            ((PAD, ROWS), BF16),
            ((PAD, 8 * WIDTH), BF16),
        ],
        [held(a) for a in (hidden, k_weight, v_weight, ids, order, mask_embed.reshape(1, -1))],
        (1 << 20, 4 << 20),
        [
            pltpu.VMEM(ids.shape, jnp.int32),
            pltpu.VMEM(ids.shape, jnp.int32),
            pltpu.VMEM((1, 8 * WIDTH), BF16),
            pltpu.SemaphoreType.DMA((6,)),
        ],
        pl.ANY,
    )
    pieces = []
    for piece in (own, *moved):
        piece, _ = lax.optimization_barrier((piece, pad))
        pieces += [piece, lax.ppermute(piece, "kv", kv_pairs(0, 1))]
    x, kv, mask_kv = call(
        kv_kernel,
        [
            ((ROWS + PAD, 8 * WIDTH), BF16),
            ((ROWS + PAD, 2 * HEAD), BF16),
            ((PAD, 2 * HEAD), BF16),
        ],
        [*pieces, pad, wk, wv, code],
        (1 << 29, 3 << 20),
    )
    pair = lax.ppermute(kv, "ctx", ctx_pairs(0, 0, 1))
    k, v = call(
        pair_kernel,
        [((2 * ROWS + PAD, HEAD), BF16), ((2 * ROWS, HEAD), BF16)],
        [kv, pair],
        (1 << 10, 1 << 18),
    )
    ks = [lax.ppermute(k, "ctx", ctx_pairs(0, d, 0)) for d in (1, 2, 3)]
    vs = [lax.ppermute(v, "ctx", ctx_pairs(d, 0, 0)) for d in (1, 2, 3)]
    ks, vs = call(
        stack_kernel,
        [((8 * ROWS + PAD, HEAD), BF16), ((8 * ROWS, HEAD), BF16)],
        [k, *ks, v, *vs],
        (1 << 10, 1 << 20),
    )
    q, flag, own_cut = call(
        q_kernel,
        [((GROUP, 2 * ROWS, HEAD), BF16), ((ROWS, HEAD), F32), ((ROWS, HEAD), F32)],
        [x, q_weight, code, cuts],
        (1 << 30, 5 << 20),
    )
    near = call(
        near_kernel,
        [((GROUP, 2 * ROWS, HEAD), F32)] * 3,
        [q, kv, mask_kv, flag, code],
        (1 << 30, 2 << 20),
    )
    all_k = [ks] + [lax.ppermute(ks, "ctx", ctx_pairs(d, 0, 0)) for d in (1, 2, 3)]
    all_v = [vs] + [lax.ppermute(vs, "ctx", ctx_pairs(0, d, 0)) for d in (1, 2, 3)]
    state = [((GROUP, 2 * ROWS, HEAD), F32)] * 3
    first = call(
        first_kernel,
        state,
        [q, *all_k[:2], *all_v[:2], *near],
        (1 << 30, 2 << 20),
    )
    far = call(
        far_kernel,
        state,
        [q, *[all_k[d] for d in (0, 1, 3)], *[all_v[d] for d in (0, 1, 3)], *first, code, own_cut, mask_kv],
        (1 << 31, 4 << 20),
    )
    third = call(
        third_kernel,
        state,
        [q, all_k[2], *[all_v[d] for d in (0, 1, 3)], *far],
        (1 << 30, 2 << 20),
    )
    return tuple(
        call(
            last_kernel,
            [((ROWS, GROUP * HEAD), BF16)] * 2,
            [q, *all_k, all_v[2], *third],
            (1 << 31, 4 << 20),
            [pltpu.VMEM((GROUP, 2 * ROWS, HEAD), F32)] * 3,
        )
    )


def solution(mesh):
    return jax.shard_map(
        shards,
        mesh=mesh,
        in_specs=(
            P("ctx", "kv"),
            P("ctx"),
            P("ctx"),
            P(),
            P(),
            P(None, "kv"),
            P(None, "kv"),
            P(None, "kv"),
        ),
        out_specs=(P("ctx", "kv"), P("ctx", "kv")),
        check_vma=False,
    )
```

```python
import math

import jax
import jax.numpy as jnp
from jax import lax
from jax.experimental import pallas as pl
from jax.experimental.pallas import tpu as pltpu
from jax.sharding import PartitionSpec as P

ROWS = 128
HEAD = 128
GROUP = 4
PAD = 16
WIDTH = 512
BLOCK = 32
LAST = 31
LOW = -1e30
FAR = 1e6
POWER = math.log2(math.e) / math.sqrt(HEAD)
LIMIT = 48 * 1024 * 1024
F32 = jnp.float32
BF16 = jnp.bfloat16


def ctx_pairs(dy, dx, dz):
    pairs = []
    for i in range(32):
        y, x, z = i // 8, (i // 2) % 4, i % 2
        pairs.append((i, ((y ^ dy) * 4 + (x ^ dx)) * 2 + (z ^ dz)))
    return pairs


def kv_pairs(dz, dc):
    pairs = []
    for i in range(8):
        z, c = i // 2, i % 2
        pairs.append((i, (z ^ dz) * 2 + (c ^ dc)))
    return pairs


def dot(a, b):
    return jnp.dot(a, b, preferred_element_type=F32)


def dot_t(a, b):
    return lax.dot_general(a, b, (((1,), (1,)), ((), ())), preferred_element_type=F32)


def call(kernel, outs, args, cost, scratch=(), space=pltpu.VMEM):
    spec = pl.BlockSpec(memory_space=pltpu.VMEM)
    return pl.pallas_call(
        kernel,
        out_shape=[jax.ShapeDtypeStruct(s, t) for s, t in outs],
        in_specs=[pl.BlockSpec(memory_space=space)] * len(args),
        out_specs=[spec] * len(outs),
        scratch_shapes=list(scratch),
        compiler_params=pltpu.CompilerParams(vmem_limit_bytes=LIMIT),
        cost_estimate=pl.CostEstimate(flops=cost[0], bytes_accessed=cost[1], transcendentals=0),
    )(*args)


def held(array):
    return pltpu.with_memory_space_constraint(array, pltpu.HBM)


def column(row):
    square = (ROWS, ROWS)
    same = lax.broadcasted_iota(jnp.int32, square, 0) == lax.broadcasted_iota(jnp.int32, square, 1)
    return jnp.sum(jnp.where(same, jnp.broadcast_to(row, square), 0.0), axis=1, keepdims=True)


def prep_kernel(*refs):
    hidden_hbm, wk_hbm, wv_hbm, ids_hbm, order_hbm, embed_hbm = refs[:6]
    own_ref, wk_ref, wv_ref, code_ref, pad_ref = refs[6:11]
    ids_ref, order_ref, embed_ref, sems = refs[11:]
    pairs = (
        (ids_hbm, ids_ref),
        (order_hbm, order_ref),
        (embed_hbm, embed_ref),
        (hidden_hbm, own_ref),
        (wk_hbm, wk_ref),
        (wv_hbm, wv_ref),
    )
    copies = [pltpu.make_async_copy(a, b, sems.at[i]) for i, (a, b) in enumerate(pairs)]
    for copy in copies:
        copy.start()
    for copy in copies:
        copy.wait()
    ids = jnp.broadcast_to(ids_ref[...].astype(F32), (PAD, ROWS))
    order = jnp.broadcast_to(order_ref[...].astype(F32), (PAD, ROWS))
    row = lax.broadcasted_iota(jnp.int32, (PAD, ROWS), 0)
    code_ref[...] = jnp.where(lax.rem(row, 2) == 0, ids, order).astype(BF16)
    pad_ref[...] = jnp.broadcast_to(embed_ref[...], pad_ref.shape)


def kv_kernel(*refs):
    pieces = refs[:8]
    pad_ref, wk_ref, wv_ref, code_ref = refs[8:12]
    x_ref, kv_ref, mkv_ref = refs[12:]
    me = lax.axis_index("kv")
    for dz in range(4):
        for dc in range(2):
            source = jnp.bitwise_xor(me, 2 * dz + dc)
            lanes = pl.ds(pl.multiple_of(source * WIDTH, WIDTH), WIDTH)
            x_ref[:ROWS, lanes] = pieces[2 * dz + dc][...]
    x_ref[ROWS:, :] = pad_ref[...]
    x = x_ref[...]
    for part, w_ref in enumerate((wk_ref, wv_ref)):
        lanes = slice(part * HEAD, (part + 1) * HEAD)
        product = dot(x, w_ref[...]).astype(BF16)
        kv_ref[:ROWS, lanes] = product[:ROWS]
        kv_ref[ROWS:, lanes] = code_ref[...]
        mkv_ref[:, lanes] = product[ROWS:]


def pair_kernel(own_ref, other_ref, k_ref, v_ref):
    for i, ref in enumerate((own_ref, other_ref)):
        rows = slice(i * ROWS, (i + 1) * ROWS)
        k_ref[rows, :] = ref[:ROWS, :HEAD]
        v_ref[rows, :] = ref[:ROWS, HEAD:]
    row = lax.broadcasted_iota(jnp.int32, (PAD, HEAD), 0)
    first = ref_tail(own_ref, ROWS)
    code = jnp.where(lax.rem(row, 4) < 2, first, ref_tail(other_ref, ROWS))
    k_ref[2 * ROWS :, :] = code.astype(BF16)


def ref_tail(ref, start):
    return ref[start:, :HEAD].astype(F32)


def stack_kernel(*refs):
    ks, vs = refs[:4], refs[4:8]
    k_ref, v_ref = refs[8:]
    row = lax.broadcasted_iota(jnp.int32, (PAD, HEAD), 0)
    code = jnp.zeros((PAD, HEAD), F32)
    for i in range(4):
        rows = slice(i * 2 * ROWS, (i + 1) * 2 * ROWS)
        k_ref[rows, :] = ks[i][: 2 * ROWS, :]
        v_ref[rows, :] = vs[i][...]
        code = jnp.where(row // 4 == i, ref_tail(ks[i], 2 * ROWS), code)
    k_ref[8 * ROWS :, :] = code.astype(BF16)


def q_kernel(x_ref, wq_ref, code_ref, cut_ref, q_ref, flag_ref, own_cut_ref):
    code = code_ref[...].astype(F32)
    ids = column(code[0:1])
    order = column(code[1:2])
    blocks = cut_ref.shape[1]
    spots = lax.broadcasted_iota(jnp.int32, (ROWS, blocks), 1).astype(F32)
    cuts = jnp.broadcast_to(cut_ref[...].astype(F32), (ROWS, blocks))
    cut = jnp.sum(jnp.where(spots == ids, cuts, 0.0), axis=1, keepdims=True)
    flag = jnp.broadcast_to(jnp.where(order >= cut, 1.0, 0.0), (ROWS, HEAD))
    flag_ref[...] = flag
    own_cut_ref[...] = jnp.broadcast_to(cut, (ROWS, HEAD))
    x = x_ref[...]
    for h in range(GROUP):
        product = dot(x, wq_ref[:, h * HEAD : (h + 1) * HEAD])
        clean = product[:ROWS]
        fixed = jnp.broadcast_to(product[ROWS : ROWS + 1], (ROWS, HEAD))
        q_ref[h, :ROWS, :] = clean.astype(BF16)
        q_ref[h, ROWS:, :] = jnp.where(flag > 0.5, fixed, clean).astype(BF16)


def near_kernel(q_ref, kv_ref, mkv_ref, flag_ref, code_ref, top_ref, total_ref, accum_ref):
    masked = flag_ref[...] > 0.5

    def both(lanes):
        clean = kv_ref[:ROWS, lanes]
        fixed = jnp.broadcast_to(mkv_ref[0:1, lanes].astype(F32), (ROWS, HEAD))
        return jnp.concatenate([clean, jnp.where(masked, fixed, clean.astype(F32)).astype(BF16)], axis=0)

    row = code_ref[...].astype(F32)[0:1]
    query = jnp.broadcast_to(column(row), (ROWS, ROWS))
    key = jnp.broadcast_to(row, (ROWS, ROWS))
    zero = jnp.zeros((ROWS, ROWS), F32)
    low = jnp.full((ROWS, ROWS), LOW, F32)
    clean_bias = jnp.concatenate([jnp.where(key <= query, zero, low), low], axis=1)
    noisy_bias = jnp.concatenate([jnp.where(key < query, zero, low), jnp.where(key == query, zero, low)], axis=1)
    bias = jnp.concatenate([clean_bias, noisy_bias], axis=0)
    keys = both(slice(0, HEAD))
    values = both(slice(HEAD, 2 * HEAD))
    for h in range(GROUP):
        scores = jnp.where(bias < -1.0, LOW, dot_t(q_ref[h], keys))
        top = jnp.max(scores, axis=1, keepdims=True)
        probs = jnp.exp2((scores - top) * POWER)
        top_ref[h] = jnp.broadcast_to(top, (2 * ROWS, HEAD))
        total_ref[h] = probs[:, :HEAD] + probs[:, HEAD:]
        accum_ref[h] = dot(probs.astype(BF16), values)


def place():
    me = lax.axis_index("ctx")
    return me, me // 8, lax.rem(me // 2, 4), lax.rem(me, 2)


def pipeline(q_ref, pieces, state_in, state, finish):
    top_ref, total_ref, accum_ref = state

    def scores_of(step):
        h, chunk, _, _ = step
        keys, _, mask, _ = pieces[chunk]
        scores = dot_t(q_ref[h], keys())
        parts = [scores[:, j : j + ROWS] for j in range(0, scores.shape[1], ROWS)]
        return mask(parts) if mask is not None else parts

    def absorb(step, parts):
        h, chunk, first, last = step
        _, values, _, seen = pieces[chunk]
        best = parts[0]
        for part in parts[1:]:
            best = jnp.maximum(best, part)
        best = jnp.max(best, axis=1, keepdims=True)
        if seen is not None:
            best = jnp.where(seen, best, LOW)
        source = state_in if first else state
        old = source[0][h]
        top = jnp.maximum(old, best)
        factor = jnp.exp2((old - top) * POWER)
        level = top if seen is None else jnp.where(seen, top, -LOW)
        probs = [jnp.exp2((part - level) * POWER) for part in parts]
        total = source[1][h] * factor
        for part in probs:
            total = total + part
        probs = jnp.concatenate([part.astype(BF16) for part in probs], axis=1)
        accum = source[2][h] * factor + dot(probs, values())
        if last and finish is not None:
            finish(h, accum, total)
        else:
            top_ref[h] = top
            total_ref[h] = total
            accum_ref[h] = accum

    order = [(h, i, i == 0, i == len(pieces) - 1) for i in range(len(pieces)) for h in range(GROUP)]
    parts = scores_of(order[0])
    for now, later in zip(order, order[1:] + [None]):
        following = None if later is None else scores_of(later)
        absorb(now, parts)
        parts = following


def blocks_of(ref, which):
    return jnp.concatenate([ref[i * 2 * ROWS : (i + 1) * 2 * ROWS, :] for i in which], axis=0)


def shard_mask(where, spots):
    me, y, x, z = where

    def mask(parts):
        kept = []
        for j, part in enumerate(parts):
            dy, dx = spots[j // 2]
            there = jnp.bitwise_xor(me, dy * 8 + dx * 2 + j % 2)
            kept.append(jnp.where(there < me - 1, part, LOW))
        return kept

    return mask


def spots_piece(where, k_of, v_of, spots):
    def keys():
        return jnp.concatenate([k_of[dy][dx * 2 * ROWS : (dx + 1) * 2 * ROWS, :] for dy, dx in spots], axis=0)

    def values():
        return jnp.concatenate([v_of[dx][dy * 2 * ROWS : (dy + 1) * 2 * ROWS, :] for dy, dx in spots], axis=0)

    return keys, values, shard_mask(where, spots), None


def first_kernel(*refs):
    q_ref = refs[0]
    k_of, v_of = dict(zip((0, 1), refs[1:3])), dict(zip((0, 1), refs[3:5]))
    piece = spots_piece(place(), k_of, v_of, ((0, 0), (0, 1), (1, 0), (1, 1)))
    pipeline(q_ref, [piece], refs[5:8], refs[8:11], None)


def far_kernel(*refs):
    q_ref = refs[0]
    k_refs = dict(zip((0, 1, 3), refs[1:4]))
    v_refs = dict(zip((0, 1, 3), refs[4:7]))
    state_in = refs[7:10]
    code_ref, own_cut_ref, mkv_ref = refs[10:13]
    state = refs[13:16]
    me, y, x, z = place()

    spots = ((0, 0), (0, 1), (0, 3), (1, 3), (3, 3))
    old_far = jnp.bitwise_xor(me, jnp.maximum(me - 1, 0)) // 2
    new_far = jnp.bitwise_xor(me, jnp.minimum(me + 1, LAST)) // 2

    def pick(far, of):
        chosen = of(*spots[0])
        for dy, dx in spots[1:]:
            chosen = jnp.where(far == dy * 4 + dx, of(dy, dx), chosen)
        return chosen

    def k_block(dy, dx):
        return k_refs[dy][(dx * 2 + 1) * ROWS : (dx * 2 + 2) * ROWS, :]

    def v_block(dy, dx):
        return v_refs[dx][(dy * 2 + 1) * ROWS : (dy * 2 + 2) * ROWS, :]

    k_old, v_old = pick(old_far, k_block), pick(old_far, v_block)
    k_new, v_new = pick(new_far, k_block), pick(new_far, v_block)
    k_new, v_new = k_new[:BLOCK], v_new[:BLOCK]

    own = code_ref[...].astype(F32)[0:1]
    tails = {dy: ref_tail(k_refs[dy], 8 * ROWS) for dy in (0, 1, 3)}

    def line(i):
        def row(dy, dx):
            return tails[dy][dx * 4 + 2 + i : dx * 4 + 3 + i]

        return pick(old_far, row), pick(new_far, row)

    old_ids, new_ids = line(0)
    old_order, new_order = line(1)
    old_ids = jnp.broadcast_to(jnp.where(me > 0, old_ids, FAR), (8, ROWS))
    new_ids = jnp.broadcast_to(jnp.where(me < LAST, new_ids, FAR), (8, ROWS))
    first_cut = own_cut_ref[0:1, :]
    last_cut = own_cut_ref[ROWS - 1 : ROWS, :]
    old_masked = column(jnp.where(old_order >= first_cut, 1.0, 0.0))[ROWS - BLOCK :]
    new_masked = column(jnp.where(new_order >= last_cut, 1.0, 0.0))[:BLOCK]

    def noisy(masked, clean, lanes):
        fixed = jnp.broadcast_to(mkv_ref[0:1, lanes].astype(F32), clean.shape)
        flag = jnp.broadcast_to(masked, clean.shape) > 0.5
        return jnp.where(flag, fixed, clean.astype(F32)).astype(BF16)

    def rim(old, new, lanes):
        parts = [old, new, noisy(old_masked, old[ROWS - BLOCK :], lanes), noisy(new_masked, new, lanes)]
        return jnp.concatenate(parts + [jnp.zeros((BLOCK, HEAD), BF16)], axis=0)

    k_rim = rim(k_old, k_new, slice(0, HEAD))
    v_rim = rim(v_old, v_new, slice(HEAD, 2 * HEAD))
    lane = lax.broadcasted_iota(jnp.int32, (8, ROWS), 1)
    mixed = jnp.where(
        lane < 32,
        new_ids,
        jnp.where(lane < 64, pltpu.roll(old_ids, 64, 1), jnp.where(lane < 96, pltpu.roll(new_ids, 64, 1), -5.0)),
    )
    square = (ROWS, ROWS)
    query = jnp.broadcast_to(column(own), square)
    old_key = jnp.broadcast_to(old_ids[0:1], square)
    mixed_key = jnp.broadcast_to(mixed[0:1], square)
    early = lax.broadcasted_iota(jnp.int32, square, 1) < 32
    zero = jnp.zeros(square, F32)
    low = jnp.full(square, LOW, F32)
    clean_bias = [
        jnp.where(old_key <= query, zero, low),
        jnp.where(early, jnp.where(mixed_key <= query, zero, low), low),
    ]
    noisy_bias = [
        jnp.where(old_key < query, zero, low),
        jnp.where(early, jnp.where(mixed_key < query, zero, low), jnp.where(mixed_key == query, zero, low)),
    ]
    bias = jnp.concatenate([jnp.concatenate(clean_bias, axis=1), jnp.concatenate(noisy_bias, axis=1)], axis=0)

    def rim_mask(parts):
        return [jnp.where(bias[:, j * ROWS : (j + 1) * ROWS] < -1.0, LOW, part) for j, part in enumerate(parts)]

    spots = ((0, 3), (1, 3), (3, 0), (3, 1), (3, 3))
    pieces = [
        (lambda: k_rim, lambda: v_rim, rim_mask, None),
        spots_piece((me, y, x, z), k_refs, v_refs, spots),
    ]
    pipeline(q_ref, pieces, state_in, state, None)


def third_kernel(*refs):
    q_ref, k_ref, v_refs = refs[0], refs[1], refs[2:5]
    where = place()
    near = (0, 1, 3)
    piece = spots_piece(where, {2: k_ref}, dict(zip(near, v_refs)), [(2, dx) for dx in near])
    pipeline(q_ref, [piece], refs[5:8], refs[8:11], None)


def last_kernel(*refs):
    q_ref, k_refs, v_ref = refs[0], refs[1:5], refs[5]
    state_in = refs[6:9]
    clean_ref, noisy_ref = refs[9:11]
    state = refs[11:]
    piece = spots_piece(place(), dict(enumerate(k_refs)), {2: v_ref}, [(dy, 2) for dy in range(4)])

    def finish(h, accum, total):
        lanes = slice(h * HEAD, (h + 1) * HEAD)
        result = (accum / jnp.sum(total, axis=1, keepdims=True)).astype(BF16)
        clean_ref[:, lanes] = result[:ROWS]
        noisy_ref[:, lanes] = result[ROWS:]

    pipeline(q_ref, [piece], state_in, state, finish)


def shards(hidden, block_ids, decode_order, step_cut, mask_embed, q_weight, k_weight, v_weight):
    ids = block_ids.reshape(1, ROWS)
    order = decode_order.reshape(1, ROWS)
    cuts = step_cut.reshape(1, -1)
    moved = [lax.ppermute(hidden, "kv", kv_pairs(d, 0)) for d in (1, 2, 3)]
    own, wk, wv, code, pad = call(
        prep_kernel,
        [
            (hidden.shape, BF16),
            (k_weight.shape, BF16),
            (v_weight.shape, BF16),
            ((PAD, ROWS), BF16),
            ((PAD, 8 * WIDTH), BF16),
        ],
        [held(a) for a in (hidden, k_weight, v_weight, ids, order, mask_embed.reshape(1, -1))],
        (1 << 20, 4 << 20),
        [
            pltpu.VMEM(ids.shape, jnp.int32),
            pltpu.VMEM(ids.shape, jnp.int32),
            pltpu.VMEM((1, 8 * WIDTH), BF16),
            pltpu.SemaphoreType.DMA((6,)),
        ],
        pl.ANY,
    )
    pieces = []
    for piece in (own, *moved):
        piece, _ = lax.optimization_barrier((piece, pad))
        pieces += [piece, lax.ppermute(piece, "kv", kv_pairs(0, 1))]
    x, kv, mask_kv = call(
        kv_kernel,
        [
            ((ROWS + PAD, 8 * WIDTH), BF16),
            ((ROWS + PAD, 2 * HEAD), BF16),
            ((PAD, 2 * HEAD), BF16),
        ],
        [*pieces, pad, wk, wv, code],
        (1 << 29, 3 << 20),
    )
    pair = lax.ppermute(kv, "ctx", ctx_pairs(0, 0, 1))
    k, v = call(
        pair_kernel,
        [((2 * ROWS + PAD, HEAD), BF16), ((2 * ROWS, HEAD), BF16)],
        [kv, pair],
        (1 << 10, 1 << 18),
    )
    ks = [lax.ppermute(k, "ctx", ctx_pairs(0, d, 0)) for d in (1, 2, 3)]
    vs = [lax.ppermute(v, "ctx", ctx_pairs(d, 0, 0)) for d in (1, 2, 3)]
    ks, vs = call(
        stack_kernel,
        [((8 * ROWS + PAD, HEAD), BF16), ((8 * ROWS, HEAD), BF16)],
        [k, *ks, v, *vs],
        (1 << 10, 1 << 20),
    )
    q, flag, own_cut = call(
        q_kernel,
        [((GROUP, 2 * ROWS, HEAD), BF16), ((ROWS, HEAD), F32), ((ROWS, HEAD), F32)],
        [x, q_weight, code, cuts],
        (1 << 30, 5 << 20),
    )
    near = call(
        near_kernel,
        [((GROUP, 2 * ROWS, HEAD), F32)] * 3,
        [q, kv, mask_kv, flag, code],
        (1 << 30, 2 << 20),
    )
    all_k = [ks] + [lax.ppermute(ks, "ctx", ctx_pairs(d, 0, 0)) for d in (1, 2, 3)]
    all_v = [vs] + [lax.ppermute(vs, "ctx", ctx_pairs(0, d, 0)) for d in (1, 2, 3)]
    state = [((GROUP, 2 * ROWS, HEAD), F32)] * 3
    first = call(
        first_kernel,
        state,
        [q, *all_k[:2], *all_v[:2], *near],
        (1 << 30, 2 << 20),
    )
    far = call(
        far_kernel,
        state,
        [q, *[all_k[d] for d in (0, 1, 3)], *[all_v[d] for d in (0, 1, 3)], *first, code, own_cut, mask_kv],
        (1 << 31, 4 << 20),
    )
    third = call(
        third_kernel,
        state,
        [q, all_k[2], *[all_v[d] for d in (0, 1, 3)], *far],
        (1 << 30, 2 << 20),
    )
    return tuple(
        call(
            last_kernel,
            [((ROWS, GROUP * HEAD), BF16)] * 2,
            [q, *all_k, all_v[2], *third],
            (1 << 31, 4 << 20),
            [pltpu.VMEM((GROUP, 2 * ROWS, HEAD), F32)] * 3,
        )
    )


def solution(mesh):
    return jax.shard_map(
        shards,
        mesh=mesh,
        in_specs=(
            P("ctx", "kv"),
            P("ctx"),
            P("ctx"),
            P(),
            P(),
            P(None, "kv"),
            P(None, "kv"),
            P(None, "kv"),
        ),
        out_specs=(P("ctx", "kv"), P("ctx", "kv")),
        check_vma=False,
    )
```

```python
import math

import jax
import jax.numpy as jnp
from jax import lax
from jax.experimental import pallas as pl
from jax.experimental.pallas import tpu as pltpu
from jax.sharding import PartitionSpec as P

ROWS = 128
HEAD = 128
GROUP = 4
PAD = 16
WIDTH = 512
BLOCK = 32
LAST = 31
LOW = -1e30
FAR = 1e6
POWER = math.log2(math.e) / math.sqrt(HEAD)
LIMIT = 48 * 1024 * 1024
F32 = jnp.float32
BF16 = jnp.bfloat16


def ctx_pairs(dy, dx, dz):
    pairs = []
    for i in range(32):
        y, x, z = i // 8, (i // 2) % 4, i % 2
        pairs.append((i, ((y ^ dy) * 4 + (x ^ dx)) * 2 + (z ^ dz)))
    return pairs


def kv_pairs(dz, dc):
    pairs = []
    for i in range(8):
        z, c = i // 2, i % 2
        pairs.append((i, (z ^ dz) * 2 + (c ^ dc)))
    return pairs


def dot(a, b):
    return jnp.dot(a, b, preferred_element_type=F32)


def dot_t(a, b):
    return lax.dot_general(a, b, (((1,), (1,)), ((), ())), preferred_element_type=F32)


def call(kernel, outs, args, cost, scratch=(), space=pltpu.VMEM):
    spec = pl.BlockSpec(memory_space=pltpu.VMEM)
    return pl.pallas_call(
        kernel,
        out_shape=[jax.ShapeDtypeStruct(s, t) for s, t in outs],
        in_specs=[pl.BlockSpec(memory_space=space)] * len(args),
        out_specs=[spec] * len(outs),
        scratch_shapes=list(scratch),
        compiler_params=pltpu.CompilerParams(vmem_limit_bytes=LIMIT),
        cost_estimate=pl.CostEstimate(flops=cost[0], bytes_accessed=cost[1], transcendentals=0),
    )(*args)


def held(array):
    return pltpu.with_memory_space_constraint(array, pltpu.HBM)


def column(row):
    square = (ROWS, ROWS)
    same = lax.broadcasted_iota(jnp.int32, square, 0) == lax.broadcasted_iota(jnp.int32, square, 1)
    return jnp.sum(jnp.where(same, jnp.broadcast_to(row, square), 0.0), axis=1, keepdims=True)


def prep_kernel(*refs):
    hidden_hbm, wk_hbm, wv_hbm, ids_hbm, order_hbm, embed_hbm = refs[:6]
    own_ref, wk_ref, wv_ref, code_ref, pad_ref = refs[6:11]
    ids_ref, order_ref, embed_ref, sems = refs[11:]
    pairs = (
        (ids_hbm, ids_ref),
        (order_hbm, order_ref),
        (embed_hbm, embed_ref),
        (hidden_hbm, own_ref),
        (wk_hbm, wk_ref),
        (wv_hbm, wv_ref),
    )
    copies = [pltpu.make_async_copy(a, b, sems.at[i]) for i, (a, b) in enumerate(pairs)]
    for copy in copies:
        copy.start()
    for copy in copies:
        copy.wait()
    ids = jnp.broadcast_to(ids_ref[...].astype(F32), (PAD, ROWS))
    order = jnp.broadcast_to(order_ref[...].astype(F32), (PAD, ROWS))
    row = lax.broadcasted_iota(jnp.int32, (PAD, ROWS), 0)
    code_ref[...] = jnp.where(lax.rem(row, 2) == 0, ids, order).astype(BF16)
    pad_ref[...] = jnp.broadcast_to(embed_ref[...], pad_ref.shape)


def kv_kernel(*refs):
    pieces = refs[:8]
    pad_ref, wk_ref, wv_ref, code_ref = refs[8:12]
    x_ref, kv_ref, mkv_ref = refs[12:]
    me = lax.axis_index("kv")
    for dz in range(4):
        for dc in range(2):
            source = jnp.bitwise_xor(me, 2 * dz + dc)
            lanes = pl.ds(pl.multiple_of(source * WIDTH, WIDTH), WIDTH)
            x_ref[:ROWS, lanes] = pieces[2 * dz + dc][...]
    x_ref[ROWS:, :] = pad_ref[...]
    x = x_ref[...]
    for part, w_ref in enumerate((wk_ref, wv_ref)):
        lanes = slice(part * HEAD, (part + 1) * HEAD)
        product = dot(x, w_ref[...]).astype(BF16)
        kv_ref[:ROWS, lanes] = product[:ROWS]
        kv_ref[ROWS:, lanes] = code_ref[...]
        mkv_ref[:, lanes] = product[ROWS:]


def pair_kernel(own_ref, other_ref, k_ref, v_ref):
    for i, ref in enumerate((own_ref, other_ref)):
        rows = slice(i * ROWS, (i + 1) * ROWS)
        k_ref[rows, :] = ref[:ROWS, :HEAD]
        v_ref[rows, :] = ref[:ROWS, HEAD:]
    row = lax.broadcasted_iota(jnp.int32, (PAD, HEAD), 0)
    first = ref_tail(own_ref, ROWS)
    code = jnp.where(lax.rem(row, 4) < 2, first, ref_tail(other_ref, ROWS))
    k_ref[2 * ROWS :, :] = code.astype(BF16)


def ref_tail(ref, start):
    return ref[start:, :HEAD].astype(F32)


def stack_kernel(*refs):
    ks, vs = refs[:4], refs[4:8]
    k_ref, v_ref = refs[8:]
    row = lax.broadcasted_iota(jnp.int32, (PAD, HEAD), 0)
    code = jnp.zeros((PAD, HEAD), F32)
    for i in range(4):
        rows = slice(i * 2 * ROWS, (i + 1) * 2 * ROWS)
        k_ref[rows, :] = ks[i][: 2 * ROWS, :]
        v_ref[rows, :] = vs[i][...]
        code = jnp.where(row // 4 == i, ref_tail(ks[i], 2 * ROWS), code)
    k_ref[8 * ROWS :, :] = code.astype(BF16)


def q_kernel(x_ref, wq_ref, code_ref, cut_ref, q_ref, flag_ref, own_cut_ref):
    code = code_ref[...].astype(F32)
    ids = column(code[0:1])
    order = column(code[1:2])
    blocks = cut_ref.shape[1]
    spots = lax.broadcasted_iota(jnp.int32, (ROWS, blocks), 1).astype(F32)
    cuts = jnp.broadcast_to(cut_ref[...].astype(F32), (ROWS, blocks))
    cut = jnp.sum(jnp.where(spots == ids, cuts, 0.0), axis=1, keepdims=True)
    flag = jnp.broadcast_to(jnp.where(order >= cut, 1.0, 0.0), (ROWS, HEAD))
    flag_ref[...] = flag
    own_cut_ref[...] = jnp.broadcast_to(cut, (ROWS, HEAD))
    x = x_ref[...]
    for h in range(GROUP):
        product = dot(x, wq_ref[:, h * HEAD : (h + 1) * HEAD])
        clean = product[:ROWS]
        fixed = jnp.broadcast_to(product[ROWS : ROWS + 1], (ROWS, HEAD))
        q_ref[h, :ROWS, :] = clean.astype(BF16)
        q_ref[h, ROWS:, :] = jnp.where(flag > 0.5, fixed, clean).astype(BF16)


def near_kernel(q_ref, kv_ref, mkv_ref, flag_ref, code_ref, top_ref, total_ref, accum_ref):
    masked = flag_ref[...] > 0.5

    def both(lanes):
        clean = kv_ref[:ROWS, lanes]
        fixed = jnp.broadcast_to(mkv_ref[0:1, lanes].astype(F32), (ROWS, HEAD))
        return jnp.concatenate([clean, jnp.where(masked, fixed, clean.astype(F32)).astype(BF16)], axis=0)

    row = code_ref[...].astype(F32)[0:1]
    query = jnp.broadcast_to(column(row), (ROWS, ROWS))
    key = jnp.broadcast_to(row, (ROWS, ROWS))
    zero = jnp.zeros((ROWS, ROWS), F32)
    low = jnp.full((ROWS, ROWS), LOW, F32)
    clean_bias = jnp.concatenate([jnp.where(key <= query, zero, low), low], axis=1)
    noisy_bias = jnp.concatenate([jnp.where(key < query, zero, low), jnp.where(key == query, zero, low)], axis=1)
    bias = jnp.concatenate([clean_bias, noisy_bias], axis=0)
    keys = both(slice(0, HEAD))
    values = both(slice(HEAD, 2 * HEAD))
    for h in range(GROUP):
        scores = jnp.where(bias < -1.0, LOW, dot_t(q_ref[h], keys))
        top = jnp.max(scores, axis=1, keepdims=True)
        probs = jnp.exp2((scores - top) * POWER)
        top_ref[h] = jnp.broadcast_to(top, (2 * ROWS, HEAD))
        total_ref[h] = jnp.broadcast_to(jnp.sum(probs, axis=1, keepdims=True), (2 * ROWS, HEAD))
        accum_ref[h] = dot(probs.astype(BF16), values)


def place():
    me = lax.axis_index("ctx")
    return me, me // 8, lax.rem(me // 2, 4), lax.rem(me, 2)


def pipeline(q_ref, pieces, state_in, state, finish):
    top_ref, total_ref, accum_ref = state

    def scores_of(step):
        h, chunk, _, _ = step
        keys, _, mask, _ = pieces[chunk]
        scores = dot_t(q_ref[h], keys())
        parts = [scores[:, j : j + ROWS] for j in range(0, scores.shape[1], ROWS)]
        return mask(parts) if mask is not None else parts

    def absorb(step, parts):
        h, chunk, first, last = step
        _, values, _, seen = pieces[chunk]
        best = parts[0]
        for part in parts[1:]:
            best = jnp.maximum(best, part)
        best = jnp.max(best, axis=1, keepdims=True)
        if seen is not None:
            best = jnp.where(seen, best, LOW)
        source = state_in if first else state
        old = source[0][h]
        top = jnp.maximum(old, best)
        factor = jnp.exp2((old - top) * POWER)
        level = top if seen is None else jnp.where(seen, top, -LOW)
        probs = [jnp.exp2((part - level) * POWER) for part in parts]
        probs = jnp.concatenate([part.astype(BF16) for part in probs], axis=1)
        right = values()
        product = dot(probs, jnp.concatenate([right, jnp.ones(right.shape, BF16)], axis=1))
        total = source[1][h] * factor + product[:, HEAD:]
        accum = source[2][h] * factor + product[:, :HEAD]
        if last and finish is not None:
            finish(h, accum, total)
        else:
            top_ref[h] = top
            total_ref[h] = total
            accum_ref[h] = accum

    order = [(h, i, i == 0, i == len(pieces) - 1) for i in range(len(pieces)) for h in range(GROUP)]
    parts = scores_of(order[0])
    for now, later in zip(order, order[1:] + [None]):
        following = None if later is None else scores_of(later)
        absorb(now, parts)
        parts = following


def blocks_of(ref, which):
    return jnp.concatenate([ref[i * 2 * ROWS : (i + 1) * 2 * ROWS, :] for i in which], axis=0)


def shard_mask(where, spots):
    me, y, x, z = where

    def mask(parts):
        kept = []
        for j, part in enumerate(parts):
            dy, dx = spots[j // 2]
            there = jnp.bitwise_xor(me, dy * 8 + dx * 2 + j % 2)
            kept.append(jnp.where(there < me - 1, part, LOW))
        return kept

    return mask


def spots_piece(where, k_of, v_of, spots):
    def keys():
        return jnp.concatenate([k_of[dy][dx * 2 * ROWS : (dx + 1) * 2 * ROWS, :] for dy, dx in spots], axis=0)

    def values():
        return jnp.concatenate([v_of[dx][dy * 2 * ROWS : (dy + 1) * 2 * ROWS, :] for dy, dx in spots], axis=0)

    return keys, values, shard_mask(where, spots), None


def first_kernel(*refs):
    q_ref = refs[0]
    k_of, v_of = dict(zip((0, 1), refs[1:3])), dict(zip((0, 1), refs[3:5]))
    piece = spots_piece(place(), k_of, v_of, ((0, 1), (1, 0), (1, 1)))
    pipeline(q_ref, [piece], refs[5:8], refs[8:11], None)


def far_kernel(*refs):
    q_ref = refs[0]
    k_refs = dict(zip((0, 1, 3), refs[1:4]))
    v_refs = dict(zip((0, 1, 3), refs[4:7]))
    state_in = refs[7:10]
    code_ref, own_cut_ref, mkv_ref = refs[10:13]
    state = refs[13:16]
    me, y, x, z = place()

    spots = ((0, 0), (0, 1), (0, 3), (1, 3), (3, 3))
    old_far = jnp.bitwise_xor(me, jnp.maximum(me - 1, 0)) // 2
    new_far = jnp.bitwise_xor(me, jnp.minimum(me + 1, LAST)) // 2

    def pick(far, of):
        chosen = of(*spots[0])
        for dy, dx in spots[1:]:
            chosen = jnp.where(far == dy * 4 + dx, of(dy, dx), chosen)
        return chosen

    def k_block(dy, dx):
        return k_refs[dy][(dx * 2 + 1) * ROWS : (dx * 2 + 2) * ROWS, :]

    def v_block(dy, dx):
        return v_refs[dx][(dy * 2 + 1) * ROWS : (dy * 2 + 2) * ROWS, :]

    k_old, v_old = pick(old_far, k_block), pick(old_far, v_block)
    k_new, v_new = pick(new_far, k_block), pick(new_far, v_block)
    k_new, v_new = k_new[:BLOCK], v_new[:BLOCK]

    own = code_ref[...].astype(F32)[0:1]
    tails = {dy: ref_tail(k_refs[dy], 8 * ROWS) for dy in (0, 1, 3)}

    def line(i):
        def row(dy, dx):
            return tails[dy][dx * 4 + 2 + i : dx * 4 + 3 + i]

        return pick(old_far, row), pick(new_far, row)

    old_ids, new_ids = line(0)
    old_order, new_order = line(1)
    old_ids = jnp.broadcast_to(jnp.where(me > 0, old_ids, FAR), (8, ROWS))
    new_ids = jnp.broadcast_to(jnp.where(me < LAST, new_ids, FAR), (8, ROWS))
    first_cut = own_cut_ref[0:1, :]
    last_cut = own_cut_ref[ROWS - 1 : ROWS, :]
    old_masked = column(jnp.where(old_order >= first_cut, 1.0, 0.0))[ROWS - BLOCK :]
    new_masked = column(jnp.where(new_order >= last_cut, 1.0, 0.0))[:BLOCK]

    def noisy(masked, clean, lanes):
        fixed = jnp.broadcast_to(mkv_ref[0:1, lanes].astype(F32), clean.shape)
        flag = jnp.broadcast_to(masked, clean.shape) > 0.5
        return jnp.where(flag, fixed, clean.astype(F32)).astype(BF16)

    def rim(old, new, lanes):
        parts = [old, new, noisy(old_masked, old[ROWS - BLOCK :], lanes), noisy(new_masked, new, lanes)]
        return jnp.concatenate(parts + [jnp.zeros((BLOCK, HEAD), BF16)], axis=0)

    k_rim = rim(k_old, k_new, slice(0, HEAD))
    v_rim = rim(v_old, v_new, slice(HEAD, 2 * HEAD))
    lane = lax.broadcasted_iota(jnp.int32, (8, ROWS), 1)
    mixed = jnp.where(
        lane < 32,
        new_ids,
        jnp.where(lane < 64, pltpu.roll(old_ids, 64, 1), jnp.where(lane < 96, pltpu.roll(new_ids, 64, 1), -5.0)),
    )
    square = (ROWS, ROWS)
    query = jnp.broadcast_to(column(own), square)
    old_key = jnp.broadcast_to(old_ids[0:1], square)
    mixed_key = jnp.broadcast_to(mixed[0:1], square)
    early = lax.broadcasted_iota(jnp.int32, square, 1) < 32
    zero = jnp.zeros(square, F32)
    low = jnp.full(square, LOW, F32)
    clean_bias = [
        jnp.where(old_key <= query, zero, low),
        jnp.where(early, jnp.where(mixed_key <= query, zero, low), low),
    ]
    noisy_bias = [
        jnp.where(old_key < query, zero, low),
        jnp.where(early, jnp.where(mixed_key < query, zero, low), jnp.where(mixed_key == query, zero, low)),
    ]
    bias = jnp.concatenate([jnp.concatenate(clean_bias, axis=1), jnp.concatenate(noisy_bias, axis=1)], axis=0)

    def rim_mask(parts):
        return [jnp.where(bias[:, j * ROWS : (j + 1) * ROWS] < -1.0, LOW, part) for j, part in enumerate(parts)]

    spots = ((0, 3), (1, 3), (3, 0), (3, 1), (3, 3))
    pieces = [
        (lambda: k_rim, lambda: v_rim, rim_mask, None),
        spots_piece((me, y, x, z), k_refs, v_refs, spots),
    ]
    pipeline(q_ref, pieces, state_in, state, None)


def third_kernel(*refs):
    q_ref, k_ref, v_refs = refs[0], refs[1], refs[2:5]
    where = place()
    near = (0, 1, 3)
    keys, values, _, _ = spots_piece(where, {2: k_ref}, dict(zip(near, v_refs)), [(2, dx) for dx in near])
    piece = (keys, values, None, where[1] >= 2)
    pipeline(q_ref, [piece], refs[5:8], refs[8:11], None)


def last_kernel(*refs):
    q_ref, k_refs, v_ref = refs[0], refs[1:5], refs[5]
    state_in = refs[6:9]
    clean_ref, noisy_ref = refs[9:11]
    state = refs[11:]
    piece = spots_piece(place(), dict(enumerate(k_refs)), {2: v_ref}, [(dy, 2) for dy in range(4)])

    def finish(h, accum, total):
        lanes = slice(h * HEAD, (h + 1) * HEAD)
        result = (accum / total).astype(BF16)
        clean_ref[:, lanes] = result[:ROWS]
        noisy_ref[:, lanes] = result[ROWS:]

    pipeline(q_ref, [piece], state_in, state, finish)


def shards(hidden, block_ids, decode_order, step_cut, mask_embed, q_weight, k_weight, v_weight):
    ids = block_ids.reshape(1, ROWS)
    order = decode_order.reshape(1, ROWS)
    cuts = step_cut.reshape(1, -1)
    moved = [lax.ppermute(hidden, "kv", kv_pairs(d, 0)) for d in (1, 2, 3)]
    own, wk, wv, code, pad = call(
        prep_kernel,
        [
            (hidden.shape, BF16),
            (k_weight.shape, BF16),
            (v_weight.shape, BF16),
            ((PAD, ROWS), BF16),
            ((PAD, 8 * WIDTH), BF16),
        ],
        [held(a) for a in (hidden, k_weight, v_weight, ids, order, mask_embed.reshape(1, -1))],
        (1 << 20, 4 << 20),
        [
            pltpu.VMEM(ids.shape, jnp.int32),
            pltpu.VMEM(ids.shape, jnp.int32),
            pltpu.VMEM((1, 8 * WIDTH), BF16),
            pltpu.SemaphoreType.DMA((6,)),
        ],
        pl.ANY,
    )
    pieces = []
    for piece in (own, *moved):
        piece, _ = lax.optimization_barrier((piece, pad))
        pieces += [piece, lax.ppermute(piece, "kv", kv_pairs(0, 1))]
    x, kv, mask_kv = call(
        kv_kernel,
        [
            ((ROWS + PAD, 8 * WIDTH), BF16),
            ((ROWS + PAD, 2 * HEAD), BF16),
            ((PAD, 2 * HEAD), BF16),
        ],
        [*pieces, pad, wk, wv, code],
        (1 << 29, 3 << 20),
    )
    pair = lax.ppermute(kv, "ctx", ctx_pairs(0, 0, 1))
    k, v = call(
        pair_kernel,
        [((2 * ROWS + PAD, HEAD), BF16), ((2 * ROWS, HEAD), BF16)],
        [kv, pair],
        (1 << 10, 1 << 18),
    )
    ks = [lax.ppermute(k, "ctx", ctx_pairs(0, d, 0)) for d in (1, 2, 3)]
    vs = [lax.ppermute(v, "ctx", ctx_pairs(d, 0, 0)) for d in (1, 2, 3)]
    ks, vs = call(
        stack_kernel,
        [((8 * ROWS + PAD, HEAD), BF16), ((8 * ROWS, HEAD), BF16)],
        [k, *ks, v, *vs],
        (1 << 10, 1 << 20),
    )
    q, flag, own_cut = call(
        q_kernel,
        [((GROUP, 2 * ROWS, HEAD), BF16), ((ROWS, HEAD), F32), ((ROWS, HEAD), F32)],
        [x, q_weight, code, cuts],
        (1 << 30, 5 << 20),
    )
    near = call(
        near_kernel,
        [((GROUP, 2 * ROWS, HEAD), F32)] * 3,
        [q, kv, mask_kv, flag, code],
        (1 << 30, 2 << 20),
    )
    all_k = [ks] + [lax.ppermute(ks, "ctx", ctx_pairs(d, 0, 0)) for d in (1, 2, 3)]
    all_v = [vs] + [lax.ppermute(vs, "ctx", ctx_pairs(0, d, 0)) for d in (1, 2, 3)]
    state = [((GROUP, 2 * ROWS, HEAD), F32)] * 3
    first = call(
        first_kernel,
        state,
        [q, *all_k[:2], *all_v[:2], *near],
        (1 << 30, 2 << 20),
    )
    far = call(
        far_kernel,
        state,
        [q, *[all_k[d] for d in (0, 1, 3)], *[all_v[d] for d in (0, 1, 3)], *first, code, own_cut, mask_kv],
        (1 << 31, 4 << 20),
    )
    third = call(
        third_kernel,
        state,
        [q, all_k[2], *[all_v[d] for d in (0, 1, 3)], *far],
        (1 << 30, 2 << 20),
    )
    return tuple(
        call(
            last_kernel,
            [((ROWS, GROUP * HEAD), BF16)] * 2,
            [q, *all_k, all_v[2], *third],
            (1 << 31, 4 << 20),
            [pltpu.VMEM((GROUP, 2 * ROWS, HEAD), F32)] * 3,
        )
    )


def solution(mesh):
    return jax.shard_map(
        shards,
        mesh=mesh,
        in_specs=(
            P("ctx", "kv"),
            P("ctx"),
            P("ctx"),
            P(),
            P(),
            P(None, "kv"),
            P(None, "kv"),
            P(None, "kv"),
        ),
        out_specs=(P("ctx", "kv"), P("ctx", "kv")),
        check_vma=False,
    )
```

```python
import math

import jax
import jax.numpy as jnp
from jax import lax
from jax.experimental import pallas as pl
from jax.experimental.pallas import tpu as pltpu
from jax.sharding import PartitionSpec as P

ROWS = 128
HEAD = 128
GROUP = 4
PAD = 16
WIDTH = 512
BLOCK = 32
LAST = 31
LOW = -1e30
FAR = 1e6
POWER = math.log2(math.e) / math.sqrt(HEAD)
LIMIT = 48 * 1024 * 1024
F32 = jnp.float32
BF16 = jnp.bfloat16


def ctx_pairs(dy, dx, dz):
    pairs = []
    for i in range(32):
        y, x, z = i // 8, (i // 2) % 4, i % 2
        pairs.append((i, ((y ^ dy) * 4 + (x ^ dx)) * 2 + (z ^ dz)))
    return pairs


def kv_pairs(dz, dc):
    pairs = []
    for i in range(8):
        z, c = i // 2, i % 2
        pairs.append((i, (z ^ dz) * 2 + (c ^ dc)))
    return pairs


def dot(a, b):
    return jnp.dot(a, b, preferred_element_type=F32)


def dot_t(a, b):
    return lax.dot_general(a, b, (((1,), (1,)), ((), ())), preferred_element_type=F32)


def call(kernel, outs, args, cost, scratch=(), space=pltpu.VMEM):
    spec = pl.BlockSpec(memory_space=pltpu.VMEM)
    return pl.pallas_call(
        kernel,
        out_shape=[jax.ShapeDtypeStruct(s, t) for s, t in outs],
        in_specs=[pl.BlockSpec(memory_space=space)] * len(args),
        out_specs=[spec] * len(outs),
        scratch_shapes=list(scratch),
        compiler_params=pltpu.CompilerParams(vmem_limit_bytes=LIMIT),
        cost_estimate=pl.CostEstimate(flops=cost[0], bytes_accessed=cost[1], transcendentals=0),
    )(*args)


def held(array):
    return pltpu.with_memory_space_constraint(array, pltpu.HBM)


def column(row):
    square = (ROWS, ROWS)
    same = lax.broadcasted_iota(jnp.int32, square, 0) == lax.broadcasted_iota(jnp.int32, square, 1)
    return jnp.sum(jnp.where(same, jnp.broadcast_to(row, square), 0.0), axis=1, keepdims=True)


def prep_kernel(*refs):
    hidden_hbm, wk_hbm, wv_hbm, ids_hbm, order_hbm, embed_hbm = refs[:6]
    own_ref, wk_ref, wv_ref, code_ref, pad_ref = refs[6:11]
    ids_ref, order_ref, embed_ref, sems = refs[11:]
    pairs = (
        (ids_hbm, ids_ref),
        (order_hbm, order_ref),
        (embed_hbm, embed_ref),
        (hidden_hbm, own_ref),
        (wk_hbm, wk_ref),
        (wv_hbm, wv_ref),
    )
    copies = [pltpu.make_async_copy(a, b, sems.at[i]) for i, (a, b) in enumerate(pairs)]
    for copy in copies:
        copy.start()
    for copy in copies:
        copy.wait()
    ids = jnp.broadcast_to(ids_ref[...].astype(F32), (PAD, ROWS))
    order = jnp.broadcast_to(order_ref[...].astype(F32), (PAD, ROWS))
    row = lax.broadcasted_iota(jnp.int32, (PAD, ROWS), 0)
    code_ref[...] = jnp.where(lax.rem(row, 2) == 0, ids, order).astype(BF16)
    pad_ref[...] = jnp.broadcast_to(embed_ref[...], pad_ref.shape)


def kv_kernel(*refs):
    pieces = refs[:8]
    pad_ref, wk_ref, wv_ref, code_ref = refs[8:12]
    x_ref, kv_ref, mkv_ref = refs[12:]
    me = lax.axis_index("kv")
    for dz in range(4):
        for dc in range(2):
            source = jnp.bitwise_xor(me, 2 * dz + dc)
            lanes = pl.ds(pl.multiple_of(source * WIDTH, WIDTH), WIDTH)
            x_ref[:ROWS, lanes] = pieces[2 * dz + dc][...]
    x_ref[ROWS:, :] = pad_ref[...]
    x = x_ref[...]
    for part, w_ref in enumerate((wk_ref, wv_ref)):
        lanes = slice(part * HEAD, (part + 1) * HEAD)
        product = dot(x, w_ref[...]).astype(BF16)
        kv_ref[:ROWS, lanes] = product[:ROWS]
        kv_ref[ROWS:, lanes] = code_ref[...]
        mkv_ref[:, lanes] = product[ROWS:]


def pair_kernel(own_ref, other_ref, k_ref, v_ref):
    for i, ref in enumerate((own_ref, other_ref)):
        rows = slice(i * ROWS, (i + 1) * ROWS)
        k_ref[rows, :] = ref[:ROWS, :HEAD]
        v_ref[rows, :] = ref[:ROWS, HEAD:]
    row = lax.broadcasted_iota(jnp.int32, (PAD, HEAD), 0)
    first = ref_tail(own_ref, ROWS)
    code = jnp.where(lax.rem(row, 4) < 2, first, ref_tail(other_ref, ROWS))
    k_ref[2 * ROWS :, :] = code.astype(BF16)


def ref_tail(ref, start):
    return ref[start:, :HEAD].astype(F32)


def stack_kernel(*refs):
    ks, vs = refs[:4], refs[4:8]
    k_ref, v_ref = refs[8:]
    row = lax.broadcasted_iota(jnp.int32, (PAD, HEAD), 0)
    code = jnp.zeros((PAD, HEAD), F32)
    for i in range(4):
        rows = slice(i * 2 * ROWS, (i + 1) * 2 * ROWS)
        k_ref[rows, :] = ks[i][: 2 * ROWS, :]
        v_ref[rows, :] = vs[i][...]
        code = jnp.where(row // 4 == i, ref_tail(ks[i], 2 * ROWS), code)
    k_ref[8 * ROWS :, :] = code.astype(BF16)


def q_kernel(x_ref, wq_ref, code_ref, cut_ref, q_ref, flag_ref, own_cut_ref):
    code = code_ref[...].astype(F32)
    ids = column(code[0:1])
    order = column(code[1:2])
    blocks = cut_ref.shape[1]
    spots = lax.broadcasted_iota(jnp.int32, (ROWS, blocks), 1).astype(F32)
    cuts = jnp.broadcast_to(cut_ref[...].astype(F32), (ROWS, blocks))
    cut = jnp.sum(jnp.where(spots == ids, cuts, 0.0), axis=1, keepdims=True)
    flag = jnp.broadcast_to(jnp.where(order >= cut, 1.0, 0.0), (ROWS, HEAD))
    flag_ref[...] = flag
    own_cut_ref[...] = jnp.broadcast_to(cut, (ROWS, HEAD))
    x = x_ref[...]
    for h in range(GROUP):
        product = dot(x, wq_ref[:, h * HEAD : (h + 1) * HEAD])
        clean = product[:ROWS]
        fixed = jnp.broadcast_to(product[ROWS : ROWS + 1], (ROWS, HEAD))
        q_ref[h, :ROWS, :] = clean.astype(BF16)
        q_ref[h, ROWS:, :] = jnp.where(flag > 0.5, fixed, clean).astype(BF16)


def near_kernel(q_ref, kv_ref, mkv_ref, flag_ref, code_ref, top_ref, total_ref, accum_ref):
    masked = flag_ref[...] > 0.5

    def both(lanes):
        clean = kv_ref[:ROWS, lanes]
        fixed = jnp.broadcast_to(mkv_ref[0:1, lanes].astype(F32), (ROWS, HEAD))
        return jnp.concatenate([clean, jnp.where(masked, fixed, clean.astype(F32)).astype(BF16)], axis=0)

    row = code_ref[...].astype(F32)[0:1]
    query = jnp.broadcast_to(column(row), (ROWS, ROWS))
    key = jnp.broadcast_to(row, (ROWS, ROWS))
    zero = jnp.zeros((ROWS, ROWS), F32)
    low = jnp.full((ROWS, ROWS), LOW, F32)
    clean_bias = jnp.concatenate([jnp.where(key <= query, zero, low), low], axis=1)
    noisy_bias = jnp.concatenate([jnp.where(key < query, zero, low), jnp.where(key == query, zero, low)], axis=1)
    bias = jnp.concatenate([clean_bias, noisy_bias], axis=0)
    keys = both(slice(0, HEAD))
    values = both(slice(HEAD, 2 * HEAD))
    for h in range(GROUP):
        scores = jnp.where(bias < -1.0, LOW, dot_t(q_ref[h], keys))
        top = jnp.max(scores, axis=1, keepdims=True)
        probs = jnp.exp2((scores - top) * POWER)
        top_ref[h] = jnp.broadcast_to(top, (2 * ROWS, HEAD))
        total_ref[h] = jnp.broadcast_to(jnp.sum(probs, axis=1, keepdims=True), (2 * ROWS, HEAD))
        accum_ref[h] = dot(probs.astype(BF16), values)


def place():
    me = lax.axis_index("ctx")
    return me, me // 8, lax.rem(me // 2, 4), lax.rem(me, 2)


def pipeline(q_ref, pieces, state_in, state, finish):
    top_ref, total_ref, accum_ref = state

    def scores_of(step):
        h, chunk, _, _ = step
        keys, _, mask, _ = pieces[chunk]
        scores = dot_t(q_ref[h], keys())
        parts = [scores[:, j : j + ROWS] for j in range(0, scores.shape[1], ROWS)]
        return mask(parts) if mask is not None else parts

    def absorb(step, parts):
        h, chunk, first, last = step
        _, values, _, seen = pieces[chunk]
        best = parts[0]
        for part in parts[1:]:
            best = jnp.maximum(best, part)
        best = jnp.max(best, axis=1, keepdims=True)
        if seen is not None:
            best = jnp.where(seen, best, LOW)
        source = state_in if first else state
        old = source[0][h]
        top = jnp.maximum(old, best)
        factor = jnp.exp2((old - top) * POWER)
        level = top if seen is None else jnp.where(seen, top, -LOW)
        probs = [jnp.exp2((part - level) * POWER) for part in parts]
        probs = jnp.concatenate([part.astype(BF16) for part in probs], axis=1)
        right = values()
        product = dot(probs, jnp.concatenate([right, jnp.ones(right.shape, BF16)], axis=1))
        total = source[1][h] * factor + product[:, HEAD:]
        accum = source[2][h] * factor + product[:, :HEAD]
        if last and finish is not None:
            finish(h, accum, total)
        else:
            top_ref[h] = top
            total_ref[h] = total
            accum_ref[h] = accum

    order = [(h, i, i == 0, i == len(pieces) - 1) for i in range(len(pieces)) for h in range(GROUP)]
    parts = scores_of(order[0])
    for now, later in zip(order, order[1:] + [None]):
        following = None if later is None else scores_of(later)
        absorb(now, parts)
        parts = following


def blocks_of(ref, which):
    return jnp.concatenate([ref[i * 2 * ROWS : (i + 1) * 2 * ROWS, :] for i in which], axis=0)


def shard_mask(where, spots):
    me, y, x, z = where

    def mask(parts):
        kept = []
        for j, part in enumerate(parts):
            dy, dx = spots[j // 2]
            there = jnp.bitwise_xor(me, dy * 8 + dx * 2 + j % 2)
            kept.append(jnp.where(there < me - 1, part, LOW))
        return kept

    return mask


def spots_piece(where, k_of, v_of, spots):
    def keys():
        return jnp.concatenate([k_of[dy][dx * 2 * ROWS : (dx + 1) * 2 * ROWS, :] for dy, dx in spots], axis=0)

    def values():
        return jnp.concatenate([v_of[dx][dy * 2 * ROWS : (dy + 1) * 2 * ROWS, :] for dy, dx in spots], axis=0)

    return keys, values, shard_mask(where, spots), None


def first_kernel(*refs):
    q_ref = refs[0]
    k_of, v_of = dict(zip((0, 1), refs[1:3])), dict(zip((0, 1), refs[3:5]))
    piece = spots_piece(place(), k_of, v_of, ((0, 1), (1, 0), (1, 1)))
    pipeline(q_ref, [piece], refs[5:8], refs[8:11], None)


def far_kernel(*refs):
    q_ref = refs[0]
    k_refs = dict(zip((0, 1, 3), refs[1:4]))
    v_refs = dict(zip((0, 1, 3), refs[4:7]))
    state_in = refs[7:10]
    code_ref, own_cut_ref, mkv_ref = refs[10:13]
    state = refs[13:16]
    me, y, x, z = place()

    spots = ((0, 0), (0, 1), (0, 3), (1, 3), (3, 3))
    old_far = jnp.bitwise_xor(me, jnp.maximum(me - 1, 0)) // 2
    new_far = jnp.bitwise_xor(me, jnp.minimum(me + 1, LAST)) // 2

    def pick(far, of):
        chosen = of(*spots[0])
        for dy, dx in spots[1:]:
            chosen = jnp.where(far == dy * 4 + dx, of(dy, dx), chosen)
        return chosen

    def k_block(dy, dx):
        return k_refs[dy][(dx * 2 + 1) * ROWS : (dx * 2 + 2) * ROWS, :]

    def v_block(dy, dx):
        return v_refs[dx][(dy * 2 + 1) * ROWS : (dy * 2 + 2) * ROWS, :]

    k_old, v_old = pick(old_far, k_block), pick(old_far, v_block)
    k_new, v_new = pick(new_far, k_block), pick(new_far, v_block)
    k_new, v_new = k_new[:BLOCK], v_new[:BLOCK]

    own = code_ref[...].astype(F32)[0:1]
    tails = {dy: ref_tail(k_refs[dy], 8 * ROWS) for dy in (0, 1, 3)}

    def line(i):
        def row(dy, dx):
            return tails[dy][dx * 4 + 2 + i : dx * 4 + 3 + i]

        return pick(old_far, row), pick(new_far, row)

    old_ids, new_ids = line(0)
    old_order, new_order = line(1)
    old_ids = jnp.broadcast_to(jnp.where(me > 0, old_ids, FAR), (8, ROWS))
    new_ids = jnp.broadcast_to(jnp.where(me < LAST, new_ids, FAR), (8, ROWS))
    first_cut = own_cut_ref[0:1, :]
    last_cut = own_cut_ref[ROWS - 1 : ROWS, :]
    old_masked = column(jnp.where(old_order >= first_cut, 1.0, 0.0))[ROWS - BLOCK :]
    new_masked = column(jnp.where(new_order >= last_cut, 1.0, 0.0))[:BLOCK]

    def noisy(masked, clean, lanes):
        fixed = jnp.broadcast_to(mkv_ref[0:1, lanes].astype(F32), clean.shape)
        flag = jnp.broadcast_to(masked, clean.shape) > 0.5
        return jnp.where(flag, fixed, clean.astype(F32)).astype(BF16)

    def rim(old, new, lanes):
        parts = [old, new, noisy(old_masked, old[ROWS - BLOCK :], lanes), noisy(new_masked, new, lanes)]
        return jnp.concatenate(parts + [jnp.zeros((BLOCK, HEAD), BF16)], axis=0)

    k_rim = rim(k_old, k_new, slice(0, HEAD))
    v_rim = rim(v_old, v_new, slice(HEAD, 2 * HEAD))
    lane = lax.broadcasted_iota(jnp.int32, (8, ROWS), 1)
    mixed = jnp.where(
        lane < 32,
        new_ids,
        jnp.where(lane < 64, pltpu.roll(old_ids, 64, 1), jnp.where(lane < 96, pltpu.roll(new_ids, 64, 1), -5.0)),
    )
    square = (ROWS, ROWS)
    query = jnp.broadcast_to(column(own), square)
    old_key = jnp.broadcast_to(old_ids[0:1], square)
    mixed_key = jnp.broadcast_to(mixed[0:1], square)
    early = lax.broadcasted_iota(jnp.int32, square, 1) < 32
    zero = jnp.zeros(square, F32)
    low = jnp.full(square, LOW, F32)
    clean_bias = [
        jnp.where(old_key <= query, zero, low),
        jnp.where(early, jnp.where(mixed_key <= query, zero, low), low),
    ]
    noisy_bias = [
        jnp.where(old_key < query, zero, low),
        jnp.where(early, jnp.where(mixed_key < query, zero, low), jnp.where(mixed_key == query, zero, low)),
    ]
    bias = jnp.concatenate([jnp.concatenate(clean_bias, axis=1), jnp.concatenate(noisy_bias, axis=1)], axis=0)

    def rim_mask(parts):
        return [jnp.where(bias[:, j * ROWS : (j + 1) * ROWS] < -1.0, LOW, part) for j, part in enumerate(parts)]

    spots = ((0, 3), (1, 3), (3, 0), (3, 1), (3, 3))
    pieces = [
        (lambda: k_rim, lambda: v_rim, rim_mask, None),
        spots_piece((me, y, x, z), k_refs, v_refs, spots),
    ]
    pipeline(q_ref, pieces, state_in, state, None)


def third_kernel(*refs):
    q_ref, k_ref, v_refs = refs[0], refs[1], refs[2:5]
    where = place()
    near = (0, 1, 3)
    keys, values, _, _ = spots_piece(where, {2: k_ref}, dict(zip(near, v_refs)), [(2, dx) for dx in near])
    piece = (keys, values, None, where[1] >= 2)
    pipeline(q_ref, [piece], refs[5:8], refs[8:11], None)


def last_kernel(*refs):
    q_ref, k_refs, v_ref = refs[0], refs[1:5], refs[5]
    state_in = refs[6:9]
    clean_ref, noisy_ref = refs[9:11]
    state = refs[11:]
    piece = spots_piece(place(), dict(enumerate(k_refs)), {2: v_ref}, [(dy, 2) for dy in range(4)])

    def finish(h, accum, total):
        lanes = slice(h * HEAD, (h + 1) * HEAD)
        result = (accum / total).astype(BF16)
        clean_ref[:, lanes] = result[:ROWS]
        noisy_ref[:, lanes] = result[ROWS:]

    pipeline(q_ref, [piece], state_in, state, finish)


def shards(hidden, block_ids, decode_order, step_cut, mask_embed, q_weight, k_weight, v_weight):
    ids = block_ids.reshape(1, ROWS)
    order = decode_order.reshape(1, ROWS)
    cuts = step_cut.reshape(1, -1)
    two, one, three = [lax.ppermute(hidden, "kv", kv_pairs(d, 0)) for d in (2, 1, 3)]
    moved = [one, two, three]
    own, wk, wv, code, pad = call(
        prep_kernel,
        [
            (hidden.shape, BF16),
            (k_weight.shape, BF16),
            (v_weight.shape, BF16),
            ((PAD, ROWS), BF16),
            ((PAD, 8 * WIDTH), BF16),
        ],
        [held(a) for a in (hidden, k_weight, v_weight, ids, order, mask_embed.reshape(1, -1))],
        (1 << 20, 4 << 20),
        [
            pltpu.VMEM(ids.shape, jnp.int32),
            pltpu.VMEM(ids.shape, jnp.int32),
            pltpu.VMEM((1, 8 * WIDTH), BF16),
            pltpu.SemaphoreType.DMA((6,)),
        ],
        pl.ANY,
    )
    pieces = []
    for piece in (own, *moved):
        piece, _ = lax.optimization_barrier((piece, pad))
        pieces += [piece, lax.ppermute(piece, "kv", kv_pairs(0, 1))]
    x, kv, mask_kv = call(
        kv_kernel,
        [
            ((ROWS + PAD, 8 * WIDTH), BF16),
            ((ROWS + PAD, 2 * HEAD), BF16),
            ((PAD, 2 * HEAD), BF16),
        ],
        [*pieces, pad, wk, wv, code],
        (1 << 29, 3 << 20),
    )
    pair = lax.ppermute(kv, "ctx", ctx_pairs(0, 0, 1))
    q, flag, own_cut = call(
        q_kernel,
        [((GROUP, 2 * ROWS, HEAD), BF16), ((ROWS, HEAD), F32), ((ROWS, HEAD), F32)],
        [x, q_weight, code, cuts],
        (1 << 30, 5 << 20),
    )
    near = call(
        near_kernel,
        [((GROUP, 2 * ROWS, HEAD), F32)] * 3,
        [q, kv, mask_kv, flag, code],
        (1 << 30, 2 << 20),
    )
    pair, _ = lax.optimization_barrier((pair, flag))
    k, v = call(
        pair_kernel,
        [((2 * ROWS + PAD, HEAD), BF16), ((2 * ROWS, HEAD), BF16)],
        [kv, pair],
        (1 << 10, 1 << 18),
    )
    ks = [lax.ppermute(k, "ctx", ctx_pairs(0, d, 0)) for d in (1, 2, 3)]
    vs = [lax.ppermute(v, "ctx", ctx_pairs(d, 0, 0)) for d in (1, 2, 3)]
    ks, vs = call(
        stack_kernel,
        [((8 * ROWS + PAD, HEAD), BF16), ((8 * ROWS, HEAD), BF16)],
        [k, *ks, v, *vs],
        (1 << 10, 1 << 20),
    )
    all_k = [ks] + [lax.ppermute(ks, "ctx", ctx_pairs(d, 0, 0)) for d in (1, 2, 3)]
    all_v = [vs] + [lax.ppermute(vs, "ctx", ctx_pairs(0, d, 0)) for d in (1, 2, 3)]
    state = [((GROUP, 2 * ROWS, HEAD), F32)] * 3
    first = call(
        first_kernel,
        state,
        [q, *all_k[:2], *all_v[:2], *near],
        (1 << 30, 2 << 20),
    )
    far = call(
        far_kernel,
        state,
        [q, *[all_k[d] for d in (0, 1, 3)], *[all_v[d] for d in (0, 1, 3)], *first, code, own_cut, mask_kv],
        (1 << 31, 4 << 20),
    )
    third = call(
        third_kernel,
        state,
        [q, all_k[2], *[all_v[d] for d in (0, 1, 3)], *far],
        (1 << 30, 2 << 20),
    )
    return tuple(
        call(
            last_kernel,
            [((ROWS, GROUP * HEAD), BF16)] * 2,
            [q, *all_k, all_v[2], *third],
            (1 << 31, 4 << 20),
            [pltpu.VMEM((GROUP, 2 * ROWS, HEAD), F32)] * 3,
        )
    )


def solution(mesh):
    return jax.shard_map(
        shards,
        mesh=mesh,
        in_specs=(
            P("ctx", "kv"),
            P("ctx"),
            P("ctx"),
            P(),
            P(),
            P(None, "kv"),
            P(None, "kv"),
            P(None, "kv"),
        ),
        out_specs=(P("ctx", "kv"), P("ctx", "kv")),
        check_vma=False,
    )
```

```python
import math

import jax
import jax.numpy as jnp
from jax import lax
from jax.experimental import pallas as pl
from jax.experimental.pallas import tpu as pltpu
from jax.sharding import PartitionSpec as P

ROWS = 128
HEAD = 128
GROUP = 4
PAD = 16
WIDTH = 512
BLOCK = 32
LAST = 31
LOW = -1e30
FAR = 1e6
POWER = math.log2(math.e) / math.sqrt(HEAD)
LIMIT = 48 * 1024 * 1024
F32 = jnp.float32
BF16 = jnp.bfloat16


def ctx_pairs(dy, dx, dz):
    pairs = []
    for i in range(32):
        y, x, z = i // 8, (i // 2) % 4, i % 2
        pairs.append((i, ((y ^ dy) * 4 + (x ^ dx)) * 2 + (z ^ dz)))
    return pairs


def kv_pairs(dz, dc):
    pairs = []
    for i in range(8):
        z, c = i // 2, i % 2
        pairs.append((i, (z ^ dz) * 2 + (c ^ dc)))
    return pairs


def dot(a, b):
    return jnp.dot(a, b, preferred_element_type=F32)


def dot_t(a, b):
    return lax.dot_general(a, b, (((1,), (1,)), ((), ())), preferred_element_type=F32)


def call(kernel, outs, args, cost, scratch=(), space=pltpu.VMEM):
    spec = pl.BlockSpec(memory_space=pltpu.VMEM)
    return pl.pallas_call(
        kernel,
        out_shape=[jax.ShapeDtypeStruct(s, t) for s, t in outs],
        in_specs=[pl.BlockSpec(memory_space=space)] * len(args),
        out_specs=[spec] * len(outs),
        scratch_shapes=list(scratch),
        compiler_params=pltpu.CompilerParams(vmem_limit_bytes=LIMIT),
        cost_estimate=pl.CostEstimate(flops=cost[0], bytes_accessed=cost[1], transcendentals=0),
    )(*args)


def held(array):
    return pltpu.with_memory_space_constraint(array, pltpu.HBM)


def column(row):
    square = (ROWS, ROWS)
    same = lax.broadcasted_iota(jnp.int32, square, 0) == lax.broadcasted_iota(jnp.int32, square, 1)
    return jnp.sum(jnp.where(same, jnp.broadcast_to(row, square), 0.0), axis=1, keepdims=True)


def prep_kernel(*refs):
    hidden_hbm, wk_hbm, wv_hbm, ids_hbm, order_hbm, embed_hbm = refs[:6]
    own_ref, wk_ref, wv_ref, code_ref, pad_ref = refs[6:11]
    ids_ref, order_ref, embed_ref, sems = refs[11:]
    pairs = (
        (ids_hbm, ids_ref),
        (order_hbm, order_ref),
        (embed_hbm, embed_ref),
        (hidden_hbm, own_ref),
        (wk_hbm, wk_ref),
        (wv_hbm, wv_ref),
    )
    copies = [pltpu.make_async_copy(a, b, sems.at[i]) for i, (a, b) in enumerate(pairs)]
    for copy in copies:
        copy.start()
    for copy in copies:
        copy.wait()
    ids = jnp.broadcast_to(ids_ref[...].astype(F32), (PAD, ROWS))
    order = jnp.broadcast_to(order_ref[...].astype(F32), (PAD, ROWS))
    row = lax.broadcasted_iota(jnp.int32, (PAD, ROWS), 0)
    code_ref[...] = jnp.where(lax.rem(row, 2) == 0, ids, order).astype(BF16)
    pad_ref[...] = jnp.broadcast_to(embed_ref[...], pad_ref.shape)


def kv_kernel(*refs):
    pieces = refs[:8]
    pad_ref, wk_ref, wv_ref, code_ref = refs[8:12]
    x_ref, kv_ref, mkv_ref = refs[12:]
    me = lax.axis_index("kv")
    for dz in range(4):
        for dc in range(2):
            source = jnp.bitwise_xor(me, 2 * dz + dc)
            lanes = pl.ds(pl.multiple_of(source * WIDTH, WIDTH), WIDTH)
            x_ref[:ROWS, lanes] = pieces[2 * dz + dc][...]
    x_ref[ROWS:, :] = pad_ref[...]
    x = x_ref[...]
    for part, w_ref in enumerate((wk_ref, wv_ref)):
        lanes = slice(part * HEAD, (part + 1) * HEAD)
        product = dot(x, w_ref[...]).astype(BF16)
        kv_ref[:ROWS, lanes] = product[:ROWS]
        kv_ref[ROWS:, lanes] = code_ref[...]
        mkv_ref[:, lanes] = product[ROWS:]


def pair_kernel(own_ref, other_ref, k_ref, v_ref):
    for i, ref in enumerate((own_ref, other_ref)):
        rows = slice(i * ROWS, (i + 1) * ROWS)
        k_ref[rows, :] = ref[:ROWS, :HEAD]
        v_ref[rows, :] = ref[:ROWS, HEAD:]
    row = lax.broadcasted_iota(jnp.int32, (PAD, HEAD), 0)
    first = ref_tail(own_ref, ROWS)
    code = jnp.where(lax.rem(row, 4) < 2, first, ref_tail(other_ref, ROWS))
    k_ref[2 * ROWS :, :] = code.astype(BF16)


def ref_tail(ref, start):
    return ref[start:, :HEAD].astype(F32)


def stack_kernel(*refs):
    ks, vs = refs[:4], refs[4:8]
    k_ref, v_ref = refs[8:]
    row = lax.broadcasted_iota(jnp.int32, (PAD, HEAD), 0)
    code = jnp.zeros((PAD, HEAD), F32)
    for i in range(4):
        rows = slice(i * 2 * ROWS, (i + 1) * 2 * ROWS)
        k_ref[rows, :] = ks[i][: 2 * ROWS, :]
        v_ref[rows, :] = vs[i][...]
        code = jnp.where(row // 4 == i, ref_tail(ks[i], 2 * ROWS), code)
    k_ref[8 * ROWS :, :] = code.astype(BF16)


def q_kernel(x_ref, wq_ref, code_ref, cut_ref, q_ref, flag_ref, own_cut_ref):
    code = code_ref[...].astype(F32)
    ids = column(code[0:1])
    order = column(code[1:2])
    blocks = cut_ref.shape[1]
    spots = lax.broadcasted_iota(jnp.int32, (ROWS, blocks), 1).astype(F32)
    cuts = jnp.broadcast_to(cut_ref[...].astype(F32), (ROWS, blocks))
    cut = jnp.sum(jnp.where(spots == ids, cuts, 0.0), axis=1, keepdims=True)
    flag = jnp.broadcast_to(jnp.where(order >= cut, 1.0, 0.0), (ROWS, HEAD))
    flag_ref[...] = flag
    own_cut_ref[...] = jnp.broadcast_to(cut, (ROWS, HEAD))
    x = x_ref[...]
    for h in range(GROUP):
        product = dot(x, wq_ref[:, h * HEAD : (h + 1) * HEAD])
        clean = product[:ROWS]
        fixed = jnp.broadcast_to(product[ROWS : ROWS + 1], (ROWS, HEAD))
        q_ref[h, :ROWS, :] = clean.astype(BF16)
        q_ref[h, ROWS:, :] = jnp.where(flag > 0.5, fixed, clean).astype(BF16)


def near_kernel(q_ref, kv_ref, mkv_ref, flag_ref, code_ref, top_ref, total_ref, accum_ref):
    masked = flag_ref[...] > 0.5

    def both(lanes):
        clean = kv_ref[:ROWS, lanes]
        fixed = jnp.broadcast_to(mkv_ref[0:1, lanes].astype(F32), (ROWS, HEAD))
        return jnp.concatenate([clean, jnp.where(masked, fixed, clean.astype(F32)).astype(BF16)], axis=0)

    row = code_ref[...].astype(F32)[0:1]
    query = jnp.broadcast_to(column(row), (ROWS, ROWS))
    key = jnp.broadcast_to(row, (ROWS, ROWS))
    zero = jnp.zeros((ROWS, ROWS), F32)
    low = jnp.full((ROWS, ROWS), LOW, F32)
    clean_bias = jnp.concatenate([jnp.where(key <= query, zero, low), low], axis=1)
    noisy_bias = jnp.concatenate([jnp.where(key < query, zero, low), jnp.where(key == query, zero, low)], axis=1)
    bias = jnp.concatenate([clean_bias, noisy_bias], axis=0)
    keys = both(slice(0, HEAD))
    values = both(slice(HEAD, 2 * HEAD))
    for h in range(GROUP):
        scores = jnp.where(bias < -1.0, LOW, dot_t(q_ref[h], keys))
        top = jnp.max(scores, axis=1, keepdims=True)
        probs = jnp.exp2((scores - top) * POWER)
        top_ref[h] = jnp.broadcast_to(top, (2 * ROWS, HEAD))
        total_ref[h] = jnp.broadcast_to(jnp.sum(probs, axis=1, keepdims=True), (2 * ROWS, HEAD))
        accum_ref[h] = dot(probs.astype(BF16), values)


def place():
    me = lax.axis_index("ctx")
    return me, me // 8, lax.rem(me // 2, 4), lax.rem(me, 2)


def pipeline(q_ref, pieces, state_in, state, finish):
    top_ref, total_ref, accum_ref = state

    def scores_of(step):
        h, chunk, _, _ = step
        keys, _, mask, _ = pieces[chunk]
        scores = dot_t(q_ref[h], keys())
        parts = [scores[:, j : j + ROWS] for j in range(0, scores.shape[1], ROWS)]
        return mask(parts) if mask is not None else parts

    def absorb(step, parts):
        h, chunk, first, last = step
        _, values, _, seen = pieces[chunk]
        best = parts[0]
        for part in parts[1:]:
            best = jnp.maximum(best, part)
        best = jnp.max(best, axis=1, keepdims=True)
        if seen is not None:
            best = jnp.where(seen, best, LOW)
        source = state_in if first else state
        old = source[0][h]
        top = jnp.maximum(old, best)
        factor = jnp.exp2((old - top) * POWER)
        level = top if seen is None else jnp.where(seen, top, -LOW)
        probs = [jnp.exp2((part - level) * POWER) for part in parts]
        probs = jnp.concatenate([part.astype(BF16) for part in probs], axis=1)
        right = values()
        product = dot(probs, jnp.concatenate([right, jnp.ones(right.shape, BF16)], axis=1))
        total = source[1][h] * factor + product[:, HEAD:]
        accum = source[2][h] * factor + product[:, :HEAD]
        if last and finish is not None:
            finish(h, accum, total)
        else:
            top_ref[h] = top
            total_ref[h] = total
            accum_ref[h] = accum

    order = [(h, i, i == 0, i == len(pieces) - 1) for i in range(len(pieces)) for h in range(GROUP)]
    parts = scores_of(order[0])
    for now, later in zip(order, order[1:] + [None]):
        following = None if later is None else scores_of(later)
        absorb(now, parts)
        parts = following


def blocks_of(ref, which):
    return jnp.concatenate([ref[i * 2 * ROWS : (i + 1) * 2 * ROWS, :] for i in which], axis=0)


def shard_mask(where, spots):
    me, y, x, z = where

    def mask(parts):
        kept = []
        for j, part in enumerate(parts):
            dy, dx = spots[j // 2]
            there = jnp.bitwise_xor(me, dy * 8 + dx * 2 + j % 2)
            kept.append(jnp.where(there < me - 1, part, LOW))
        return kept

    return mask


def spots_piece(where, k_of, v_of, spots):
    def keys():
        return jnp.concatenate([k_of[dy][dx * 2 * ROWS : (dx + 1) * 2 * ROWS, :] for dy, dx in spots], axis=0)

    def values():
        return jnp.concatenate([v_of[dx][dy * 2 * ROWS : (dy + 1) * 2 * ROWS, :] for dy, dx in spots], axis=0)

    return keys, values, shard_mask(where, spots), None


def first_kernel(*refs):
    q_ref = refs[0]
    k_of, v_of = dict(zip((0, 1), refs[1:3])), dict(zip((0, 1), refs[3:5]))
    piece = spots_piece(place(), k_of, v_of, ((0, 1), (1, 0), (1, 1)))
    pipeline(q_ref, [piece], refs[5:8], refs[8:11], None)


def far_kernel(*refs):
    q_ref = refs[0]
    k_refs = dict(zip((0, 1, 3), refs[1:4]))
    v_refs = dict(zip((0, 1, 3), refs[4:7]))
    state_in = refs[7:10]
    code_ref, own_cut_ref, mkv_ref = refs[10:13]
    state = refs[13:16]
    me, y, x, z = place()

    spots = ((0, 0), (0, 1), (0, 3), (1, 3), (3, 3))
    old_far = jnp.bitwise_xor(me, jnp.maximum(me - 1, 0)) // 2
    new_far = jnp.bitwise_xor(me, jnp.minimum(me + 1, LAST)) // 2

    def pick(far, of):
        chosen = of(*spots[0])
        for dy, dx in spots[1:]:
            chosen = jnp.where(far == dy * 4 + dx, of(dy, dx), chosen)
        return chosen

    def k_block(dy, dx):
        return k_refs[dy][(dx * 2 + 1) * ROWS : (dx * 2 + 2) * ROWS, :]

    def v_block(dy, dx):
        return v_refs[dx][(dy * 2 + 1) * ROWS : (dy * 2 + 2) * ROWS, :]

    k_old, v_old = pick(old_far, k_block), pick(old_far, v_block)
    k_new, v_new = pick(new_far, k_block), pick(new_far, v_block)
    k_new, v_new = k_new[:BLOCK], v_new[:BLOCK]

    own = code_ref[...].astype(F32)[0:1]
    tails = {dy: ref_tail(k_refs[dy], 8 * ROWS) for dy in (0, 1, 3)}

    def line(i):
        def row(dy, dx):
            return tails[dy][dx * 4 + 2 + i : dx * 4 + 3 + i]

        return pick(old_far, row), pick(new_far, row)

    old_ids, new_ids = line(0)
    old_order, new_order = line(1)
    old_ids = jnp.broadcast_to(jnp.where(me > 0, old_ids, FAR), (8, ROWS))
    new_ids = jnp.broadcast_to(jnp.where(me < LAST, new_ids, FAR), (8, ROWS))
    first_cut = own_cut_ref[0:1, :]
    last_cut = own_cut_ref[ROWS - 1 : ROWS, :]
    old_masked = column(jnp.where(old_order >= first_cut, 1.0, 0.0))[ROWS - BLOCK :]
    new_masked = column(jnp.where(new_order >= last_cut, 1.0, 0.0))[:BLOCK]

    def noisy(masked, clean, lanes):
        fixed = jnp.broadcast_to(mkv_ref[0:1, lanes].astype(F32), clean.shape)
        flag = jnp.broadcast_to(masked, clean.shape) > 0.5
        return jnp.where(flag, fixed, clean.astype(F32)).astype(BF16)

    def rim(old, new, lanes):
        parts = [old, new, noisy(old_masked, old[ROWS - BLOCK :], lanes), noisy(new_masked, new, lanes)]
        return jnp.concatenate(parts + [jnp.zeros((BLOCK, HEAD), BF16)], axis=0)

    k_rim = rim(k_old, k_new, slice(0, HEAD))
    v_rim = rim(v_old, v_new, slice(HEAD, 2 * HEAD))
    lane = lax.broadcasted_iota(jnp.int32, (8, ROWS), 1)
    mixed = jnp.where(
        lane < 32,
        new_ids,
        jnp.where(lane < 64, pltpu.roll(old_ids, 64, 1), jnp.where(lane < 96, pltpu.roll(new_ids, 64, 1), -5.0)),
    )
    square = (ROWS, ROWS)
    query = jnp.broadcast_to(column(own), square)
    old_key = jnp.broadcast_to(old_ids[0:1], square)
    mixed_key = jnp.broadcast_to(mixed[0:1], square)
    early = lax.broadcasted_iota(jnp.int32, square, 1) < 32
    zero = jnp.zeros(square, F32)
    low = jnp.full(square, LOW, F32)
    clean_bias = [
        jnp.where(old_key <= query, zero, low),
        jnp.where(early, jnp.where(mixed_key <= query, zero, low), low),
    ]
    noisy_bias = [
        jnp.where(old_key < query, zero, low),
        jnp.where(early, jnp.where(mixed_key < query, zero, low), jnp.where(mixed_key == query, zero, low)),
    ]
    bias = jnp.concatenate([jnp.concatenate(clean_bias, axis=1), jnp.concatenate(noisy_bias, axis=1)], axis=0)

    def rim_mask(parts):
        return [jnp.where(bias[:, j * ROWS : (j + 1) * ROWS] < -1.0, LOW, part) for j, part in enumerate(parts)]

    spots = ((0, 3), (1, 3), (3, 0), (3, 1), (3, 3))
    pieces = [
        (lambda: k_rim, lambda: v_rim, rim_mask, None),
        spots_piece((me, y, x, z), k_refs, v_refs, spots),
    ]
    pipeline(q_ref, pieces, state_in, state, None)


def last_kernel(*refs):
    q_ref, k_refs, v_refs = refs[0], refs[1:5], refs[5:9]
    state_in = refs[9:12]
    clean_ref, noisy_ref = refs[12:14]
    state = refs[14:17]
    where = place()
    k_of, v_of = dict(enumerate(k_refs)), dict(enumerate(v_refs))
    keys, values, _, _ = spots_piece(where, k_of, v_of, [(2, dx) for dx in range(4)])
    pieces = [
        (keys, values, None, where[1] >= 2),
        spots_piece(where, k_of, v_of, [(dy, 2) for dy in (0, 1, 3)]),
    ]

    def finish(h, accum, total):
        lanes = slice(h * HEAD, (h + 1) * HEAD)
        result = (accum / total).astype(BF16)
        clean_ref[:, lanes] = result[:ROWS]
        noisy_ref[:, lanes] = result[ROWS:]

    pipeline(q_ref, pieces, state_in, state, finish)


def shards(hidden, block_ids, decode_order, step_cut, mask_embed, q_weight, k_weight, v_weight):
    ids = block_ids.reshape(1, ROWS)
    order = decode_order.reshape(1, ROWS)
    cuts = step_cut.reshape(1, -1)
    two, one, three = [lax.ppermute(hidden, "kv", kv_pairs(d, 0)) for d in (2, 1, 3)]
    moved = [one, two, three]
    own, wk, wv, code, pad = call(
        prep_kernel,
        [
            (hidden.shape, BF16),
            (k_weight.shape, BF16),
            (v_weight.shape, BF16),
            ((PAD, ROWS), BF16),
            ((PAD, 8 * WIDTH), BF16),
        ],
        [held(a) for a in (hidden, k_weight, v_weight, ids, order, mask_embed.reshape(1, -1))],
        (1 << 20, 4 << 20),
        [
            pltpu.VMEM(ids.shape, jnp.int32),
            pltpu.VMEM(ids.shape, jnp.int32),
            pltpu.VMEM((1, 8 * WIDTH), BF16),
            pltpu.SemaphoreType.DMA((6,)),
        ],
        pl.ANY,
    )
    pieces = []
    for piece in (own, *moved):
        piece, _ = lax.optimization_barrier((piece, pad))
        pieces += [piece, lax.ppermute(piece, "kv", kv_pairs(0, 1))]
    x, kv, mask_kv = call(
        kv_kernel,
        [
            ((ROWS + PAD, 8 * WIDTH), BF16),
            ((ROWS + PAD, 2 * HEAD), BF16),
            ((PAD, 2 * HEAD), BF16),
        ],
        [*pieces, pad, wk, wv, code],
        (1 << 29, 3 << 20),
    )
    pair = lax.ppermute(kv, "ctx", ctx_pairs(0, 0, 1))
    q, flag, own_cut = call(
        q_kernel,
        [((GROUP, 2 * ROWS, HEAD), BF16), ((ROWS, HEAD), F32), ((ROWS, HEAD), F32)],
        [x, q_weight, code, cuts],
        (1 << 30, 5 << 20),
    )
    near = call(
        near_kernel,
        [((GROUP, 2 * ROWS, HEAD), F32)] * 3,
        [q, kv, mask_kv, flag, code],
        (1 << 30, 2 << 20),
    )
    pair, _ = lax.optimization_barrier((pair, flag))
    k, v = call(
        pair_kernel,
        [((2 * ROWS + PAD, HEAD), BF16), ((2 * ROWS, HEAD), BF16)],
        [kv, pair],
        (1 << 10, 1 << 18),
    )
    ks = [lax.ppermute(k, "ctx", ctx_pairs(0, d, 0)) for d in (1, 2, 3)]
    vs = [lax.ppermute(v, "ctx", ctx_pairs(d, 0, 0)) for d in (1, 2, 3)]
    ks, vs = call(
        stack_kernel,
        [((8 * ROWS + PAD, HEAD), BF16), ((8 * ROWS, HEAD), BF16)],
        [k, *ks, v, *vs],
        (1 << 10, 1 << 20),
    )
    all_k = [ks] + [lax.ppermute(ks, "ctx", ctx_pairs(d, 0, 0)) for d in (1, 2, 3)]
    all_v = [vs] + [lax.ppermute(vs, "ctx", ctx_pairs(0, d, 0)) for d in (1, 2, 3)]
    state = [((GROUP, 2 * ROWS, HEAD), F32)] * 3
    first = call(
        first_kernel,
        state,
        [q, *all_k[:2], *all_v[:2], *near],
        (1 << 30, 2 << 20),
    )
    far = call(
        far_kernel,
        state,
        [q, *[all_k[d] for d in (0, 1, 3)], *[all_v[d] for d in (0, 1, 3)], *first, code, own_cut, mask_kv],
        (1 << 31, 4 << 20),
    )
    return tuple(
        call(
            last_kernel,
            [((ROWS, GROUP * HEAD), BF16)] * 2,
            [q, *all_k, *all_v, *far],
            (1 << 31, 4 << 20),
            [pltpu.VMEM((GROUP, 2 * ROWS, HEAD), F32)] * 3,
        )
    )


def solution(mesh):
    return jax.shard_map(
        shards,
        mesh=mesh,
        in_specs=(
            P("ctx", "kv"),
            P("ctx"),
            P("ctx"),
            P(),
            P(),
            P(None, "kv"),
            P(None, "kv"),
            P(None, "kv"),
        ),
        out_specs=(P("ctx", "kv"), P("ctx", "kv")),
        check_vma=False,
    )
```

```python
import math

import jax
import jax.numpy as jnp
from jax import lax
from jax.experimental import pallas as pl
from jax.experimental.pallas import tpu as pltpu
from jax.sharding import PartitionSpec as P

ROWS = 128
HEAD = 128
GROUP = 4
PAD = 16
WIDTH = 512
BLOCK = 32
LAST = 31
LOW = -1e30
FAR = 1e6
POWER = math.log2(math.e) / math.sqrt(HEAD)
LIMIT = 48 * 1024 * 1024
F32 = jnp.float32
BF16 = jnp.bfloat16


def ctx_pairs(dy, dx, dz):
    pairs = []
    for i in range(32):
        y, x, z = i // 8, (i // 2) % 4, i % 2
        pairs.append((i, ((y ^ dy) * 4 + (x ^ dx)) * 2 + (z ^ dz)))
    return pairs


def kv_pairs(dz, dc):
    pairs = []
    for i in range(8):
        z, c = i // 2, i % 2
        pairs.append((i, (z ^ dz) * 2 + (c ^ dc)))
    return pairs


def dot(a, b):
    return jnp.dot(a, b, preferred_element_type=F32)


def dot_t(a, b):
    return lax.dot_general(a, b, (((1,), (1,)), ((), ())), preferred_element_type=F32)


def call(kernel, outs, args, cost, scratch=(), space=pltpu.VMEM, out_space=pltpu.VMEM):
    spec = pl.BlockSpec(memory_space=out_space)
    return pl.pallas_call(
        kernel,
        out_shape=[jax.ShapeDtypeStruct(s, t) for s, t in outs],
        in_specs=[pl.BlockSpec(memory_space=space)] * len(args),
        out_specs=[spec] * len(outs),
        scratch_shapes=list(scratch),
        compiler_params=pltpu.CompilerParams(vmem_limit_bytes=LIMIT),
        cost_estimate=pl.CostEstimate(flops=cost[0], bytes_accessed=cost[1], transcendentals=0),
    )(*args)


def held(array):
    return pltpu.with_memory_space_constraint(array, pltpu.HBM)


def column(row):
    square = (ROWS, ROWS)
    same = lax.broadcasted_iota(jnp.int32, square, 0) == lax.broadcasted_iota(jnp.int32, square, 1)
    return jnp.sum(jnp.where(same, jnp.broadcast_to(row, square), 0.0), axis=1, keepdims=True)


def prep_kernel(*refs):
    hidden_hbm, wk_hbm, wv_hbm, ids_hbm, order_hbm, embed_hbm = refs[:6]
    own_ref, wk_ref, wv_ref, code_ref, pad_ref = refs[6:11]
    ids_ref, order_ref, embed_ref, sems = refs[11:]
    pairs = (
        (ids_hbm, ids_ref),
        (order_hbm, order_ref),
        (embed_hbm, embed_ref),
        (hidden_hbm, own_ref),
        (wk_hbm, wk_ref),
        (wv_hbm, wv_ref),
    )
    copies = [pltpu.make_async_copy(a, b, sems.at[i]) for i, (a, b) in enumerate(pairs)]
    for copy in copies:
        copy.start()
    for copy in copies:
        copy.wait()
    ids = jnp.broadcast_to(ids_ref[...].astype(F32), (PAD, ROWS))
    order = jnp.broadcast_to(order_ref[...].astype(F32), (PAD, ROWS))
    row = lax.broadcasted_iota(jnp.int32, (PAD, ROWS), 0)
    code_ref[...] = jnp.where(lax.rem(row, 2) == 0, ids, order).astype(BF16)
    pad_ref[...] = jnp.broadcast_to(embed_ref[...], pad_ref.shape)


def kv_kernel(*refs):
    pieces = refs[:8]
    pad_ref, wk_ref, wv_ref, code_ref = refs[8:12]
    x_ref, kv_ref, mkv_ref = refs[12:]
    me = lax.axis_index("kv")
    for dz in range(4):
        for dc in range(2):
            source = jnp.bitwise_xor(me, 2 * dz + dc)
            lanes = pl.ds(pl.multiple_of(source * WIDTH, WIDTH), WIDTH)
            x_ref[:ROWS, lanes] = pieces[2 * dz + dc][...]
    x_ref[ROWS:, :] = pad_ref[...]
    x = x_ref[...]
    for part, w_ref in enumerate((wk_ref, wv_ref)):
        lanes = slice(part * HEAD, (part + 1) * HEAD)
        product = dot(x, w_ref[...]).astype(BF16)
        kv_ref[:ROWS, lanes] = product[:ROWS]
        kv_ref[ROWS:, lanes] = code_ref[...]
        mkv_ref[:, lanes] = product[ROWS:]


def pair_kernel(own_ref, other_ref, k_ref, v_ref):
    for i, ref in enumerate((own_ref, other_ref)):
        rows = slice(i * ROWS, (i + 1) * ROWS)
        k_ref[rows, :] = ref[:ROWS, :HEAD]
        v_ref[rows, :] = ref[:ROWS, HEAD:]
    row = lax.broadcasted_iota(jnp.int32, (PAD, HEAD), 0)
    first = ref_tail(own_ref, ROWS)
    code = jnp.where(lax.rem(row, 4) < 2, first, ref_tail(other_ref, ROWS))
    k_ref[2 * ROWS :, :] = code.astype(BF16)


def ref_tail(ref, start):
    return ref[start:, :HEAD].astype(F32)


def stack_kernel(*refs):
    ks, vs = refs[:4], refs[4:8]
    k_ref, v_ref = refs[8:]
    row = lax.broadcasted_iota(jnp.int32, (PAD, HEAD), 0)
    code = jnp.zeros((PAD, HEAD), F32)
    for i in range(4):
        rows = slice(i * 2 * ROWS, (i + 1) * 2 * ROWS)
        k_ref[rows, :] = ks[i][: 2 * ROWS, :]
        v_ref[rows, :] = vs[i][...]
        code = jnp.where(row // 4 == i, ref_tail(ks[i], 2 * ROWS), code)
    k_ref[8 * ROWS :, :] = code.astype(BF16)


def q_kernel(x_ref, wq_ref, code_ref, cut_ref, q_ref, flag_ref, own_cut_ref):
    code = code_ref[...].astype(F32)
    ids = column(code[0:1])
    order = column(code[1:2])
    blocks = cut_ref.shape[1]
    spots = lax.broadcasted_iota(jnp.int32, (ROWS, blocks), 1).astype(F32)
    cuts = jnp.broadcast_to(cut_ref[...].astype(F32), (ROWS, blocks))
    cut = jnp.sum(jnp.where(spots == ids, cuts, 0.0), axis=1, keepdims=True)
    flag = jnp.broadcast_to(jnp.where(order >= cut, 1.0, 0.0), (ROWS, HEAD))
    flag_ref[...] = flag
    own_cut_ref[...] = jnp.broadcast_to(cut, (ROWS, HEAD))
    x = x_ref[...]
    for h in range(GROUP):
        product = dot(x, wq_ref[:, h * HEAD : (h + 1) * HEAD])
        clean = product[:ROWS]
        fixed = jnp.broadcast_to(product[ROWS : ROWS + 1], (ROWS, HEAD))
        q_ref[h, :ROWS, :] = clean.astype(BF16)
        q_ref[h, ROWS:, :] = jnp.where(flag > 0.5, fixed, clean).astype(BF16)


def near_kernel(q_ref, kv_ref, mkv_ref, flag_ref, code_ref, top_ref, total_ref, accum_ref):
    masked = flag_ref[...] > 0.5

    def both(lanes):
        clean = kv_ref[:ROWS, lanes]
        fixed = jnp.broadcast_to(mkv_ref[0:1, lanes].astype(F32), (ROWS, HEAD))
        return jnp.concatenate([clean, jnp.where(masked, fixed, clean.astype(F32)).astype(BF16)], axis=0)

    row = code_ref[...].astype(F32)[0:1]
    query = jnp.broadcast_to(column(row), (ROWS, ROWS))
    key = jnp.broadcast_to(row, (ROWS, ROWS))
    zero = jnp.zeros((ROWS, ROWS), F32)
    low = jnp.full((ROWS, ROWS), LOW, F32)
    clean_bias = jnp.concatenate([jnp.where(key <= query, zero, low), low], axis=1)
    noisy_bias = jnp.concatenate([jnp.where(key < query, zero, low), jnp.where(key == query, zero, low)], axis=1)
    bias = jnp.concatenate([clean_bias, noisy_bias], axis=0)
    keys = both(slice(0, HEAD))
    values = both(slice(HEAD, 2 * HEAD))
    for h in range(GROUP):
        scores = jnp.where(bias < -1.0, LOW, dot_t(q_ref[h], keys))
        top = jnp.max(scores, axis=1, keepdims=True)
        probs = jnp.exp2((scores - top) * POWER)
        top_ref[h] = jnp.broadcast_to(top, (2 * ROWS, HEAD))
        total_ref[h] = jnp.broadcast_to(jnp.sum(probs, axis=1, keepdims=True), (2 * ROWS, HEAD))
        accum_ref[h] = dot(probs.astype(BF16), values)


def place():
    me = lax.axis_index("ctx")
    return me, me // 8, lax.rem(me // 2, 4), lax.rem(me, 2)


def pipeline(q_ref, pieces, state_in, state, finish):
    top_ref, total_ref, accum_ref = state

    def scores_of(step):
        h, chunk, _, _ = step
        keys, _, mask, _ = pieces[chunk]
        scores = dot_t(q_ref[h], keys())
        parts = [scores[:, j : j + ROWS] for j in range(0, scores.shape[1], ROWS)]
        return mask(parts) if mask is not None else parts

    def absorb(step, parts):
        h, chunk, first, last = step
        _, values, _, seen = pieces[chunk]
        best = parts[0]
        for part in parts[1:]:
            best = jnp.maximum(best, part)
        best = jnp.max(best, axis=1, keepdims=True)
        if seen is not None:
            best = jnp.where(seen, best, LOW)
        source = state_in if first else state
        old = source[0][h]
        top = jnp.maximum(old, best)
        factor = jnp.exp2((old - top) * POWER)
        level = top if seen is None else jnp.where(seen, top, -LOW)
        probs = [jnp.exp2((part - level) * POWER) for part in parts]
        probs = jnp.concatenate([part.astype(BF16) for part in probs], axis=1)
        right = values()
        product = dot(probs, jnp.concatenate([right, jnp.ones(right.shape, BF16)], axis=1))
        total = source[1][h] * factor + product[:, HEAD:]
        accum = source[2][h] * factor + product[:, :HEAD]
        if last and finish is not None:
            finish(h, accum, total)
        else:
            top_ref[h] = top
            total_ref[h] = total
            accum_ref[h] = accum

    order = [(h, i, i == 0, i == len(pieces) - 1) for i in range(len(pieces)) for h in range(GROUP)]
    parts = scores_of(order[0])
    for now, later in zip(order, order[1:] + [None]):
        following = None if later is None else scores_of(later)
        absorb(now, parts)
        parts = following


def blocks_of(ref, which):
    return jnp.concatenate([ref[i * 2 * ROWS : (i + 1) * 2 * ROWS, :] for i in which], axis=0)


def shard_mask(where, spots):
    me, y, x, z = where

    def mask(parts):
        kept = []
        for j, part in enumerate(parts):
            dy, dx = spots[j // 2]
            there = jnp.bitwise_xor(me, dy * 8 + dx * 2 + j % 2)
            kept.append(jnp.where(there < me - 1, part, LOW))
        return kept

    return mask


def spots_piece(where, k_of, v_of, spots):
    def keys():
        return jnp.concatenate([k_of[dy][dx * 2 * ROWS : (dx + 1) * 2 * ROWS, :] for dy, dx in spots], axis=0)

    def values():
        return jnp.concatenate([v_of[dx][dy * 2 * ROWS : (dy + 1) * 2 * ROWS, :] for dy, dx in spots], axis=0)

    return keys, values, shard_mask(where, spots), None


def first_kernel(*refs):
    q_ref = refs[0]
    k_of, v_of = dict(zip((0, 1), refs[1:3])), dict(zip((0, 1), refs[3:5]))
    piece = spots_piece(place(), k_of, v_of, ((0, 1), (1, 0), (1, 1)))
    pipeline(q_ref, [piece], refs[5:8], refs[8:11], None)


def far_kernel(*refs):
    q_ref = refs[0]
    k_refs = dict(zip((0, 1, 3), refs[1:4]))
    v_refs = dict(zip((0, 1, 3), refs[4:7]))
    state_in = refs[7:10]
    code_ref, own_cut_ref, mkv_ref = refs[10:13]
    state = refs[13:16]
    me, y, x, z = place()

    spots = ((0, 0), (0, 1), (0, 3), (1, 3), (3, 3))
    old_far = jnp.bitwise_xor(me, jnp.maximum(me - 1, 0)) // 2
    new_far = jnp.bitwise_xor(me, jnp.minimum(me + 1, LAST)) // 2

    def pick(far, of):
        chosen = of(*spots[0])
        for dy, dx in spots[1:]:
            chosen = jnp.where(far == dy * 4 + dx, of(dy, dx), chosen)
        return chosen

    def k_block(dy, dx):
        return k_refs[dy][(dx * 2 + 1) * ROWS : (dx * 2 + 2) * ROWS, :]

    def v_block(dy, dx):
        return v_refs[dx][(dy * 2 + 1) * ROWS : (dy * 2 + 2) * ROWS, :]

    k_old, v_old = pick(old_far, k_block), pick(old_far, v_block)
    k_new, v_new = pick(new_far, k_block), pick(new_far, v_block)
    k_new, v_new = k_new[:BLOCK], v_new[:BLOCK]

    own = code_ref[...].astype(F32)[0:1]
    tails = {dy: ref_tail(k_refs[dy], 8 * ROWS) for dy in (0, 1, 3)}

    def line(i):
        def row(dy, dx):
            return tails[dy][dx * 4 + 2 + i : dx * 4 + 3 + i]

        return pick(old_far, row), pick(new_far, row)

    old_ids, new_ids = line(0)
    old_order, new_order = line(1)
    old_ids = jnp.broadcast_to(jnp.where(me > 0, old_ids, FAR), (8, ROWS))
    new_ids = jnp.broadcast_to(jnp.where(me < LAST, new_ids, FAR), (8, ROWS))
    first_cut = own_cut_ref[0:1, :]
    last_cut = own_cut_ref[ROWS - 1 : ROWS, :]
    old_masked = column(jnp.where(old_order >= first_cut, 1.0, 0.0))[ROWS - BLOCK :]
    new_masked = column(jnp.where(new_order >= last_cut, 1.0, 0.0))[:BLOCK]

    def noisy(masked, clean, lanes):
        fixed = jnp.broadcast_to(mkv_ref[0:1, lanes].astype(F32), clean.shape)
        flag = jnp.broadcast_to(masked, clean.shape) > 0.5
        return jnp.where(flag, fixed, clean.astype(F32)).astype(BF16)

    def rim(old, new, lanes):
        parts = [old, new, noisy(old_masked, old[ROWS - BLOCK :], lanes), noisy(new_masked, new, lanes)]
        return jnp.concatenate(parts + [jnp.zeros((BLOCK, HEAD), BF16)], axis=0)

    k_rim = rim(k_old, k_new, slice(0, HEAD))
    v_rim = rim(v_old, v_new, slice(HEAD, 2 * HEAD))
    lane = lax.broadcasted_iota(jnp.int32, (8, ROWS), 1)
    mixed = jnp.where(
        lane < 32,
        new_ids,
        jnp.where(lane < 64, pltpu.roll(old_ids, 64, 1), jnp.where(lane < 96, pltpu.roll(new_ids, 64, 1), -5.0)),
    )
    square = (ROWS, ROWS)
    query = jnp.broadcast_to(column(own), square)
    old_key = jnp.broadcast_to(old_ids[0:1], square)
    mixed_key = jnp.broadcast_to(mixed[0:1], square)
    early = lax.broadcasted_iota(jnp.int32, square, 1) < 32
    zero = jnp.zeros(square, F32)
    low = jnp.full(square, LOW, F32)
    clean_bias = [
        jnp.where(old_key <= query, zero, low),
        jnp.where(early, jnp.where(mixed_key <= query, zero, low), low),
    ]
    noisy_bias = [
        jnp.where(old_key < query, zero, low),
        jnp.where(early, jnp.where(mixed_key < query, zero, low), jnp.where(mixed_key == query, zero, low)),
    ]
    bias = jnp.concatenate([jnp.concatenate(clean_bias, axis=1), jnp.concatenate(noisy_bias, axis=1)], axis=0)

    def rim_mask(parts):
        return [jnp.where(bias[:, j * ROWS : (j + 1) * ROWS] < -1.0, LOW, part) for j, part in enumerate(parts)]

    spots = ((0, 3), (1, 3), (3, 0), (3, 1), (3, 3))
    pieces = [
        (lambda: k_rim, lambda: v_rim, rim_mask, None),
        spots_piece((me, y, x, z), k_refs, v_refs, spots),
    ]
    pipeline(q_ref, pieces, state_in, state, None)


def third_kernel(*refs):
    q_ref, k_ref, v_refs = refs[0], refs[1], refs[2:5]
    where = place()
    near = (0, 1, 3)
    keys, values, _, _ = spots_piece(where, {2: k_ref}, dict(zip(near, v_refs)), [(2, dx) for dx in near])
    piece = (keys, values, None, where[1] >= 2)
    pipeline(q_ref, [piece], refs[5:8], refs[8:11], None)


def last_kernel(*refs):
    q_ref, k_refs, v_ref = refs[0], refs[1:5], refs[5]
    state_in = refs[6:9]
    clean_ref, noisy_ref = refs[9:11]
    state = refs[11:14]
    piece = spots_piece(place(), dict(enumerate(k_refs)), {2: v_ref}, [(dy, 2) for dy in range(4)])

    stage_ref, sems = refs[-2:]
    copies = []

    def finish(h, accum, total):
        lanes = slice(h * HEAD, (h + 1) * HEAD)
        stage_ref[h] = (accum / total).astype(BF16)
        for i, ref in enumerate((clean_ref, noisy_ref)):
            source = stage_ref.at[h, i * ROWS : (i + 1) * ROWS]
            copies.append(pltpu.make_async_copy(source, ref.at[:, lanes], sems.at[2 * h + i]))
            copies[-1].start()

    pipeline(q_ref, [piece], state_in, state, finish)
    for copy in copies:
        copy.wait()


def shards(hidden, block_ids, decode_order, step_cut, mask_embed, q_weight, k_weight, v_weight):
    ids = block_ids.reshape(1, ROWS)
    order = decode_order.reshape(1, ROWS)
    cuts = step_cut.reshape(1, -1)
    two, one, three = [lax.ppermute(hidden, "kv", kv_pairs(d, 0)) for d in (2, 1, 3)]
    moved = [one, two, three]
    own, wk, wv, code, pad = call(
        prep_kernel,
        [
            (hidden.shape, BF16),
            (k_weight.shape, BF16),
            (v_weight.shape, BF16),
            ((PAD, ROWS), BF16),
            ((PAD, 8 * WIDTH), BF16),
        ],
        [held(a) for a in (hidden, k_weight, v_weight, ids, order, mask_embed.reshape(1, -1))],
        (1 << 20, 4 << 20),
        [
            pltpu.VMEM(ids.shape, jnp.int32),
            pltpu.VMEM(ids.shape, jnp.int32),
            pltpu.VMEM((1, 8 * WIDTH), BF16),
            pltpu.SemaphoreType.DMA((6,)),
        ],
        pl.ANY,
    )
    pieces = []
    for piece in (own, *moved):
        piece, _ = lax.optimization_barrier((piece, pad))
        pieces += [piece, lax.ppermute(piece, "kv", kv_pairs(0, 1))]
    x, kv, mask_kv = call(
        kv_kernel,
        [
            ((ROWS + PAD, 8 * WIDTH), BF16),
            ((ROWS + PAD, 2 * HEAD), BF16),
            ((PAD, 2 * HEAD), BF16),
        ],
        [*pieces, pad, wk, wv, code],
        (1 << 29, 3 << 20),
    )
    pair = lax.ppermute(kv, "ctx", ctx_pairs(0, 0, 1))
    q, flag, own_cut = call(
        q_kernel,
        [((GROUP, 2 * ROWS, HEAD), BF16), ((ROWS, HEAD), F32), ((ROWS, HEAD), F32)],
        [x, q_weight, code, cuts],
        (1 << 30, 5 << 20),
    )
    near = call(
        near_kernel,
        [((GROUP, 2 * ROWS, HEAD), F32)] * 3,
        [q, kv, mask_kv, flag, code],
        (1 << 30, 2 << 20),
    )
    pair, _ = lax.optimization_barrier((pair, flag))
    k, v = call(
        pair_kernel,
        [((2 * ROWS + PAD, HEAD), BF16), ((2 * ROWS, HEAD), BF16)],
        [kv, pair],
        (1 << 10, 1 << 18),
    )
    ks = [lax.ppermute(k, "ctx", ctx_pairs(0, d, 0)) for d in (1, 2, 3)]
    vs = [lax.ppermute(v, "ctx", ctx_pairs(d, 0, 0)) for d in (1, 2, 3)]
    ks, vs = call(
        stack_kernel,
        [((8 * ROWS + PAD, HEAD), BF16), ((8 * ROWS, HEAD), BF16)],
        [k, *ks, v, *vs],
        (1 << 10, 1 << 20),
    )
    all_k = [ks] + [lax.ppermute(ks, "ctx", ctx_pairs(d, 0, 0)) for d in (1, 2, 3)]
    all_v = [vs] + [lax.ppermute(vs, "ctx", ctx_pairs(0, d, 0)) for d in (1, 2, 3)]
    state = [((GROUP, 2 * ROWS, HEAD), F32)] * 3
    first = call(
        first_kernel,
        state,
        [q, *all_k[:2], *all_v[:2], *near],
        (1 << 30, 2 << 20),
    )
    far = call(
        far_kernel,
        state,
        [q, *[all_k[d] for d in (0, 1, 3)], *[all_v[d] for d in (0, 1, 3)], *first, code, own_cut, mask_kv],
        (1 << 31, 4 << 20),
    )
    third = call(
        third_kernel,
        state,
        [q, all_k[2], *[all_v[d] for d in (0, 1, 3)], *far],
        (1 << 30, 2 << 20),
    )
    return tuple(
        call(
            last_kernel,
            [((ROWS, GROUP * HEAD), BF16)] * 2,
            [q, *all_k, all_v[2], *third],
            (1 << 31, 4 << 20),
            [pltpu.VMEM((GROUP, 2 * ROWS, HEAD), F32)] * 3
            + [pltpu.VMEM((GROUP, 2 * ROWS, HEAD), BF16), pltpu.SemaphoreType.DMA((2 * GROUP,))],
            out_space=pl.ANY,
        )
    )


def solution(mesh):
    return jax.shard_map(
        shards,
        mesh=mesh,
        in_specs=(
            P("ctx", "kv"),
            P("ctx"),
            P("ctx"),
            P(),
            P(),
            P(None, "kv"),
            P(None, "kv"),
            P(None, "kv"),
        ),
        out_specs=(P("ctx", "kv"), P("ctx", "kv")),
        check_vma=False,
    )
```
